32 devices in a mesh: rows: 4 (over z), crops: 8 (over y, x, core).
Axes of the slice: x: 2, y: 2, z: 4, core: 2. Of those that a mesh axis runs over, the one named last changes fastest.
Arguments:
- images: bfloat16 [32, 56, 56, 256], P('crops', 'rows'), may hold values from -6 to 6
- reduce_one: bfloat16 [256, 128], replicated, may hold values from -0.375 to 0.375
- spatial_one: bfloat16 [3, 3, 128, 128], replicated, may hold values from -0.1875 to 0.1875
- expand_one: bfloat16 [128, 512], replicated, may hold values from -0.5 to 0.5
- shortcut: bfloat16 [256, 512], replicated, may hold values from -0.375 to 0.375
- reduce_two: bfloat16 [512, 128], replicated, may hold values from -0.25 to 0.25
- spatial_two: bfloat16 [3, 3, 128, 128], replicated, may hold values from -0.1875 to 0.1875
- expand_two: bfloat16 [128, 512], replicated, may hold values from -0.5 to 0.5
- mid_gain: float32 [4, 128], replicated, may hold values from 0.1 to 1.9
- mid_bias: float32 [4, 128], replicated, may hold values from -3 to 3
- wide_gain: float32 [3, 512], replicated, may hold values from 0.1 to 1.9
- wide_bias: float32 [3, 512], replicated, may hold values from -3 to 3
- widths: int32 [32, 2], P('crops'), may hold values from 32 to 128, as said below
- depth_gate: int32 [32], P('crops'), may hold values 0 or 1
- cotangent: bfloat16 [32, 28, 28, 512], P(('crops', 'rows')), may hold values from -6 to 6
Outputs:
- output: bfloat16 [32, 28, 28, 512], P(('crops', 'rows'))
- images_grad: bfloat16 [32, 56, 56, 256], P('crops', 'rows')
- reduce_one_grad: float32 [256, 128], replicated
- spatial_one_grad: float32 [3, 3, 128, 128], replicated
- expand_one_grad: float32 [128, 512], replicated
- shortcut_grad: float32 [256, 512], replicated
- reduce_two_grad: float32 [512, 128], replicated
- spatial_two_grad: float32 [3, 3, 128, 128], replicated
- expand_two_grad: float32 [128, 512], replicated
- mid_gain_grad: float32 [4, 128], replicated
- mid_bias_grad: float32 [4, 128], replicated
- wide_gain_grad: float32 [3, 512], replicated
- wide_bias_grad: float32 [3, 512], replicated
The draws below stay inside these ranges and needn't reach their ends.
Inputs may be any that keep to these rules, and one draw needn't show every extreme that they name: `widths`: every entry is a multiple of 32.
All inputs are finite; a program needn't handle non-finite values. No bound on the sum of `depth_gate` on one device may be relied on, other than what follows from the above.
Results may differ from the reference program's by a relative error of at most 0.015.
Values may be sent and summed in bfloat16 or wider, within the bound.
A program may use at most 128 MiB of HBM per device.

```python
import jax
import jax.numpy as jnp
from jax import lax

C_IN = 256
MID = 128
C_OUT = 512
SIDE = 56
CROPS = 32
HALF = 28


def draw_widths(key, part):
    levels = jax.random.randint(key, (CROPS, 2), 1, 5)
    levels = levels.at[0].set(4).at[1].set(1)
    return (levels * (MID // 4)).astype(jnp.int32)


def with_ends(values, rng, low, high):
    longest = values.shape.index(max(values.shape))
    spots = []
    for shift in (0, 1):
        where = [jax.random.randint(jax.random.fold_in(rng, axis), (), 0, length) for axis, length in enumerate(values.shape)]
        where[longest] = (where[longest] + shift) % values.shape[longest]
        spots.append(tuple(where))
    return values.at[spots[0]].set(low).at[spots[1]].set(high)


def steps_of(rng, shape, shards, low, top_value):
    factor_of, own = 1.0, jax.random.fold_in(rng, 6)
    for position, parts in shards:
        draws = jnp.exp(jax.random.uniform(jax.random.fold_in(own, position), (parts,), jnp.float32, low / len(shards), top_value / len(shards)))
        factor_of = factor_of * jnp.repeat(draws, shape[position] // parts).reshape([-1 if axis == position else 1 for axis in range(len(shape))])
    return factor_of


def gaussian(stream_key, dims, scale, most, pieces=(), kind=jnp.bfloat16):
    values = scale * jax.random.normal(stream_key, dims, jnp.float32)
    if pieces:
        values = values * steps_of(stream_key, dims, pieces, -0.22, 0.18)
    return jnp.clip(values, -most, most).astype(kind)


def setup_inputs(seed: int = 0) -> dict:
    arg_keys = jax.random.split(jax.random.key(seed), 16)
    images = gaussian(arg_keys[0], (CROPS, SIDE, SIDE, C_IN), 1.0, 6.0, ((0, 8), (1, 4)))
    reduce_one = gaussian(arg_keys[1], (C_IN, MID), C_IN ** -0.5, 0.375)
    spatial_one = gaussian(arg_keys[2], (3, 3, MID, MID), (9 * MID) ** -0.5, 0.1875)
    expand_one = gaussian(arg_keys[3], (MID, C_OUT), MID ** -0.5, 0.5)
    shortcut = gaussian(arg_keys[4], (C_IN, C_OUT), C_IN ** -0.5, 0.375)
    reduce_two = gaussian(arg_keys[5], (C_OUT, MID), C_OUT ** -0.5, 0.25)
    spatial_two = gaussian(arg_keys[6], (3, 3, MID, MID), (9 * MID) ** -0.5, 0.1875)
    expand_two = gaussian(arg_keys[7], (MID, C_OUT), MID ** -0.5, 0.5)
    mid_gain = jnp.clip(1.0 + 0.18 * jax.random.normal(arg_keys[8], (4, MID), jnp.float32), 0.1, 1.9)
    mid_bias = gaussian(arg_keys[9], (4, MID), 0.5, 3.0, (), jnp.float32)
    wide_gain = jnp.clip(1.0 + 0.18 * jax.random.normal(arg_keys[10], (3, C_OUT), jnp.float32), 0.1, 1.9)
    wide_bias = gaussian(arg_keys[11], (3, C_OUT), 0.5, 3.0, (), jnp.float32)
    widths = draw_widths(jax.random.fold_in(arg_keys[15], 71), 0)
    depth_gate = with_ends((jax.random.randint(arg_keys[13], (CROPS,), 0, 4) < 3).astype(jnp.int32), jax.random.fold_in(arg_keys[13], 1), 0, 1)
    cotangent = gaussian(arg_keys[14], (CROPS, HALF, HALF, C_OUT), 1.0, 6.0, ((0, 32),))
    return {"images": images, "reduce_one": reduce_one, "spatial_one": spatial_one, "expand_one": expand_one, "shortcut": shortcut, "reduce_two": reduce_two, "spatial_two": spatial_two, "expand_two": expand_two, "mid_gain": mid_gain, "mid_bias": mid_bias, "wide_gain": wide_gain, "wide_bias": wide_bias, "widths": widths, "depth_gate": depth_gate, "cotangent": cotangent}


epsilon = 1e-05
highest = lax.Precision.HIGHEST

@jax.custom_vjp
def low(v):
    return lax.optimization_barrier(v.astype(jnp.bfloat16)).astype(jnp.float32)

@jax.custom_vjp
def low_back(v):
    return v

def low_keep(v):
    return (low(v), None)

def low_pass(kept, grad):
    return (grad,)

def back_keep(v):
    return (v, None)

def back_low(kept, grad):
    return (low(grad),)
low.defvjp(low_keep, low_pass)
low_back.defvjp(back_keep, back_low)

def dense_map(activation, weight):
    return jnp.einsum('nhwc,cd->nhwd', activation, weight, precision=highest)

def spatial(activation, kernel, stride):
    return lax.conv_general_dilated(activation, kernel, (stride, stride), ((1, 1), (1, 1)), dimension_numbers=('NHWC', 'HWIO', 'NHWC'), precision=highest)

def norm(values, selector, gain_row, bias_row):
    count_all = jnp.maximum(lax.optimization_barrier(jnp.sum(selector, axis=(0, 1, 2))) * (values.shape[1] * values.shape[2]), 1.0)
    masked = selector * values
    center = lax.optimization_barrier(jnp.sum(masked, axis=(0, 1, 2))) / count_all
    spread = lax.optimization_barrier(jnp.sum(masked * values, axis=(0, 1, 2))) / count_all - center * center
    return selector * (gain_row * ((values - center) * lax.rsqrt(spread + epsilon)) + bias_row)

def reference(images, reduce_one, spatial_one, expand_one, shortcut, reduce_two, spatial_two, expand_two, mid_gain, mid_bias, wide_gain, wide_bias, widths, depth_gate, cotangent):
    float_type = jnp.float32
    channel = jnp.arange(MID, dtype=jnp.int32)
    gate_scale = (depth_gate > 0).astype(float_type)[:, None, None, None]
    mask_one = (channel[None, :] < widths[:, 0:1]).astype(float_type)[:, None, None, :]
    mask_two = (channel[None, :] < widths[:, 1:2]).astype(float_type)[:, None, None, :] * gate_scale
    wide_ones = jnp.ones((CROPS, 1, 1, C_OUT), float_type)
    gate_wide = jnp.broadcast_to(gate_scale, (CROPS, 1, 1, C_OUT))

    def forward(params):
        source, first_reduce, first_spatial, first_expand, skip_weight, second_reduce, second_spatial, second_expand, gains_mid, biases_mid, gains_wide, biases_wide = params
        reduced = low_back(dense_map(source, first_reduce))
        act_one = low(jax.nn.silu(norm(reduced, mask_one, gains_mid[0], biases_mid[0])))
        spatial_out = low_back(spatial(act_one, first_spatial, 2))
        act_two = low(jax.nn.silu(norm(spatial_out, mask_one, gains_mid[1], biases_mid[1])))
        expanded = low_back(dense_map(act_two, first_expand))
        skipped = low_back(dense_map(source[:, ::2, ::2, :], skip_weight))
        pre_one = norm(expanded, wide_ones, gains_wide[0], biases_wide[0]) + norm(skipped, wide_ones, gains_wide[1], biases_wide[1])
        hidden = low_back(low(jax.nn.silu(pre_one)))
        reduced_two = low_back(dense_map(hidden, second_reduce))
        act_four = low(jax.nn.silu(norm(reduced_two, mask_two, gains_mid[2], biases_mid[2])))
        spatial_mid = low_back(spatial(act_four, second_spatial, 1))
        act_five = low(jax.nn.silu(norm(spatial_mid, mask_two, gains_mid[3], biases_mid[3])))
        expanded_two = low_back(dense_map(act_five, second_expand))
        branch = jax.nn.silu(hidden + norm(expanded_two, gate_wide, gains_wide[2], biases_wide[2]))
        return gate_scale * branch + (1.0 - gate_scale) * hidden
    params = (images.astype(float_type), reduce_one.astype(float_type), spatial_one.astype(float_type), expand_one.astype(float_type), shortcut.astype(float_type), reduce_two.astype(float_type), spatial_two.astype(float_type), expand_two.astype(float_type), mid_gain.astype(float_type), mid_bias.astype(float_type), wide_gain.astype(float_type), wide_bias.astype(float_type))
    result, pullback = jax.vjp(forward, params)
    grads, = pullback(cotangent.astype(float_type))
    return (result.astype(jnp.bfloat16), grads[0].astype(jnp.bfloat16), grads[1], grads[2], grads[3], grads[4], grads[5], grads[6], grads[7], grads[8], grads[9], grads[10], grads[11])
```

```python
import jax
import jax.numpy as jnp
import functools
from jax import lax
from jax.experimental import pallas as pl
from jax.experimental.pallas import tpu as pltpu
from jax.sharding import PartitionSpec as P

epsilon = 1e-05
layout_spec = ("NHWC", "HWIO", "NHWC")


MESH = pl.DeviceIdType.MESH


def sum_kernel(nr, nc, x_ref, o_ref, buf, send_sem, recv_sem):
    row = lax.axis_index("rows")
    col = lax.axis_index("crops")
    total = nr * nc
    me = row * nc + col

    def place(i):
        return (lax.div(i, nc), lax.rem(i, nc))

    barrier = pltpu.get_barrier_semaphore()

    def greet(k, c):
        pl.semaphore_signal(
            barrier, inc=1, device_id=place(lax.rem(me + k, total)), device_id_type=MESH
        )
        return c

    lax.fori_loop(1, total, greet, 0)
    buf[me] = x_ref[...]
    pl.semaphore_wait(barrier, total - 1)

    def send(k, c):
        pltpu.make_async_remote_copy(
            src_ref=buf.at[me],
            dst_ref=buf.at[me],
            send_sem=send_sem,
            recv_sem=recv_sem,
            device_id=place(lax.rem(me + k, total)),
            device_id_type=MESH,
        ).start()
        return c

    lax.fori_loop(1, total, send, 0)
    others = buf.at[pl.ds(0, total - 1)]
    pltpu.make_async_copy(others, others, recv_sem).wait()
    o_ref[...] = lax.fori_loop(1, total, lambda k, v: v + buf[k], buf[0])
    pltpu.make_async_copy(others, others, send_sem).wait()


def summed_small(parts):
    sizes = [p.size for p in parts]
    flat = jnp.concatenate([p.reshape(-1) for p in parts])
    rows = -(-flat.size // 1024) * 8
    flat = jnp.pad(flat, (0, rows * 128 - flat.size)).reshape(rows, 128)
    nr, nc = lax.axis_size("rows"), lax.axis_size("crops")
    out = pl.pallas_call(
        functools.partial(sum_kernel, nr, nc),
        out_shape=jax.ShapeDtypeStruct((rows, 128), jnp.float32),
        in_specs=[pl.BlockSpec(memory_space=pltpu.VMEM)],
        out_specs=pl.BlockSpec(memory_space=pltpu.VMEM),
        scratch_shapes=[
            pltpu.VMEM((nr * nc, rows, 128), jnp.float32),
            pltpu.SemaphoreType.DMA,
            pltpu.SemaphoreType.DMA,
        ],
        compiler_params=pltpu.CompilerParams(
            collective_id=rows // 8, has_side_effects=True, vmem_limit_bytes=16 << 20
        ),
    )(flat).reshape(-1)
    result, at = [], 0
    for p, n in zip(parts, sizes):
        result.append(out[at : at + n].reshape(p.shape))
        at += n
    return tuple(result)


def passed_along(block, axis, distance):
    devices = range(lax.axis_size(axis))
    route = [(i - distance, i) for i in devices if i - distance in devices]
    return lax.ppermute(block, axis, route)


def padded_2(block, sides, width):
    for axis, dim in sides:
        count = lax.axis_size(axis)
        forward = [(i, i + 1) for i in range(count - 1)]
        backward = [(target, source) for source, target in forward]
        low = lax.ppermute(
            lax.slice_in_dim(block, block.shape[dim] - width, None, axis=dim), axis, forward
        )
        high = lax.ppermute(lax.slice_in_dim(block, 0, width, axis=dim), axis, backward)
        block = jnp.concatenate([low, block, high], axis=dim)
    return block


def shortened(shard):
    return jax.tree.map(lambda a: a.astype(jnp.bfloat16) if a.dtype == jnp.float32 else a, shard)


def smooth_slope(values):
    sigma = jax.nn.sigmoid(values)
    return sigma * (1.0 + values * (1.0 - sigma))


def dense_map(activation, weight):
    return jnp.einsum("nhwc,cd->nhwd", activation, weight, preferred_element_type=jnp.float32)


def dense_back(upstream, weight):
    return jnp.einsum("nhwd,cd->nhwc", upstream, weight, preferred_element_type=jnp.float32)


def weight_of(activation, upstream):
    return jnp.einsum("nhwc,nhwd->cd", activation, upstream, preferred_element_type=jnp.float32)


def spatial_map(padded, kernel, stride):
    return lax.conv_general_dilated(
        padded,
        kernel,
        (stride, stride),
        "VALID",
        dimension_numbers=layout_spec,
        preferred_element_type=jnp.float32,
    )


def spatial_weight(padded, upstream, stride):
    rows_out, cols_out = upstream.shape[1:3]
    used = padded[:, : stride * (rows_out - 1) + 3, : stride * (cols_out - 1) + 3]
    return lax.conv_general_dilated(
        used,
        upstream,
        (1, 1),
        "VALID",
        rhs_dilation=(stride, stride),
        dimension_numbers=("CHWN", "IHWO", "HWNC"),
        preferred_element_type=jnp.float32,
    )


def flipped(kernel):
    return jnp.transpose(kernel[::-1, ::-1], (0, 1, 3, 2))


def local_stats(values, selector):
    masked = selector * values
    count_local = jnp.sum(selector, axis=(0, 1, 2)) * (values.shape[1] * values.shape[2])
    return (jnp.sum(masked, axis=(0, 1, 2)), jnp.sum(masked * values, axis=(0, 1, 2)), count_local)


def norm_finish(values, selector, gain_row, bias_row, total_sum, square_sum, number):
    number = jnp.maximum(number, 1.0)
    center = total_sum / number
    spread = square_sum / number - center * center
    inv_scale = lax.rsqrt(spread + epsilon)
    normed = (values - center) * inv_scale
    return (selector * (gain_row * normed + bias_row), (normed, inv_scale, number))


def norm_forward(values, selector, gain_row, bias_row):
    total_sum, square_sum, number = summed_small(local_stats(values, selector))
    return norm_finish(values, selector, gain_row, bias_row, total_sum, square_sum, number)


def local_grads(upstream, selector, stored):
    masked = selector * upstream
    return (jnp.sum(masked, axis=(0, 1, 2)), jnp.sum(masked * stored[0], axis=(0, 1, 2)))


def norm_back_finish(upstream, selector, gain_row, stored, bias_grad, gain_grad):
    normed, inv_scale, number = stored
    values_grad = (
        selector
        * (gain_row * inv_scale)
        * (upstream - bias_grad / number - normed * gain_grad / number)
    )
    return (values_grad, gain_grad, bias_grad)


def norm_backward(upstream, selector, gain_row, stored):
    bias_grad, gain_grad = summed_small(local_grads(upstream, selector, stored))
    return norm_back_finish(upstream, selector, gain_row, stored, bias_grad, gain_grad)


def masks_of(width_rows, gate_rows, mid_width):
    channel = jnp.arange(mid_width, dtype=jnp.int32)
    gate_scale = (gate_rows > 0).astype(jnp.float32)[:, None, None, None]
    mask_first = (channel[None, :] < width_rows[:, 0:1]).astype(jnp.float32)[:, None, None, :]
    mask_second = (channel[None, :] < width_rows[:, 1:2]).astype(jnp.float32)[
        :, None, None, :
    ] * gate_scale
    return (mask_first, mask_second, gate_scale)


def on_device(
    images,
    reduce_one,
    spatial_one,
    expand_one,
    shortcut,
    reduce_two,
    spatial_two,
    expand_two,
    mid_gain,
    mid_bias,
    wide_gain,
    wide_bias,
    widths,
    depth_gate,
    cotangent,
):
    float_type = jnp.float32
    low_type = jnp.bfloat16
    mid_width = reduce_one.shape[1]
    wide_width = expand_one.shape[1]
    crops_here = images.shape[0]
    mask_one, mask_two_rows, gate_rows = masks_of(widths, depth_gate, mid_width)
    wide_ones = jnp.ones((crops_here, 1, 1, wide_width), float_type)
    col_pad = ((0, 0), (0, 0), (1, 1), (0, 0))
    reduced_one = dense_map(images, reduce_one)
    normed_one, stored_one = norm_forward(reduced_one, mask_one, mid_gain[0], mid_bias[0])
    act_one = jax.nn.silu(normed_one).astype(low_type)
    upper_row = passed_along(act_one[:, -1:], "rows", 1)
    padded_one = jnp.pad(jnp.concatenate([upper_row, act_one], 1), col_pad)
    spatial_out = spatial_map(padded_one, spatial_one, 2)
    normed_two, stored_two = norm_forward(spatial_out, mask_one, mid_gain[1], mid_bias[1])
    act_two = jax.nn.silu(normed_two).astype(low_type)
    expanded = dense_map(act_two, expand_one)
    skip_input = images[:, ::2, ::2, :]
    skipped = dense_map(skip_input, shortcut)
    normed_three, stored_three = norm_forward(expanded, wide_ones, wide_gain[0], wide_bias[0])
    normed_skip, stored_skip = norm_forward(skipped, wide_ones, wide_gain[1], wide_bias[1])
    pre_one = normed_three + normed_skip
    hidden_rows = jax.nn.silu(pre_one).astype(low_type)
    upstream = lax.all_to_all(cotangent, "rows", split_axis=1, concat_axis=0, tiled=True).astype(
        float_type
    )
    reduced_two = dense_map(hidden_rows, reduce_two)
    normed_four, stored_four = norm_forward(reduced_two, mask_two_rows, mid_gain[2], mid_bias[2])
    act_four = jax.nn.silu(normed_four).astype(low_type)
    framed = padded_2(act_four, (("rows", 1),), 1)
    padded_four = jnp.pad(framed, col_pad)
    spatial_mid = spatial_map(padded_four, spatial_two, 1)
    normed_five, stored_five = norm_forward(spatial_mid, mask_two_rows, mid_gain[3], mid_bias[3])
    act_five = jax.nn.silu(normed_five).astype(low_type)
    expanded_two = dense_map(act_five, expand_two)
    gate_wide = jnp.broadcast_to(gate_rows, (gate_rows.shape[0], 1, 1, wide_width))
    normed_six, stored_six = norm_forward(expanded_two, gate_wide, wide_gain[2], wide_bias[2])
    hidden_float = hidden_rows.astype(float_type)
    pre_two = hidden_float + normed_six
    result = (gate_rows * jax.nn.silu(pre_two) + (1.0 - gate_rows) * hidden_float).astype(low_type)
    result = lax.all_to_all(result, "rows", split_axis=0, concat_axis=1, tiled=True)
    live = gate_rows * upstream * smooth_slope(pre_two)
    grad_six, gain_six, bias_six = norm_backward(live, gate_wide, wide_gain[2], stored_six)
    grad_six = grad_six.astype(low_type)
    expand_two_grad = weight_of(act_five, grad_six)
    back_five = dense_back(grad_six, expand_two) * smooth_slope(normed_five)
    grad_five, gain_five, bias_five = norm_backward(
        back_five, mask_two_rows, mid_gain[3], stored_five
    )
    grad_five = grad_five.astype(low_type)
    spatial_two_grad = spatial_weight(padded_four, grad_five, 1)
    framed_grad = padded_2(grad_five, (("rows", 1),), 1)
    back_four = spatial_map(jnp.pad(framed_grad, col_pad), flipped(spatial_two), 1) * smooth_slope(
        normed_four
    )
    grad_four, gain_four, bias_four = norm_backward(
        back_four, mask_two_rows, mid_gain[2], stored_four
    )
    grad_four = grad_four.astype(low_type)
    reduce_two_grad = weight_of(hidden_rows, grad_four)
    hidden_grad = (dense_back(grad_four, reduce_two) + (1.0 - gate_rows) * upstream + live).astype(
        low_type
    )
    pre_grad = hidden_grad.astype(float_type) * smooth_slope(pre_one)
    grad_three, gain_three, bias_three = norm_backward(
        pre_grad, wide_ones, wide_gain[0], stored_three
    )
    grad_skip, gain_skip, bias_skip = norm_backward(pre_grad, wide_ones, wide_gain[1], stored_skip)
    grad_three = grad_three.astype(low_type)
    grad_skip = grad_skip.astype(low_type)
    expand_one_grad = weight_of(act_two, grad_three)
    shortcut_grad = weight_of(skip_input, grad_skip)
    back_two = dense_back(grad_three, expand_one) * smooth_slope(normed_two)
    grad_two, gain_two, bias_two = norm_backward(back_two, mask_one, mid_gain[1], stored_two)
    grad_two = grad_two.astype(low_type)
    spatial_one_grad = spatial_weight(padded_one, grad_two, 2)
    spread_grad = lax.conv_general_dilated(
        grad_two,
        flipped(spatial_one),
        (1, 1),
        ((2, 2), (2, 3)),
        lhs_dilation=(2, 2),
        dimension_numbers=layout_spec,
        preferred_element_type=float_type,
    )
    from_below = passed_along(shortened(spread_grad[:, 0:1, 1:-1]), "rows", -1)
    inner_grad = spread_grad[:, 1:, 1:-1]
    back_one = jnp.concatenate(
        [inner_grad[:, :-1], inner_grad[:, -1:] + from_below], 1
    ) * smooth_slope(normed_one)
    grad_one, gain_one, bias_one = norm_backward(back_one, mask_one, mid_gain[0], stored_one)
    grad_one = grad_one.astype(low_type)
    reduce_one_grad = weight_of(images, grad_one)
    skip_back = dense_back(grad_skip, shortcut)
    crops_n, rows_half, cols_half, chan_in = skip_back.shape
    placed = jnp.stack([skip_back, jnp.zeros_like(skip_back)], 2).reshape(
        crops_n, 2 * rows_half, cols_half, chan_in
    )
    placed = jnp.stack([placed, jnp.zeros_like(placed)], 3).reshape(
        crops_n, 2 * rows_half, 2 * cols_half, chan_in
    )
    images_grad = (dense_back(grad_one, reduce_one) + placed).astype(low_type)
    summed = lax.psum(
        (
            reduce_one_grad,
            spatial_one_grad,
            expand_one_grad,
            shortcut_grad,
            reduce_two_grad,
            spatial_two_grad,
            expand_two_grad,
        ),
        ("rows", "crops"),
    )
    mid_gain_grad = jnp.stack([gain_one, gain_two, gain_four, gain_five])
    mid_bias_grad = jnp.stack([bias_one, bias_two, bias_four, bias_five])
    wide_gain_grad = jnp.stack([gain_three, gain_skip, gain_six])
    wide_bias_grad = jnp.stack([bias_three, bias_skip, bias_six])
    return (
        result,
        images_grad,
        summed[0],
        summed[1],
        summed[2],
        summed[3],
        summed[4],
        summed[5],
        summed[6],
        mid_gain_grad,
        mid_bias_grad,
        wide_gain_grad,
        wide_bias_grad,
    )


def solution(mesh):
    return jax.shard_map(
        on_device,
        mesh=mesh,
        in_specs=(
            P("crops", "rows", None, None),
            P(),
            P(),
            P(),
            P(),
            P(),
            P(),
            P(),
            P(),
            P(),
            P(),
            P(),
            P("crops", None),
            P("crops"),
            P(("crops", "rows"), None, None, None),
        ),
        out_specs=(
            P(("crops", "rows"), None, None, None),
            P("crops", "rows", None, None),
            P(),
            P(),
            P(),
            P(),
            P(),
            P(),
            P(),
            P(),
            P(),
            P(),
            P(),
        ),
        check_vma=False,
    )
```

```python
import functools
from types import SimpleNamespace

import jax
import jax.numpy as jnp
from jax import lax
from jax.experimental import pallas as pl
from jax.experimental.pallas import tpu as pltpu
from jax.sharding import PartitionSpec as P

MESH = pl.DeviceIdType.MESH
F32 = jnp.float32
BF16 = jnp.bfloat16
epsilon = 1e-05
PAD = 32
LANES = 128

ROUND_ROWS = (4, 2, 16, 2, 2, 8, 8, 2, 2, 12, 2, 2)

GROUPS = (
    (("expand_two", 512), ("spatial_two", 1152)),
    (("reduce_two", 512), ("expand_one", 512), ("shortcut", 1024)),
    (("spatial_one", 1152), ("reduce_one", 256)),
)


def group_rows(group, devices):
    unit = 16 * devices
    return -(-sum(rows for _, rows in group) // unit) * unit


def dot(a, b):
    return lax.dot_general(a, b, (((1,), (0,)), ((), ())), preferred_element_type=F32)


def dot_nt(a, b):
    return lax.dot_general(a, b, (((1,), (1,)), ((), ())), preferred_element_type=F32)


def dot_tn(a, b):
    return lax.dot_general(a, b, (((0,), (0,)), ((), ())), preferred_element_type=F32)


def half_silu(h, half_mask=0.5):
    t = jnp.tanh(h)
    p = h * t
    return h + p, (half_mask + half_mask * t) * (1.0 + (h - p))


def folded(x):
    return jnp.sum(x.reshape(-1, 8, x.shape[-1]), axis=0)


def row_sum(x):
    return jnp.sum(x, axis=0, keepdims=True)


def flat2(x):
    return x.reshape(-1, x.shape[-1])


def mega(cfg, *refs):
    r = SimpleNamespace(**dict(zip(cfg.names, refs)))
    nr, nc, nk, hh, wv = cfg.nr, cfg.nc, cfg.nk, cfg.hh, cfg.wv
    ndev, nxy, own = nr * nc, nc // 2, nk // nr
    m_half = hh * PAD
    row = lax.axis_index("rows")
    col = lax.axis_index("crops")
    xy, core = lax.div(col, 2), lax.rem(col, 2)
    me = row * nc + col

    image_copies = [
        pltpu.make_async_copy(r.images.at[k], r.x_in.at[k], r.image_sem.at[k]) for k in range(nk)
    ]
    for copy in image_copies:
        copy.start()

    barrier = pltpu.get_barrier_semaphore()

    def place(i):
        return (lax.div(i, nc), lax.rem(i, nc))

    def greet(k, c):
        pl.semaphore_signal(
            barrier, inc=1, device_id=place(lax.rem(me + k, ndev)), device_id_type=MESH
        )
        return c

    lax.fori_loop(1, ndev, greet, 0)

    lane = lax.broadcasted_iota(jnp.int32, (1, LANES), 1)
    for k in range(nk):
        gate = (jnp.full((1, LANES), r.depth_gate[k], jnp.int32) > 0).astype(F32)
        r.mask_one[k] = (lane < r.widths[k, 0]).astype(F32)
        r.mask_two[k] = (lane < r.widths[k, 1]).astype(F32) * gate
        r.gates[k] = jnp.concatenate([gate] * 4, axis=1)
    col_mask = (lax.broadcasted_iota(jnp.int32, (PAD, 1), 0) < wv).astype(F32)
    half_mask = 0.5 * col_mask

    def tap(ref, i, j):
        return ref[i, j * LANES : (j + 1) * LANES, :].T

    for i in range(3):
        for j in range(3):
            r.back_two[i, j * LANES : (j + 1) * LANES, :] = tap(r.spatial_two, 2 - i, 2 - j)
    zeros = jnp.zeros((LANES, LANES), BF16)
    k1 = r.spatial_one
    here = [[tap(k1, 2, 2), tap(k1, 1, 2), tap(k1, 2, 1), tap(k1, 1, 1)],
            [tap(k1, 2, 0), tap(k1, 1, 0), zeros, zeros]]
    below = [[tap(k1, 0, 2), tap(k1, 0, 1)], [tap(k1, 0, 0), zeros]]
    for ref, blocks in ((r.back_here, here), (r.back_below, below)):
        for i, line in enumerate(blocks):
            for j, block in enumerate(line):
                ref[i * LANES : (i + 1) * LANES, j * LANES : (j + 1) * LANES] = block

    def send_sums(idx, vectors):
        buf, rows = r.sums[idx], ROUND_ROWS[idx]
        at = 0
        for v in vectors:
            for q in range(v.shape[1] // LANES):
                buf[me, at : at + 1, :] = v[:, q * LANES : (q + 1) * LANES]
                at += 1
        assert at == rows

        def send(k, c):
            pltpu.make_async_remote_copy(
                src_ref=buf.at[me],
                dst_ref=buf.at[me],
                send_sem=r.sum_send.at[idx],
                recv_sem=r.sum_recv.at[idx],
                device_id=place(lax.rem(me + k, ndev)),
                device_id_type=MESH,
            ).start()
            return c

        lax.fori_loop(1, ndev, send, 0)

    def take_sums(idx, widths):
        buf = r.sums[idx]
        others = buf.at[pl.ds(0, ndev - 1)]
        pltpu.make_async_copy(others, others, r.sum_recv.at[idx]).wait()
        total = jnp.sum(buf[...], axis=0)
        pltpu.make_async_copy(others, others, r.sum_send.at[idx]).wait()
        result, at = [], 0
        for w in widths:
            parts = [total[at + q : at + q + 1, :] for q in range(w // LANES)]
            at += w // LANES
            result.append(jnp.concatenate(parts, axis=1) if len(parts) > 1 else parts[0])
        return result

    up_ok, down_ok = row > 0, row < nr - 1
    from_above = jnp.where(row > 0, 1.0, 0.0)
    from_below = jnp.where(row < nr - 1, 1.0, 0.0)

    def halo(idx, up, src, dst):
        shift = -1 if up else 1
        return pltpu.make_async_remote_copy(
            src_ref=src,
            dst_ref=dst,
            send_sem=r.halo_send.at[idx],
            recv_sem=r.halo_recv.at[idx],
            device_id=(row + shift, col),
            device_id_type=MESH,
        )

    def halo_start(idx, up, src, dst):
        @pl.when(up_ok if up else down_ok)
        def _():
            halo(idx, up, src, dst).start()

    def halo_wait(idx, up, src, dst):
        @pl.when(up_ok if up else down_ok)
        def _():
            halo(idx, up, src, dst).wait_send()

        @pl.when(down_ok if up else up_ok)
        def _():
            halo(idx, up, src, dst).wait_recv()

    axes = (("core", 2), ("xy", nxy), ("rows", nr))
    seat = {"core": core, "xy": xy, "rows": row}

    def device_of(kind, i):
        if kind == "core":
            return (row, xy * 2 + i)
        if kind == "xy":
            return (row, i * 2 + core)
        return (i, col)

    def level_rows(g, level):
        size = cfg.group_size[g]
        for _, n in axes[:level]:
            size //= n
        return size

    def offset(g, level):
        at = 0
        for i, (kind, _) in enumerate(axes[:level]):
            at = at + seat[kind] * level_rows(g, i + 1)
        return pl.multiple_of(at, 16) if level else 0

    def scatter_send(g, level):
        kind, n = axes[level]
        chunk = level_rows(g, level + 1)
        for k in range(1, n):
            p = lax.rem(seat[kind] + k, n)
            pltpu.make_async_remote_copy(
                src_ref=r.part[g][level].at[pl.ds(pl.multiple_of(p * chunk, 16), chunk)],
                dst_ref=r.came[g][level].at[k - 1],
                send_sem=r.grad_send.at[g, level],
                recv_sem=r.grad_recv.at[g, level],
                device_id=device_of(kind, p),
                device_id_type=MESH,
            ).start()

    def scatter_take(g, level):
        kind, n = axes[level]
        chunk = level_rows(g, level + 1)
        came = r.came[g][level]
        pltpu.make_async_copy(came, came, r.grad_recv.at[g, level]).wait()
        mine = pl.ds(pl.multiple_of(seat[kind] * chunk, 16), chunk)
        total = r.part[g][level][mine, :].astype(F32) + jnp.sum(came[...].astype(F32), axis=0)
        pltpu.make_async_copy(came, came, r.grad_send.at[g, level]).wait()
        if level + 1 < len(axes):
            r.part[g][level + 1][...] = total.astype(BF16)
        else:
            r.full[g][pl.ds(offset(g, 3), chunk), :] = total.astype(BF16)

    def gather_send(g, level):
        kind, n = axes[level]
        size = level_rows(g, level + 1)
        region = r.full[g].at[pl.ds(offset(g, level + 1), size)]
        for k in range(1, n):
            p = lax.rem(seat[kind] + k, n)
            pltpu.make_async_remote_copy(
                src_ref=region,
                dst_ref=region,
                send_sem=r.grad_send.at[g, 3 + level],
                recv_sem=r.grad_recv.at[g, 3 + level],
                device_id=device_of(kind, p),
                device_id_type=MESH,
            ).start()

    def gather_take(g, level):
        n = axes[level][1]
        size = level_rows(g, level + 1) * (n - 1)
        bytes_of = r.full[g].at[pl.ds(0, size)]
        pltpu.make_async_copy(bytes_of, bytes_of, r.grad_recv.at[g, 3 + level]).wait()
        pltpu.make_async_copy(bytes_of, bytes_of, r.grad_send.at[g, 3 + level]).wait()

    steps = (
        (scatter_send, 0), (scatter_take, 0), (scatter_send, 1), (scatter_take, 1),
        (scatter_send, 2), (scatter_take, 2), (gather_send, 2), (gather_take, 2),
        (gather_send, 1), (gather_take, 1), (gather_send, 0), (gather_take, 0),
    )

    def advance(g, phase):
        for fn, level in steps[max(0, 2 * phase - 1) : 2 * phase + 1]:
            fn(g, level)

    def stage(g, name, value):
        at = 0
        for other, rows in GROUPS[g]:
            if other == name:
                break
            at += rows
        blocks = value.shape[1] // LANES
        for q in range(blocks):
            n = value.shape[0]
            lo = at + q * n
            r.part[g][0][lo : lo + n, :] = value[:, q * LANES : (q + 1) * LANES].astype(BF16)

    def unstage(g, name, ref):
        at = 0
        for other, rows in GROUPS[g]:
            if other == name:
                break
            at += rows
        n = ref.shape[0]
        for q in range(ref.shape[1] // LANES):
            lo = at + q * n
            ref[:, q * LANES : (q + 1) * LANES] = r.full[g][lo : lo + n, :].astype(F32)

    def coefficients(total, square, count, gain, bias):
        n = jnp.maximum(count, 1.0)
        mu = total / n
        inv = lax.rsqrt(square / n - mu * mu + epsilon)
        scale = gain * inv
        return SimpleNamespace(n=n, mu=mu, inv=inv, scale=scale, shift=bias - mu * scale)

    def backward(norm, dbias, dz_sum):
        dgain = norm.inv * (dz_sum - norm.mu * dbias)
        c2 = -norm.scale * norm.inv * dgain / norm.n
        c3 = -norm.scale * dbias / norm.n - c2 * norm.mu
        return dgain, (norm.scale, c2, c3)

    def loop(body, init=0):
        return lax.fori_loop(0, nk, body, init)

    def zero8(width, count):
        return tuple(jnp.zeros((8, width), F32) for _ in range(count))

    lane_blocks = cfg.c_in // LANES
    for slot in range(2 * hh):
        for q in range(lane_blocks):
            r.spread[q, slot, 2 * wv : 2 * PAD, :] = jnp.zeros((2 * PAD - 2 * wv, LANES), F32)
    w1 = r.reduce_one[...]
    acc = zero8(LANES, 2)
    for copy in image_copies:
        copy.wait()

    def first(k, acc):
        for i in range(2 * hh):
            for q in range(lane_blocks):
                lanes = slice(q * LANES, (q + 1) * LANES)
                r.spread[q, i, 0 : 2 * wv, :] = r.x_in[k, i, :, lanes].astype(F32)
        m = r.mask_one[k]
        s1, s2 = acc
        for pr in range(2):
            for pc in range(2):
                for i in range(hh):
                    for q in range(lane_blocks):
                        lanes = slice(q * LANES, (q + 1) * LANES)
                        r.x[pr, pc, k, i, :, lanes] = r.spread[
                            q, 2 * i + pr, pl.ds(pc, PAD, stride=2), :
                        ].astype(BF16)
                z = dot(flat2(r.x[pr, pc, k]), w1)
                r.z1[pr, pc, k] = z.reshape(hh, PAD, LANES)
                s1 += m * folded(z)
                s2 += m * folded(z * z)
        return s1, s2

    s1, s2 = loop(first, acc)
    count_one = sum(r.mask_one[k] for k in range(nk))
    count_two = sum(r.mask_two[k] for k in range(nk))
    pl.semaphore_wait(barrier, ndev - 1)
    send_sums(0, [row_sum(s1), row_sum(s2), count_one, count_two])
    halo_z1 = (0, False, r.z1.at[1, :, :, hh - 1], r.h1)
    halo_start(*halo_z1)

    def cot_copy(k, p):
        return pltpu.make_async_remote_copy(
            src_ref=r.cot.at[:, pl.ds(p * hh, hh)],
            dst_ref=r.cot_rows.at[pl.ds(row * own, own)],
            send_sem=r.cot_send.at[k],
            recv_sem=r.cot_recv.at[k],
            device_id=(p, col),
            device_id_type=MESH,
        )

    cot_copies = [cot_copy(k, lax.rem(row + k, nr)) for k in range(1, nr)]
    cot_local = pltpu.make_async_copy(
        r.cot.at[:, pl.ds(row * hh, hh)], r.cot_rows.at[pl.ds(row * own, own)], r.local_sem.at[0]
    )
    for copy in cot_copies:
        copy.start()
    cot_local.start()

    sc = r.shortcut[...]

    def skip(k, acc):
        z = dot(flat2(r.x[0, 0, k]), sc)
        r.zs[k] = z.reshape(hh, PAD, cfg.c_out)
        return acc[0] + folded(z), acc[1] + folded(z * z)

    zs1, zs2 = loop(skip, zero8(cfg.c_out, 2))

    t1, t2, active_one, active_two = take_sums(0, [LANES] * 4)
    half_px, full_px = float(hh * wv), float(4 * hh * wv)
    active_gate = active_two[:, 0:1]
    g1, b1 = r.mid_gain[0:1, :], r.mid_bias[0:1, :]
    n1 = coefficients(t1, t2, active_one * full_px, g1, b1)
    halo_wait(*halo_z1)

    def shifted_right(a):
        return pltpu.roll(a, 1, axis=a.ndim - 2)

    def shifted_left(a):
        return pltpu.roll(a, PAD - 1, axis=a.ndim - 2)

    def affine(norm, m):
        return 0.5 * m * norm.scale, (0.5 * m * norm.shift) * col_mask

    k_one = [r.spatial_one[i] for i in range(3)]

    def second(k, acc):
        m = r.mask_one[k]
        ah, bh = affine(n1, m)
        for pr in range(2):
            for pc in range(2):
                a, s = half_silu(r.z1[pr, pc, k] * ah + bh, half_mask)
                r.s1[pr, pc, k] = s
                dst = r.even if pr == 0 else r.odd
                rows = pl.ds(0, hh) if pr == 0 else pl.ds(1, hh)
                if pc == 0:
                    dst[k, rows, :, LANES : 2 * LANES] = a.astype(BF16)
                else:
                    dst[k, rows, :, 2 * LANES : 3 * LANES] = a.astype(BF16)
                    dst[k, rows, :, 0:LANES] = shifted_right(a).astype(BF16)
        for pc in range(2):
            a, _ = half_silu(r.h1[pc, k] * ah + bh)
            a = jnp.where(row > 0, a, 0.0)
            if pc == 0:
                r.odd[k, 0, :, LANES : 2 * LANES] = a.astype(BF16)
            else:
                r.odd[k, 0, :, 2 * LANES : 3 * LANES] = a.astype(BF16)
                r.odd[k, 0, :, 0:LANES] = shifted_right(a).astype(BF16)
        z = dot(flat2(r.even[k]), k_one[1])
        z += dot(flat2(r.odd[k, 1 : hh + 1]), k_one[2])
        z += dot(flat2(r.odd[k, 0:hh]), k_one[0])
        z = z.reshape(hh, PAD, LANES) * col_mask
        r.z2[k] = z
        return acc[0] + m * folded(z), acc[1] + m * folded(z * z)

    s1, s2 = loop(second, zero8(LANES, 2))
    send_sums(1, [row_sum(s1), row_sum(s2)])
    halo_z2 = (1, True, r.z2.at[:, 0], r.h2)
    halo_start(*halo_z2)
    t1, t2 = take_sums(1, [LANES] * 2)
    n2 = coefficients(t1, t2, active_one * half_px, r.mid_gain[1:2, :], r.mid_bias[1:2, :])
    e1 = r.expand_one[...]

    def third(k, acc):
        ah, bh = affine(n2, r.mask_one[k])
        a, s = half_silu(r.z2[k] * ah + bh, half_mask)
        r.s2[k] = s
        a = a.astype(BF16)
        r.a2[k] = a
        z = dot(flat2(a), e1)
        r.z3[k] = z.reshape(hh, PAD, cfg.c_out)
        return acc[0] + folded(z), acc[1] + folded(z * z)

    s1, s2 = loop(third, zero8(cfg.c_out, 2))
    send_sums(2, [row_sum(s1), row_sum(s2), row_sum(zs1), row_sum(zs2)])
    t1, t2, ts1, ts2 = take_sums(2, [cfg.c_out] * 4)
    all_px = float(nk * nc) * float(nr) * half_px
    n3 = coefficients(t1, t2, all_px, r.wide_gain[0:1, :], r.wide_bias[0:1, :])
    ns = coefficients(ts1, ts2, all_px, r.wide_gain[1:2, :], r.wide_bias[1:2, :])
    w2 = r.reduce_two[...]

    def fourth(k, acc):
        a3, as_ = 0.5 * n3.scale, 0.5 * ns.scale
        b3 = (0.5 * (n3.shift + ns.shift)) * col_mask
        for i in range(hh):
            a, s = half_silu(r.z3[k, i] * a3 + r.zs[k, i] * as_ + b3, half_mask)
            r.hidden[k, i] = a.astype(BF16)
            r.s3[k, i] = s
        z = dot(flat2(r.hidden[k]), w2)
        r.z4[k] = z.reshape(hh, PAD, LANES)
        m = r.mask_two[k]
        return acc[0] + m * folded(z), acc[1] + m * folded(z * z)

    s1, s2 = loop(fourth, zero8(LANES, 2))
    send_sums(3, [row_sum(s1), row_sum(s2)])
    halos_z4 = [
        (2, False, r.z4.at[:, hh - 1], r.h4.at[0]),
        (3, True, r.z4.at[:, 0], r.h4.at[1]),
    ]
    for h in halos_z4:
        halo_start(*h)
    t1, t2 = take_sums(3, [LANES] * 2)
    n4 = coefficients(t1, t2, active_two * half_px, r.mid_gain[2:3, :], r.mid_bias[2:3, :])
    for h in halos_z4:
        halo_wait(*h)

    def put3(dst, k, rows, a):
        dst[k, rows, :, LANES : 2 * LANES] = a.astype(BF16)
        dst[k, rows, :, 0:LANES] = shifted_right(a).astype(BF16)
        dst[k, rows, :, 2 * LANES : 3 * LANES] = shifted_left(a).astype(BF16)

    k_two = [r.spatial_two[i] for i in range(3)]

    def fifth(k, acc):
        m = r.mask_two[k]
        ah, bh = affine(n4, m)
        a, s = half_silu(r.z4[k] * ah + bh, half_mask)
        r.s4[k] = s
        put3(r.a4, k, pl.ds(1, hh), a)
        a, _ = half_silu(r.h4[0, k] * ah + bh)
        put3(r.a4, k, 0, jnp.where(row > 0, a, 0.0))
        a, _ = half_silu(r.h4[1, k] * ah + bh)
        put3(r.a4, k, hh + 1, jnp.where(row < nr - 1, a, 0.0))
        z = sum(dot(flat2(r.a4[k, i : i + hh]), k_two[i]) for i in range(3))
        z = z.reshape(hh, PAD, LANES) * col_mask
        r.z5[k] = z
        return acc[0] + m * folded(z), acc[1] + m * folded(z * z)

    s1, s2 = loop(fifth, zero8(LANES, 2))
    send_sums(4, [row_sum(s1), row_sum(s2)])
    halos_z5 = [
        (4, False, r.z5.at[:, hh - 1], r.h5.at[0]),
        (5, True, r.z5.at[:, 0], r.h5.at[1]),
    ]
    for h in halos_z5:
        halo_start(*h)
    t1, t2 = take_sums(4, [LANES] * 2)
    n5 = coefficients(t1, t2, active_two * half_px, r.mid_gain[3:4, :], r.mid_bias[3:4, :])
    e2 = r.expand_two[...]

    def sixth(k, acc):
        ah, bh = affine(n5, r.mask_two[k])
        a, s = half_silu(r.z5[k] * ah + bh, half_mask)
        r.s5[k] = s
        a = a.astype(BF16)
        r.a5[k] = a
        z = dot(flat2(a), e2)
        r.z6[k] = z.reshape(hh, PAD, cfg.c_out)
        g = r.gates[k]
        return acc[0] + g * folded(z), acc[1] + g * folded(z * z)

    s1, s2 = loop(sixth, zero8(cfg.c_out, 2))
    send_sums(5, [row_sum(s1), row_sum(s2)])
    for copy in cot_copies:
        copy.wait()
    cot_local.wait()
    t1, t2 = take_sums(5, [cfg.c_out] * 2)
    gate_count = active_gate * half_px
    n6 = coefficients(t1, t2, gate_count, r.wide_gain[2:3, :], r.wide_bias[2:3, :])
    pad_rows = jnp.zeros((PAD - wv, cfg.c_out), F32)

    def cot_row(k, i):
        return jnp.concatenate([r.cot_rows[k, i].astype(F32), pad_rows], axis=0)

    def seventh(k, acc):
        g = r.gates[k]
        a6, b6 = (0.5 * g) * n6.scale, ((0.5 * g) * n6.shift) * col_mask
        d1, d2 = acc
        for i in range(hh):
            hid = r.hidden[k, i].astype(F32)
            z = r.z6[k, i]
            a, s = half_silu(0.5 * hid + (z * a6 + b6))
            r.out_rows[k, i] = jnp.where(g > 0.0, a, hid).astype(BF16)
            live = g * cot_row(k, i) * s
            r.live[k, i] = live
            d1 += folded(live)
            d2 += folded(live * z)
        return d1, d2

    d1, d2 = loop(seventh, zero8(cfg.c_out, 2))
    send_sums(6, [row_sum(d1), row_sum(d2)])

    def out_copy(k, p):
        return pltpu.make_async_remote_copy(
            src_ref=r.out_rows.at[pl.ds(p * own, own)],
            dst_ref=r.out.at[:, pl.ds(row * hh, hh)],
            send_sem=r.out_send.at[k],
            recv_sem=r.out_recv.at[k],
            device_id=(p, col),
            device_id_type=MESH,
        )

    out_copies = [out_copy(k, lax.rem(row + k, nr)) for k in range(1, nr)]
    out_local = pltpu.make_async_copy(
        r.out_rows.at[pl.ds(row * own, own)], r.out.at[:, pl.ds(row * hh, hh)], r.local_sem.at[1]
    )
    for copy in out_copies:
        copy.start()
    out_local.start()
    db6, q6 = take_sums(6, [cfg.c_out] * 2)
    dg6, (c1, c2, c3) = backward(n6, db6, q6)

    def eighth(k, acc, c1=c1, c2=c2, c3=c3):
        g = r.gates[k]
        f1, f2, f3 = g * c1, g * c2, (g * c3) * col_mask
        for i in range(hh):
            r.dz6[k, i] = (r.live[k, i] * f1 + r.z6[k, i] * f2 + f3).astype(BF16)
        q = dot_nt(flat2(r.dz6[k]), e2).reshape(hh, PAD, LANES) * r.s5[k]
        r.q5[k] = q
        m = r.mask_two[k]
        return acc[0] + m * folded(q), acc[1] + m * folded(q * r.z5[k])

    d1, d2 = loop(eighth, zero8(LANES, 2))
    send_sums(7, [row_sum(d1), row_sum(d2)])
    halos_q5 = [
        (6, False, r.q5.at[:, hh - 1], r.hq5.at[0]),
        (7, True, r.q5.at[:, 0], r.hq5.at[1]),
    ]
    for h in halos_q5:
        halo_start(*h)
    stage(0, "expand_two", dot_tn(flat2(r.a5[...]), flat2(r.dz6[...])))
    for h in halos_z5:
        halo_wait(*h)
    db5, q5 = take_sums(7, [LANES] * 2)
    dg5, (c1, c2, c3) = backward(n5, db5, q5)
    for h in halos_q5:
        halo_wait(*h)

    def ninth(k, acc, c1=c1, c2=c2, c3=c3):
        m = r.mask_two[k]
        f1, f2, f3 = m * c1, m * c2, (m * c3) * col_mask
        put3(r.dz5, k, pl.ds(1, hh), r.q5[k] * f1 + r.z5[k] * f2 + f3)
        d = r.hq5[0, k] * f1 + r.h5[0, k] * f2 + f3
        put3(r.dz5, k, 0, jnp.where(row > 0, d, 0.0))
        d = r.hq5[1, k] * f1 + r.h5[1, k] * f2 + f3
        put3(r.dz5, k, hh + 1, jnp.where(row < nr - 1, d, 0.0))
        q = sum(dot(flat2(r.dz5[k, i : i + hh]), r.back_two[i]) for i in range(3))
        q = q.reshape(hh, PAD, LANES) * r.s4[k]
        r.q4[k] = q
        return acc[0] + m * folded(q), acc[1] + m * folded(q * r.z4[k])

    d1, d2 = loop(ninth, zero8(LANES, 2))
    send_sums(8, [row_sum(d1), row_sum(d2)])
    d5 = flat2(r.dz5[:, 1 : hh + 1, :, LANES : 2 * LANES])
    stage(
        0,
        "spatial_two",
        jnp.concatenate([dot_tn(flat2(r.a4[:, i : i + hh]), d5) for i in range(3)], axis=0),
    )
    advance(0, 0)
    db4, q4 = take_sums(8, [LANES] * 2)
    dg4, (c1, c2, c3) = backward(n4, db4, q4)

    def tenth(k, acc, c1=c1, c2=c2, c3=c3):
        m, g = r.mask_two[k], r.gates[k]
        f1, f2, f3 = m * c1, m * c2, (m * c3) * col_mask
        r.dz4[k] = (r.q4[k] * f1 + r.z4[k] * f2 + f3).astype(BF16)
        back = dot_nt(flat2(r.dz4[k]), w2).reshape(hh, PAD, cfg.c_out)
        e1_, e2_, e3_ = acc
        for i in range(hh):
            d = back[i] + (1.0 - g) * cot_row(k, i) + r.live[k, i]
            q = d.astype(BF16).astype(F32) * r.s3[k, i]
            r.q3[k, i] = q
            e1_ += folded(q)
            e2_ += folded(q * r.z3[k, i])
            e3_ += folded(q * r.zs[k, i])
        return e1_, e2_, e3_

    d1, d2, d3 = loop(tenth, zero8(cfg.c_out, 3))
    send_sums(9, [row_sum(d1), row_sum(d2), row_sum(d3)])
    stage(1, "reduce_two", dot_tn(flat2(r.hidden[...]), flat2(r.dz4[...])))
    advance(0, 1)
    db3, q3, qs = take_sums(9, [cfg.c_out] * 3)
    dg3, (c1, c2, c3) = backward(n3, db3, q3)
    dgs, (p1, p2, p3) = backward(ns, db3, qs)

    def eleventh(k, acc, c1=c1, c2=c2, c3=c3):
        f3, h3 = c3 * col_mask, p3 * col_mask
        for i in range(hh):
            q = r.q3[k, i]
            r.dz3[k, i] = (q * c1 + r.z3[k, i] * c2 + f3).astype(BF16)
            r.dzs[k, i] = (q * p1 + r.zs[k, i] * p2 + h3).astype(BF16)
        q = dot_nt(flat2(r.dz3[k]), e1).reshape(hh, PAD, LANES) * r.s2[k]
        r.q2[k] = q
        m = r.mask_one[k]
        return acc[0] + m * folded(q), acc[1] + m * folded(q * r.z2[k])

    d1, d2 = loop(eleventh, zero8(LANES, 2))
    send_sums(10, [row_sum(d1), row_sum(d2)])
    halo_q2 = (8, True, r.q2.at[:, 0], r.hq2)
    halo_start(*halo_q2)
    stage(1, "expand_one", dot_tn(flat2(r.a2[...]), flat2(r.dz3[...])))
    stage(1, "shortcut", dot_tn(flat2(r.x[0, 0]), flat2(r.dzs[...])))
    advance(1, 0)
    advance(0, 2)
    halo_wait(*halo_z2)
    db2, q2 = take_sums(10, [LANES] * 2)
    dg2, (c1, c2, c3) = backward(n2, db2, q2)
    halo_wait(*halo_q2)

    def twelfth(k, acc, c1=c1, c2=c2, c3=c3):
        m = r.mask_one[k]
        f1, f2, f3 = m * c1, m * c2, (m * c3) * col_mask
        d = r.q2[k] * f1 + r.z2[k] * f2 + f3
        r.dz2[k, 0:hh, :, 0:LANES] = d.astype(BF16)
        r.dz2[k, 0:hh, :, LANES : 2 * LANES] = shifted_left(d).astype(BF16)
        d = jnp.where(row < nr - 1, r.hq2[k] * f1 + r.h2[k] * f2 + f3, 0.0)
        r.dz2[k, hh, :, 0:LANES] = d.astype(BF16)
        r.dz2[k, hh, :, LANES : 2 * LANES] = shifted_left(d).astype(BF16)
        u = dot(flat2(r.dz2[k, 0:hh]), r.back_here[...])
        v = dot(flat2(r.dz2[k, 1 : hh + 1]), r.back_below[...])
        s1, s2 = acc
        planes = (
            (1, 1, u[:, 0:LANES] + v[:, 0:LANES]),
            (0, 1, u[:, LANES : 2 * LANES]),
            (1, 0, u[:, 2 * LANES : 3 * LANES] + v[:, LANES : 2 * LANES]),
            (0, 0, u[:, 3 * LANES : 4 * LANES]),
        )
        for pr, pc, q in planes:
            q = q.reshape(hh, PAD, LANES) * r.s1[pr, pc, k]
            r.q1[pr, pc, k] = q
            s1 += m * folded(q)
            s2 += m * folded(q * r.z1[pr, pc, k])
        return s1, s2

    d1, d2 = loop(twelfth, zero8(LANES, 2))
    send_sums(11, [row_sum(d1), row_sum(d2)])
    d2_ = flat2(r.dz2[:, 0:hh, :, 0:LANES])
    lines = [r.odd[:, 0:hh], r.even[...], r.odd[:, 1 : hh + 1]]
    stage(
        2, "spatial_one", jnp.concatenate([dot_tn(flat2(a), d2_) for a in lines], axis=0)
    )
    advance(1, 1)
    advance(0, 3)

    def skip_back(k, c):
        r.skip_back[k] = dot_nt(flat2(r.dzs[k]), sc).reshape(hh, PAD, cfg.c_in)
        return c

    loop(skip_back)
    db1, q1 = take_sums(11, [LANES] * 2)
    dg1, (c1, c2, c3) = backward(n1, db1, q1)

    def last(k, acc, c1=c1, c2=c2, c3=c3):
        m = r.mask_one[k]
        f1, f2, f3 = m * c1, m * c2, (m * c3) * col_mask
        for pr in range(2):
            for pc in range(2):
                d = (r.q1[pr, pc, k] * f1 + r.z1[pr, pc, k] * f2 + f3).astype(BF16)
                r.dz1[pr, pc, k] = d
        return acc

    loop(last)
    total = sum(
        dot_tn(flat2(r.x[pr, pc]), flat2(r.dz1[pr, pc])) for pr in range(2) for pc in range(2)
    )
    stage(2, "reduce_one", total)
    advance(2, 0)
    advance(1, 2)
    advance(0, 4)

    def images_back(k, c):
        for pr in range(2):
            for pc in range(2):
                g = dot_nt(flat2(r.dz1[pr, pc, k]), w1).reshape(hh, PAD, cfg.c_in)
                if pr == 0 and pc == 0:
                    g += r.skip_back[k]
                for i in range(hh):
                    for q in range(lane_blocks):
                        r.spread[q, 2 * i + pr, pl.ds(pc, PAD, stride=2), :] = g[
                            i, :, q * LANES : (q + 1) * LANES
                        ]
        for i in range(2 * hh):
            for q in range(lane_blocks):
                lanes = slice(q * LANES, (q + 1) * LANES)
                r.x_in[k, i, :, lanes] = r.spread[q, i, 0 : 2 * wv, :].astype(BF16)
        return c

    loop(images_back)
    back_copy = pltpu.make_async_copy(r.x_in, r.images_grad, r.local_sem.at[2])
    back_copy.start()

    for k in range(4):
        r.mid_gain_grad[k : k + 1, :] = (dg1, dg2, dg4, dg5)[k]
        r.mid_bias_grad[k : k + 1, :] = (db1, db2, db4, db5)[k]
    for k in range(3):
        r.wide_gain_grad[k : k + 1, :] = (dg3, dgs, dg6)[k]
        r.wide_bias_grad[k : k + 1, :] = (db3, db3, db6)[k]

    for phase in range(1, 7):
        advance(2, phase)
        if phase + 2 <= 6:
            advance(1, phase + 2)
        if phase + 4 <= 6:
            advance(0, phase + 4)
    for g, group in enumerate(GROUPS):
        for name, _ in group:
            unstage(g, name, getattr(r, name + "_grad"))
    for copy in out_copies:
        copy.wait()
    out_local.wait()
    back_copy.wait()


def on_device(nr, nc, *args):
    (images, reduce_one, spatial_one, expand_one, shortcut, reduce_two, spatial_two, expand_two,
     mid_gain, mid_bias, wide_gain, wide_bias, widths, depth_gate, cot) = args
    nk, full_rows, full_cols, c_in = images.shape
    hh, wv, c_out = full_rows // 2, full_cols // 2, expand_one.shape[1]
    own = cot.shape[0]
    ndev, nxy = nr * nc, nc // 2
    sizes = [group_rows(g, ndev) for g in GROUPS]

    vmem, smem, hbm = pltpu.VMEM, pltpu.SMEM, pl.ANY
    ins = [
        ("images", images, hbm), ("cot", cot, hbm),
        ("reduce_one", reduce_one, vmem), ("spatial_one", spatial_one.reshape(3, 3 * LANES, LANES), vmem),
        ("expand_one", expand_one, vmem), ("shortcut", shortcut, vmem), ("reduce_two", reduce_two, vmem),
        ("spatial_two", spatial_two.reshape(3, 3 * LANES, LANES), vmem), ("expand_two", expand_two, vmem),
        ("mid_gain", mid_gain, vmem), ("mid_bias", mid_bias, vmem),
        ("wide_gain", wide_gain, vmem), ("wide_bias", wide_bias, vmem),
        ("widths", widths, smem), ("depth_gate", depth_gate, smem),
    ]
    outs = [
        ("out", (own, nr * hh, PAD, c_out), BF16, hbm),
        ("images_grad", images.shape, BF16, hbm),
        ("reduce_one_grad", (c_in, LANES), F32, vmem),
        ("spatial_one_grad", (9 * LANES, LANES), F32, vmem),
        ("expand_one_grad", (LANES, c_out), F32, vmem),
        ("shortcut_grad", (c_in, c_out), F32, vmem),
        ("reduce_two_grad", (c_out, LANES), F32, vmem),
        ("spatial_two_grad", (9 * LANES, LANES), F32, vmem),
        ("expand_two_grad", (LANES, c_out), F32, vmem),
        ("mid_gain_grad", mid_gain.shape, F32, vmem), ("mid_bias_grad", mid_bias.shape, F32, vmem),
        ("wide_gain_grad", wide_gain.shape, F32, vmem), ("wide_bias_grad", wide_bias.shape, F32, vmem),
    ]
    half, quad = (nk, hh, PAD), (2, 2, nk, hh, PAD)
    dma = pltpu.SemaphoreType.DMA
    scratch = [
        ("x_in", vmem(images.shape, BF16)),
        ("spread", vmem((c_in // LANES, 2 * hh, 2 * PAD, LANES), F32)),
        ("x", vmem(quad + (c_in,), BF16)),
        ("z1", vmem(quad + (LANES,), F32)),
        ("s1", vmem(quad + (LANES,), F32)),
        ("q1", vmem(quad + (LANES,), F32)),
        ("dz1", vmem(quad + (LANES,), BF16)),
        ("h1", vmem((2, nk, PAD, LANES), F32)),
        ("even", vmem(half + (3 * LANES,), BF16)),
        ("odd", vmem((nk, hh + 1, PAD, 3 * LANES), BF16)),
        ("dz2", vmem((nk, hh + 1, PAD, 2 * LANES), BF16)),
        ("a4", vmem((nk, hh + 2, PAD, 3 * LANES), BF16)),
        ("dz5", vmem((nk, hh + 2, PAD, 3 * LANES), BF16)),
        ("h2", vmem((nk, PAD, LANES), F32)),
        ("hq2", vmem((nk, PAD, LANES), F32)),
        ("h4", vmem((2, nk, PAD, LANES), F32)),
        ("h5", vmem((2, nk, PAD, LANES), F32)),
        ("hq5", vmem((2, nk, PAD, LANES), F32)),
        ("cot_rows", vmem((nk, hh, wv, c_out), BF16)),
        ("out_rows", vmem(half + (c_out,), BF16)),
        ("skip_back", vmem(half + (c_in,), F32)),
        ("back_two", vmem((3, 3 * LANES, LANES), BF16)),
        ("back_here", vmem((2 * LANES, 4 * LANES), BF16)),
        ("back_below", vmem((2 * LANES, 2 * LANES), BF16)),
        ("mask_one", vmem((nk, 1, LANES), F32)),
        ("mask_two", vmem((nk, 1, LANES), F32)),
        ("gates", vmem((nk, 1, c_out), F32)),
    ]
    scratch += [(n, vmem(half + (LANES,), F32)) for n in ("z2", "s2", "q2", "z4", "s4", "q4", "z5", "s5", "q5")]
    scratch += [(n, vmem(half + (c_out,), F32)) for n in ("z3", "zs", "s3", "q3", "z6", "live")]
    scratch += [(n, vmem(half + (LANES,), BF16)) for n in ("a2", "a5", "dz4")]
    scratch += [(n, vmem(half + (c_out,), BF16)) for n in ("hidden", "dz6", "dz3", "dzs")]
    scratch += [
        ("image_sem", dma((nk,))), ("local_sem", dma((3,))),
        ("sum_send", dma((len(ROUND_ROWS),))), ("sum_recv", dma((len(ROUND_ROWS),))),
        ("halo_send", dma((9,))), ("halo_recv", dma((9,))),
        ("cot_send", dma((nr,))), ("cot_recv", dma((nr,))),
        ("out_send", dma((nr,))), ("out_recv", dma((nr,))),
        ("grad_send", dma((len(GROUPS), 6))), ("grad_recv", dma((len(GROUPS), 6))),
    ]
    scratch += [(f"sums{i}", vmem((ndev, n, LANES), F32)) for i, n in enumerate(ROUND_ROWS)]
    for g, size in enumerate(sizes):
        levels = (size, size // 2, size // nc, size // ndev)
        for level, n in enumerate((2, nxy, nr)):
            scratch.append((f"part{g}_{level}", vmem((levels[level], LANES), BF16)))
            scratch.append((f"came{g}_{level}", vmem((n - 1, levels[level + 1], LANES), BF16)))
        scratch.append((f"full{g}", vmem((size, LANES), BF16)))
    cfg = SimpleNamespace(
        nr=nr, nc=nc, nk=nk, hh=hh, wv=wv, c_in=c_in, c_out=c_out, group_size=sizes,
        names=[n for n, *_ in ins] + [n for n, *_ in outs] + [n for n, _ in scratch],
    )

    def body(*refs):
        named = dict(zip(cfg.names, refs))
        named["sums"] = [named[f"sums{i}"] for i in range(len(ROUND_ROWS))]
        named["part"] = [[named[f"part{g}_{j}"] for j in range(3)] for g in range(len(GROUPS))]
        named["came"] = [[named[f"came{g}_{j}"] for j in range(3)] for g in range(len(GROUPS))]
        named["full"] = [named[f"full{g}"] for g in range(len(GROUPS))]
        inner = SimpleNamespace(**vars(cfg))
        inner.names = list(named)
        mega(inner, *named.values())

    result = pl.pallas_call(
        body,
        out_shape=[jax.ShapeDtypeStruct(s, t) for _, s, t, _ in outs],
        in_specs=[pl.BlockSpec(memory_space=m) for _, _, m in ins],
        out_specs=[pl.BlockSpec(memory_space=m) for _, _, _, m in outs],
        scratch_shapes=[s for _, s in scratch],
        compiler_params=pltpu.CompilerParams(
            collective_id=0, has_side_effects=True, vmem_limit_bytes=60 << 20
        ),
    )(*[a for _, a, _ in ins])
    result = list(result)
    result[0] = result[0][:, :, :wv, :]
    result[3] = result[3].reshape(3, 3, LANES, LANES)
    result[7] = result[7].reshape(3, 3, LANES, LANES)
    return tuple(result)


def solution(mesh):
    nr, nc = mesh.shape["rows"], mesh.shape["crops"]
    whole = P()
    return jax.shard_map(
        functools.partial(on_device, nr, nc),
        mesh=mesh,
        in_specs=(P("crops", "rows", None, None),)
        + (whole,) * 11
        + (P("crops", None), P("crops"), P(("crops", "rows"), None, None, None)),
        out_specs=(P(("crops", "rows"), None, None, None), P("crops", "rows", None, None))
        + (whole,) * 11,
        check_vma=False,
    )
```

```python
import functools
from types import SimpleNamespace

import jax
import jax.numpy as jnp
from jax import lax
from jax.experimental import pallas as pl
from jax.experimental.pallas import tpu as pltpu
from jax.sharding import PartitionSpec as P

MESH = pl.DeviceIdType.MESH
F32 = jnp.float32
BF16 = jnp.bfloat16
epsilon = 1e-05
PAD = 32
LANES = 128

ROUND_ROWS = (4, 2, 16, 2, 2, 8, 8, 2, 2, 12, 2, 2)

GROUPS = (
    (("expand_two", 512), ("spatial_two", 1152)),
    (("reduce_two", 512), ("expand_one", 512), ("shortcut", 1024)),
    (("spatial_one", 1152), ("reduce_one", 256)),
)


def group_rows(group, devices):
    unit = 16 * devices
    return -(-sum(rows for _, rows in group) // unit) * unit


def dot(a, b):
    return lax.dot_general(a, b, (((1,), (0,)), ((), ())), preferred_element_type=F32)


def dot_nt(a, b):
    return lax.dot_general(a, b, (((1,), (1,)), ((), ())), preferred_element_type=F32)


def dot_tn(a, b):
    return lax.dot_general(a, b, (((0,), (0,)), ((), ())), preferred_element_type=F32)


def half_silu(h, half_mask=0.5):
    t = jnp.tanh(h)
    p = h * t
    return h + p, (half_mask + half_mask * t) * (1.0 + (h - p))


def folded(x):
    return jnp.sum(x.reshape(-1, 8, x.shape[-1]), axis=0)


def row_sum(x):
    return jnp.sum(x, axis=0, keepdims=True)


def flat2(x):
    return x.reshape(-1, x.shape[-1])


def mega(cfg, *refs):
    r = SimpleNamespace(**dict(zip(cfg.names, refs)))
    nr, nc, nk, hh, wv = cfg.nr, cfg.nc, cfg.nk, cfg.hh, cfg.wv
    ndev, nxy, own = nr * nc, nc // 2, nk // nr
    m_half = hh * PAD
    row = lax.axis_index("rows")
    col = lax.axis_index("crops")
    xy, core = lax.div(col, 2), lax.rem(col, 2)
    me = row * nc + col

    image_copies = [
        pltpu.make_async_copy(r.images.at[k], r.x_in.at[k], r.image_sem.at[k]) for k in range(nk)
    ]
    for copy in image_copies:
        copy.start()

    barrier = pltpu.get_barrier_semaphore()

    def place(i):
        return (lax.div(i, nc), lax.rem(i, nc))

    def greet(k, c):
        pl.semaphore_signal(
            barrier, inc=1, device_id=place(lax.rem(me + k, ndev)), device_id_type=MESH
        )
        return c

    lax.fori_loop(1, ndev, greet, 0)

    lane = lax.broadcasted_iota(jnp.int32, (1, LANES), 1)
    for k in range(nk):
        gate = (jnp.full((1, LANES), r.depth_gate[k], jnp.int32) > 0).astype(F32)
        r.mask_one[k] = (lane < r.widths[0, k]).astype(F32)
        r.mask_two[k] = (lane < r.widths[1, k]).astype(F32) * gate
        r.gates[k] = jnp.concatenate([gate] * 4, axis=1)
    col_mask = (lax.broadcasted_iota(jnp.int32, (PAD, 1), 0) < wv).astype(F32)
    half_mask = 0.5 * col_mask

    def tap(ref, i, j):
        return ref[i, j * LANES : (j + 1) * LANES, :].T

    for i in range(3):
        for j in range(3):
            r.back_two[i, j * LANES : (j + 1) * LANES, :] = tap(r.spatial_two, 2 - i, 2 - j)
    zeros = jnp.zeros((LANES, LANES), BF16)
    k1 = r.spatial_one
    here = [[tap(k1, 2, 2), tap(k1, 1, 2), tap(k1, 2, 1), tap(k1, 1, 1)],
            [tap(k1, 2, 0), tap(k1, 1, 0), zeros, zeros]]
    below = [[tap(k1, 0, 2), tap(k1, 0, 1)], [tap(k1, 0, 0), zeros]]
    for ref, blocks in ((r.back_here, here), (r.back_below, below)):
        for i, line in enumerate(blocks):
            for j, block in enumerate(line):
                ref[i * LANES : (i + 1) * LANES, j * LANES : (j + 1) * LANES] = block

    def send_sums(idx, vectors):
        buf, rows = r.sums[idx], ROUND_ROWS[idx]
        at = 0
        for v in vectors:
            for q in range(v.shape[1] // LANES):
                buf[me, at : at + 1, :] = v[:, q * LANES : (q + 1) * LANES]
                at += 1
        assert at == rows

        def send(k, c):
            pltpu.make_async_remote_copy(
                src_ref=buf.at[me],
                dst_ref=buf.at[me],
                send_sem=r.sum_send.at[idx],
                recv_sem=r.sum_recv.at[idx],
                device_id=place(lax.rem(me + k, ndev)),
                device_id_type=MESH,
            ).start()
            return c

        lax.fori_loop(1, ndev, send, 0)

    def take_sums(idx, widths):
        buf = r.sums[idx]
        others = buf.at[pl.ds(0, ndev - 1)]
        pltpu.make_async_copy(others, others, r.sum_recv.at[idx]).wait()
        total = jnp.sum(buf[...], axis=0)
        pltpu.make_async_copy(others, others, r.sum_send.at[idx]).wait()
        result, at = [], 0
        for w in widths:
            parts = [total[at + q : at + q + 1, :] for q in range(w // LANES)]
            at += w // LANES
            result.append(jnp.concatenate(parts, axis=1) if len(parts) > 1 else parts[0])
        return result

    up_ok, down_ok = row > 0, row < nr - 1
    from_above = jnp.where(row > 0, 1.0, 0.0)
    from_below = jnp.where(row < nr - 1, 1.0, 0.0)

    def halo(idx, up, src, dst):
        shift = -1 if up else 1
        return pltpu.make_async_remote_copy(
            src_ref=src,
            dst_ref=dst,
            send_sem=r.halo_send.at[idx],
            recv_sem=r.halo_recv.at[idx],
            device_id=(row + shift, col),
            device_id_type=MESH,
        )

    def halo_start(idx, up, src, dst):
        @pl.when(up_ok if up else down_ok)
        def _():
            halo(idx, up, src, dst).start()

    def halo_wait(idx, up, src, dst):
        @pl.when(up_ok if up else down_ok)
        def _():
            halo(idx, up, src, dst).wait_send()

        @pl.when(down_ok if up else up_ok)
        def _():
            halo(idx, up, src, dst).wait_recv()

    axes = (("core", 2), ("xy", nxy), ("rows", nr))
    seat = {"core": core, "xy": xy, "rows": row}

    def device_of(kind, i):
        if kind == "core":
            return (row, xy * 2 + i)
        if kind == "xy":
            return (row, i * 2 + core)
        return (i, col)

    def level_rows(g, level):
        size = cfg.group_size[g]
        for _, n in axes[:level]:
            size //= n
        return size

    def offset(g, level):
        at = 0
        for i, (kind, _) in enumerate(axes[:level]):
            at = at + seat[kind] * level_rows(g, i + 1)
        return pl.multiple_of(at, 16) if level else 0

    def scatter_send(g, level):
        kind, n = axes[level]
        chunk = level_rows(g, level + 1)
        for k in range(1, n):
            p = lax.rem(seat[kind] + k, n)
            pltpu.make_async_remote_copy(
                src_ref=r.part[g][level].at[pl.ds(pl.multiple_of(p * chunk, 16), chunk)],
                dst_ref=r.came[g][level].at[k - 1],
                send_sem=r.grad_send.at[g, level],
                recv_sem=r.grad_recv.at[g, level],
                device_id=device_of(kind, p),
                device_id_type=MESH,
            ).start()

    def scatter_take(g, level):
        kind, n = axes[level]
        chunk = level_rows(g, level + 1)
        came = r.came[g][level]
        pltpu.make_async_copy(came, came, r.grad_recv.at[g, level]).wait()
        mine = pl.ds(pl.multiple_of(seat[kind] * chunk, 16), chunk)
        total = r.part[g][level][mine, :].astype(F32) + jnp.sum(came[...].astype(F32), axis=0)
        pltpu.make_async_copy(came, came, r.grad_send.at[g, level]).wait()
        if level + 1 < len(axes):
            r.part[g][level + 1][...] = total.astype(BF16)
        else:
            r.full[g][pl.ds(offset(g, 3), chunk), :] = total.astype(BF16)

    def gather_send(g, level):
        kind, n = axes[level]
        size = level_rows(g, level + 1)
        region = r.full[g].at[pl.ds(offset(g, level + 1), size)]
        for k in range(1, n):
            p = lax.rem(seat[kind] + k, n)
            pltpu.make_async_remote_copy(
                src_ref=region,
                dst_ref=region,
                send_sem=r.grad_send.at[g, 3 + level],
                recv_sem=r.grad_recv.at[g, 3 + level],
                device_id=device_of(kind, p),
                device_id_type=MESH,
            ).start()

    def gather_take(g, level):
        n = axes[level][1]
        size = level_rows(g, level + 1) * (n - 1)
        bytes_of = r.full[g].at[pl.ds(0, size)]
        pltpu.make_async_copy(bytes_of, bytes_of, r.grad_recv.at[g, 3 + level]).wait()
        pltpu.make_async_copy(bytes_of, bytes_of, r.grad_send.at[g, 3 + level]).wait()

    steps = (
        (scatter_send, 0), (scatter_take, 0), (scatter_send, 1), (scatter_take, 1),
        (scatter_send, 2), (scatter_take, 2), (gather_send, 2), (gather_take, 2),
        (gather_send, 1), (gather_take, 1), (gather_send, 0), (gather_take, 0),
    )

    def advance(g, phase):
        for fn, level in steps[max(0, 2 * phase - 1) : 2 * phase + 1]:
            fn(g, level)

    def stage(g, name, value):
        at = 0
        for other, rows in GROUPS[g]:
            if other == name:
                break
            at += rows
        blocks = value.shape[1] // LANES
        for q in range(blocks):
            n = value.shape[0]
            lo = at + q * n
            r.part[g][0][lo : lo + n, :] = value[:, q * LANES : (q + 1) * LANES].astype(BF16)

    def coefficients(total, square, count, gain, bias):
        n = jnp.maximum(count, 1.0)
        mu = total / n
        inv = lax.rsqrt(square / n - mu * mu + epsilon)
        scale = gain * inv
        return SimpleNamespace(n=n, mu=mu, inv=inv, scale=scale, shift=bias - mu * scale)

    def backward(norm, dbias, dz_sum):
        dgain = norm.inv * (dz_sum - norm.mu * dbias)
        c2 = -norm.scale * norm.inv * dgain / norm.n
        c3 = -norm.scale * dbias / norm.n - c2 * norm.mu
        return dgain, (norm.scale, c2, c3)

    def loop(body, init=0):
        return lax.fori_loop(0, nk, body, init)

    def zero8(width, count):
        return tuple(jnp.zeros((8, width), F32) for _ in range(count))

    def row_pieces(src_of, dst_of, send, recv, local):
        pieces = []
        for w, (lo, hi) in enumerate(cfg.pieces):
            for k in range(1, nr):
                p = lax.rem(row + k, nr)
                pieces.append(
                    pltpu.make_async_remote_copy(
                        src_ref=src_of(p, lo, hi - lo),
                        dst_ref=dst_of(lo, hi - lo),
                        send_sem=send.at[w, k],
                        recv_sem=recv.at[w, k],
                        device_id=(p, col),
                        device_id_type=MESH,
                    )
                )
        here = pltpu.make_async_copy(src_of(row, 0, hh), dst_of(0, hh), local)
        return pieces, here

    def start_pieces(pieces, w):
        for copy in pieces[w * (nr - 1) : (w + 1) * (nr - 1)]:
            copy.start()

    cot_copies, cot_local = row_pieces(
        lambda p, lo, n: r.cot.at[:, pl.ds(p * hh + lo, n)],
        lambda lo, n: r.cot_rows.at[pl.ds(row * own, own), pl.ds(lo, n)],
        r.cot_send, r.cot_recv, r.local_sem.at[0],
    )
    out_copies, out_local = row_pieces(
        lambda p, lo, n: r.out_rows.at[pl.ds(p * own, own), pl.ds(lo, n)],
        lambda lo, n: r.out.at[:, pl.ds(row * hh + lo, n)],
        r.out_send, r.out_recv, r.local_sem.at[1],
    )
    cot_local.start()

    lane_blocks = cfg.c_in // LANES
    for slot in range(2 * hh):
        for q in range(lane_blocks):
            r.spread[q, slot, 2 * wv : 2 * PAD, :] = jnp.zeros((2 * PAD - 2 * wv, LANES), F32)
    w1 = r.reduce_one[...]
    acc = zero8(LANES, 2)
    for copy in image_copies:
        copy.wait()

    def first(k, acc):
        for i in range(2 * hh):
            for q in range(lane_blocks):
                lanes = slice(q * LANES, (q + 1) * LANES)
                r.spread[q, i, 0 : 2 * wv, :] = r.x_in[k, i, :, lanes].astype(F32)
        m = r.mask_one[k]
        s1, s2 = acc
        for pr in range(2):
            for pc in range(2):
                for i in range(hh):
                    for q in range(lane_blocks):
                        lanes = slice(q * LANES, (q + 1) * LANES)
                        r.x[pr, pc, k, i, :, lanes] = r.spread[
                            q, 2 * i + pr, pl.ds(pc, PAD, stride=2), :
                        ].astype(BF16)
                z = dot(flat2(r.x[pr, pc, k]), w1)
                r.z1[pr, pc, k] = z.reshape(hh, PAD, LANES)
                s1 += m * folded(z)
                s2 += m * folded(z * z)
        return s1, s2

    acc = lax.fori_loop(0, nk // 2, first, acc)
    pl.semaphore_wait(barrier, ndev - 1)
    start_pieces(cot_copies, 0)
    s1, s2 = lax.fori_loop(nk // 2, nk, first, acc)
    count_one = sum(r.mask_one[k] for k in range(nk))
    count_two = sum(r.mask_two[k] for k in range(nk))
    send_sums(0, [row_sum(s1), row_sum(s2), count_one, count_two])
    halo_z1 = (0, False, r.z1.at[1, :, :, hh - 1], r.h1)
    halo_start(*halo_z1)
    start_pieces(cot_copies, 1)

    sc = r.shortcut[...]

    def skip(k, acc):
        z = dot(flat2(r.x[0, 0, k]), sc)
        r.zs[k] = z.reshape(hh, PAD, cfg.c_out)
        return acc[0] + folded(z), acc[1] + folded(z * z)

    zs1, zs2 = loop(skip, zero8(cfg.c_out, 2))

    t1, t2, active_one, active_two = take_sums(0, [LANES] * 4)
    half_px, full_px = float(hh * wv), float(4 * hh * wv)
    active_gate = active_two[:, 0:1]
    g1, b1 = r.mid_gain[0:1, :], r.mid_bias[0:1, :]
    n1 = coefficients(t1, t2, active_one * full_px, g1, b1)
    halo_wait(*halo_z1)

    def shifted_right(a):
        return pltpu.roll(a, 1, axis=a.ndim - 2)

    def shifted_left(a):
        return pltpu.roll(a, PAD - 1, axis=a.ndim - 2)

    def affine(norm, m):
        return 0.5 * m * norm.scale, (0.5 * m * norm.shift) * col_mask

    k_one = [r.spatial_one[i] for i in range(3)]

    def second(k, acc):
        m = r.mask_one[k]
        ah, bh = affine(n1, m)
        for pr in range(2):
            for pc in range(2):
                a, s = half_silu(r.z1[pr, pc, k] * ah + bh, half_mask)
                r.s1[pr, pc, k] = s
                dst = r.even if pr == 0 else r.odd
                rows = pl.ds(0, hh) if pr == 0 else pl.ds(1, hh)
                if pc == 0:
                    dst[k, rows, :, LANES : 2 * LANES] = a.astype(BF16)
                else:
                    dst[k, rows, :, 2 * LANES : 3 * LANES] = a.astype(BF16)
                    dst[k, rows, :, 0:LANES] = shifted_right(a).astype(BF16)
        for pc in range(2):
            a, _ = half_silu(r.h1[pc, k] * ah + bh)
            a = jnp.where(row > 0, a, 0.0)
            if pc == 0:
                r.odd[k, 0, :, LANES : 2 * LANES] = a.astype(BF16)
            else:
                r.odd[k, 0, :, 2 * LANES : 3 * LANES] = a.astype(BF16)
                r.odd[k, 0, :, 0:LANES] = shifted_right(a).astype(BF16)
        z = dot(flat2(r.even[k]), k_one[1])
        z += dot(flat2(r.odd[k, 1 : hh + 1]), k_one[2])
        z += dot(flat2(r.odd[k, 0:hh]), k_one[0])
        z = z.reshape(hh, PAD, LANES) * col_mask
        r.z2[k] = z
        return acc[0] + m * folded(z), acc[1] + m * folded(z * z)

    s1, s2 = loop(second, zero8(LANES, 2))
    send_sums(1, [row_sum(s1), row_sum(s2)])
    halo_z2 = (1, True, r.z2.at[:, 0], r.h2)
    halo_start(*halo_z2)
    start_pieces(cot_copies, 2)
    t1, t2 = take_sums(1, [LANES] * 2)
    n2 = coefficients(t1, t2, active_one * half_px, r.mid_gain[1:2, :], r.mid_bias[1:2, :])
    e1 = r.expand_one[...]

    def third(k, acc):
        ah, bh = affine(n2, r.mask_one[k])
        a, s = half_silu(r.z2[k] * ah + bh, half_mask)
        r.s2[k] = s
        a = a.astype(BF16)
        r.a2[k] = a
        z = dot(flat2(a), e1)
        r.z3[k] = z.reshape(hh, PAD, cfg.c_out)
        return acc[0] + folded(z), acc[1] + folded(z * z)

    s1, s2 = loop(third, zero8(cfg.c_out, 2))
    send_sums(2, [row_sum(s1), row_sum(s2), row_sum(zs1), row_sum(zs2)])
    start_pieces(cot_copies, 3)
    t1, t2, ts1, ts2 = take_sums(2, [cfg.c_out] * 4)
    all_px = float(nk * nc) * float(nr) * half_px
    n3 = coefficients(t1, t2, all_px, r.wide_gain[0:1, :], r.wide_bias[0:1, :])
    ns = coefficients(ts1, ts2, all_px, r.wide_gain[1:2, :], r.wide_bias[1:2, :])
    w2 = r.reduce_two[...]

    def fourth(k, acc):
        a3, as_ = 0.5 * n3.scale, 0.5 * ns.scale
        b3 = (0.5 * (n3.shift + ns.shift)) * col_mask
        for i in range(hh):
            a, s = half_silu(r.z3[k, i] * a3 + r.zs[k, i] * as_ + b3, half_mask)
            r.hidden[k, i] = a.astype(BF16)
            r.s3[k, i] = s
        z = dot(flat2(r.hidden[k]), w2)
        r.z4[k] = z.reshape(hh, PAD, LANES)
        m = r.mask_two[k]
        return acc[0] + m * folded(z), acc[1] + m * folded(z * z)

    s1, s2 = loop(fourth, zero8(LANES, 2))
    send_sums(3, [row_sum(s1), row_sum(s2)])
    halos_z4 = [
        (2, False, r.z4.at[:, hh - 1], r.h4.at[0]),
        (3, True, r.z4.at[:, 0], r.h4.at[1]),
    ]
    for h in halos_z4:
        halo_start(*h)
    start_pieces(cot_copies, 4)
    t1, t2 = take_sums(3, [LANES] * 2)
    n4 = coefficients(t1, t2, active_two * half_px, r.mid_gain[2:3, :], r.mid_bias[2:3, :])
    for h in halos_z4:
        halo_wait(*h)

    def put3(dst, k, rows, a):
        dst[k, rows, :, LANES : 2 * LANES] = a.astype(BF16)
        dst[k, rows, :, 0:LANES] = shifted_right(a).astype(BF16)
        dst[k, rows, :, 2 * LANES : 3 * LANES] = shifted_left(a).astype(BF16)

    k_two = [r.spatial_two[i] for i in range(3)]

    def fifth(k, acc):
        m = r.mask_two[k]
        ah, bh = affine(n4, m)
        a, s = half_silu(r.z4[k] * ah + bh, half_mask)
        r.s4[k] = s
        put3(r.a4, k, pl.ds(1, hh), a)
        a, _ = half_silu(r.h4[0, k] * ah + bh)
        put3(r.a4, k, 0, jnp.where(row > 0, a, 0.0))
        a, _ = half_silu(r.h4[1, k] * ah + bh)
        put3(r.a4, k, hh + 1, jnp.where(row < nr - 1, a, 0.0))
        z = sum(dot(flat2(r.a4[k, i : i + hh]), k_two[i]) for i in range(3))
        z = z.reshape(hh, PAD, LANES) * col_mask
        r.z5[k] = z
        return acc[0] + m * folded(z), acc[1] + m * folded(z * z)

    s1, s2 = loop(fifth, zero8(LANES, 2))
    send_sums(4, [row_sum(s1), row_sum(s2)])
    halos_z5 = [
        (4, False, r.z5.at[:, hh - 1], r.h5.at[0]),
        (5, True, r.z5.at[:, 0], r.h5.at[1]),
    ]
    for h in halos_z5:
        halo_start(*h)
    start_pieces(cot_copies, 5)
    t1, t2 = take_sums(4, [LANES] * 2)
    n5 = coefficients(t1, t2, active_two * half_px, r.mid_gain[3:4, :], r.mid_bias[3:4, :])
    e2 = r.expand_two[...]

    def sixth(k, acc):
        ah, bh = affine(n5, r.mask_two[k])
        a, s = half_silu(r.z5[k] * ah + bh, half_mask)
        r.s5[k] = s
        a = a.astype(BF16)
        r.a5[k] = a
        z = dot(flat2(a), e2)
        r.z6[k] = z.reshape(hh, PAD, cfg.c_out)
        g = r.gates[k]
        return acc[0] + g * folded(z), acc[1] + g * folded(z * z)

    s1, s2 = loop(sixth, zero8(cfg.c_out, 2))
    send_sums(5, [row_sum(s1), row_sum(s2)])
    for copy in cot_copies:
        copy.wait()
    cot_local.wait()
    t1, t2 = take_sums(5, [cfg.c_out] * 2)
    gate_count = active_gate * half_px
    n6 = coefficients(t1, t2, gate_count, r.wide_gain[2:3, :], r.wide_bias[2:3, :])
    pad_rows = jnp.zeros((PAD - wv, cfg.c_out), F32)

    def cot_row(k, i):
        return jnp.concatenate([r.cot_rows[k, i].astype(F32), pad_rows], axis=0)

    def seventh(k, acc):
        g = r.gates[k]
        a6, b6 = (0.5 * g) * n6.scale, ((0.5 * g) * n6.shift) * col_mask
        d1, d2 = acc
        for i in range(hh):
            hid = r.hidden[k, i].astype(F32)
            z = r.z6[k, i]
            a, s = half_silu(0.5 * hid + (z * a6 + b6))
            r.out_rows[k, i] = jnp.where(g > 0.0, a, hid)[:wv].astype(BF16)
            live = g * cot_row(k, i) * s
            r.live[k, i] = live
            d1 += folded(live)
            d2 += folded(live * z)
        return d1, d2

    d1, d2 = loop(seventh, zero8(cfg.c_out, 2))
    send_sums(6, [row_sum(d1), row_sum(d2)])

    start_pieces(out_copies, 0)
    out_local.start()
    db6, q6 = take_sums(6, [cfg.c_out] * 2)
    dg6, (c1, c2, c3) = backward(n6, db6, q6)

    def eighth(k, acc, c1=c1, c2=c2, c3=c3):
        g = r.gates[k]
        f1, f2, f3 = g * c1, g * c2, (g * c3) * col_mask
        for i in range(hh):
            r.dz6[k, i] = (r.live[k, i] * f1 + r.z6[k, i] * f2 + f3).astype(BF16)
        q = dot_nt(flat2(r.dz6[k]), e2).reshape(hh, PAD, LANES) * r.s5[k]
        r.q5[k] = q
        m = r.mask_two[k]
        return acc[0] + m * folded(q), acc[1] + m * folded(q * r.z5[k])

    d1, d2 = loop(eighth, zero8(LANES, 2))
    send_sums(7, [row_sum(d1), row_sum(d2)])
    halos_q5 = [
        (6, False, r.q5.at[:, hh - 1], r.hq5.at[0]),
        (7, True, r.q5.at[:, 0], r.hq5.at[1]),
    ]
    for h in halos_q5:
        halo_start(*h)
    start_pieces(out_copies, 1)
    stage(0, "expand_two", dot_tn(flat2(r.a5[...]), flat2(r.dz6[...])))
    for h in halos_z5:
        halo_wait(*h)
    db5, q5 = take_sums(7, [LANES] * 2)
    dg5, (c1, c2, c3) = backward(n5, db5, q5)
    for h in halos_q5:
        halo_wait(*h)

    def ninth(k, acc, c1=c1, c2=c2, c3=c3):
        m = r.mask_two[k]
        f1, f2, f3 = m * c1, m * c2, (m * c3) * col_mask
        put3(r.dz5, k, pl.ds(1, hh), r.q5[k] * f1 + r.z5[k] * f2 + f3)
        d = r.hq5[0, k] * f1 + r.h5[0, k] * f2 + f3
        put3(r.dz5, k, 0, jnp.where(row > 0, d, 0.0))
        d = r.hq5[1, k] * f1 + r.h5[1, k] * f2 + f3
        put3(r.dz5, k, hh + 1, jnp.where(row < nr - 1, d, 0.0))
        q = sum(dot(flat2(r.dz5[k, i : i + hh]), r.back_two[i]) for i in range(3))
        q = q.reshape(hh, PAD, LANES) * r.s4[k]
        r.q4[k] = q
        return acc[0] + m * folded(q), acc[1] + m * folded(q * r.z4[k])

    d1, d2 = loop(ninth, zero8(LANES, 2))
    send_sums(8, [row_sum(d1), row_sum(d2)])
    start_pieces(out_copies, 2)
    d5 = flat2(r.dz5[:, 1 : hh + 1, :, LANES : 2 * LANES])
    stage(
        0,
        "spatial_two",
        jnp.concatenate([dot_tn(flat2(r.a4[:, i : i + hh]), d5) for i in range(3)], axis=0),
    )
    advance(0, 0)
    db4, q4 = take_sums(8, [LANES] * 2)
    dg4, (c1, c2, c3) = backward(n4, db4, q4)

    def tenth(k, acc, c1=c1, c2=c2, c3=c3):
        m, g = r.mask_two[k], r.gates[k]
        f1, f2, f3 = m * c1, m * c2, (m * c3) * col_mask
        r.dz4[k] = (r.q4[k] * f1 + r.z4[k] * f2 + f3).astype(BF16)
        back = dot_nt(flat2(r.dz4[k]), w2).reshape(hh, PAD, cfg.c_out)
        e1_, e2_, e3_ = acc
        for i in range(hh):
            d = back[i] + (1.0 - g) * cot_row(k, i) + r.live[k, i]
            q = d.astype(BF16).astype(F32) * r.s3[k, i]
            r.q3[k, i] = q
            e1_ += folded(q)
            e2_ += folded(q * r.z3[k, i])
            e3_ += folded(q * r.zs[k, i])
        return e1_, e2_, e3_

    d1, d2, d3 = loop(tenth, zero8(cfg.c_out, 3))
    send_sums(9, [row_sum(d1), row_sum(d2), row_sum(d3)])
    start_pieces(out_copies, 3)
    stage(1, "reduce_two", dot_tn(flat2(r.hidden[...]), flat2(r.dz4[...])))
    advance(0, 1)
    db3, q3, qs = take_sums(9, [cfg.c_out] * 3)
    dg3, (c1, c2, c3) = backward(n3, db3, q3)
    dgs, (p1, p2, p3) = backward(ns, db3, qs)

    def eleventh(k, acc, c1=c1, c2=c2, c3=c3):
        f3, h3 = c3 * col_mask, p3 * col_mask
        for i in range(hh):
            q = r.q3[k, i]
            r.dz3[k, i] = (q * c1 + r.z3[k, i] * c2 + f3).astype(BF16)
            r.dzs[k, i] = (q * p1 + r.zs[k, i] * p2 + h3).astype(BF16)
        q = dot_nt(flat2(r.dz3[k]), e1).reshape(hh, PAD, LANES) * r.s2[k]
        r.q2[k] = q
        m = r.mask_one[k]
        return acc[0] + m * folded(q), acc[1] + m * folded(q * r.z2[k])

    d1, d2 = loop(eleventh, zero8(LANES, 2))
    send_sums(10, [row_sum(d1), row_sum(d2)])
    halo_q2 = (8, True, r.q2.at[:, 0], r.hq2)
    halo_start(*halo_q2)
    start_pieces(out_copies, 4)
    stage(1, "expand_one", dot_tn(flat2(r.a2[...]), flat2(r.dz3[...])))
    stage(1, "shortcut", dot_tn(flat2(r.x[0, 0]), flat2(r.dzs[...])))
    advance(1, 0)
    advance(0, 2)
    halo_wait(*halo_z2)
    db2, q2 = take_sums(10, [LANES] * 2)
    dg2, (c1, c2, c3) = backward(n2, db2, q2)
    halo_wait(*halo_q2)

    def twelfth(k, acc, c1=c1, c2=c2, c3=c3):
        m = r.mask_one[k]
        f1, f2, f3 = m * c1, m * c2, (m * c3) * col_mask
        d = r.q2[k] * f1 + r.z2[k] * f2 + f3
        r.dz2[k, 0:hh, :, 0:LANES] = d.astype(BF16)
        r.dz2[k, 0:hh, :, LANES : 2 * LANES] = shifted_left(d).astype(BF16)
        d = jnp.where(row < nr - 1, r.hq2[k] * f1 + r.h2[k] * f2 + f3, 0.0)
        r.dz2[k, hh, :, 0:LANES] = d.astype(BF16)
        r.dz2[k, hh, :, LANES : 2 * LANES] = shifted_left(d).astype(BF16)
        u = dot(flat2(r.dz2[k, 0:hh]), r.back_here[...])
        v = dot(flat2(r.dz2[k, 1 : hh + 1]), r.back_below[...])
        s1, s2 = acc
        planes = (
            (1, 1, u[:, 0:LANES] + v[:, 0:LANES]),
            (0, 1, u[:, LANES : 2 * LANES]),
            (1, 0, u[:, 2 * LANES : 3 * LANES] + v[:, LANES : 2 * LANES]),
            (0, 0, u[:, 3 * LANES : 4 * LANES]),
        )
        for pr, pc, q in planes:
            q = q.reshape(hh, PAD, LANES) * r.s1[pr, pc, k]
            r.q1[pr, pc, k] = q
            s1 += m * folded(q)
            s2 += m * folded(q * r.z1[pr, pc, k])
        return s1, s2

    d1, d2 = loop(twelfth, zero8(LANES, 2))
    send_sums(11, [row_sum(d1), row_sum(d2)])
    start_pieces(out_copies, 5)
    d2_ = flat2(r.dz2[:, 0:hh, :, 0:LANES])
    lines = [r.odd[:, 0:hh], r.even[...], r.odd[:, 1 : hh + 1]]
    stage(
        2, "spatial_one", jnp.concatenate([dot_tn(flat2(a), d2_) for a in lines], axis=0)
    )
    advance(1, 1)
    advance(0, 3)

    def skip_back(k, c):
        r.skip_back[k] = dot_nt(flat2(r.dzs[k]), sc).reshape(hh, PAD, cfg.c_in)
        return c

    loop(skip_back)
    db1, q1 = take_sums(11, [LANES] * 2)
    dg1, (c1, c2, c3) = backward(n1, db1, q1)

    def last(k, acc, c1=c1, c2=c2, c3=c3):
        m = r.mask_one[k]
        f1, f2, f3 = m * c1, m * c2, (m * c3) * col_mask
        for pr in range(2):
            for pc in range(2):
                d = (r.q1[pr, pc, k] * f1 + r.z1[pr, pc, k] * f2 + f3).astype(BF16)
                r.dz1[pr, pc, k] = d
        return acc

    loop(last)
    total = sum(
        dot_tn(flat2(r.x[pr, pc]), flat2(r.dz1[pr, pc])) for pr in range(2) for pc in range(2)
    )
    stage(2, "reduce_one", total)
    advance(2, 0)
    advance(1, 2)
    advance(0, 4)

    def images_back(k, c):
        for pr in range(2):
            for pc in range(2):
                g = dot_nt(flat2(r.dz1[pr, pc, k]), w1).reshape(hh, PAD, cfg.c_in)
                if pr == 0 and pc == 0:
                    g += r.skip_back[k]
                for i in range(hh):
                    for q in range(lane_blocks):
                        r.spread[q, 2 * i + pr, pl.ds(pc, PAD, stride=2), :] = g[
                            i, :, q * LANES : (q + 1) * LANES
                        ]
        for i in range(2 * hh):
            for q in range(lane_blocks):
                lanes = slice(q * LANES, (q + 1) * LANES)
                r.x_in[k, i, :, lanes] = r.spread[q, i, 0 : 2 * wv, :].astype(BF16)
        return c

    loop(images_back)
    back_copy = pltpu.make_async_copy(r.x_in, r.images_grad, r.local_sem.at[2])
    back_copy.start()

    for k, v in enumerate((dg1, dg2, dg4, dg5, db1, db2, db4, db5)):
        r.mid_grads[k : k + 1, :] = v
    for k, v in enumerate((dg3, dgs, dg6, db3, db3, db6)):
        r.wide_grads[k : k + 1, :] = v

    for phase in range(1, 7):
        advance(2, phase)
        if phase + 2 <= 6:
            advance(1, phase + 2)
        if phase + 4 <= 6:
            advance(0, phase + 4)
    result_copies = [
        pltpu.make_async_copy(r.full[g], result, r.full_sem.at[g])
        for g, result in enumerate((r.summed0, r.summed1, r.summed2))
    ]
    for copy in result_copies:
        copy.start()
    for copy in result_copies:
        copy.wait()
    for copy in out_copies:
        copy.wait()
    out_local.wait()
    back_copy.wait()


def on_device(nr, nc, *args):
    (images, reduce_one, spatial_one, expand_one, shortcut, reduce_two, spatial_two, expand_two,
     mid_gain, mid_bias, wide_gain, wide_bias, widths, depth_gate, cot) = args
    nk, full_rows, full_cols, c_in = images.shape
    hh, wv, c_out = full_rows // 2, full_cols // 2, expand_one.shape[1]
    own = cot.shape[0]
    ndev, nxy = nr * nc, nc // 2
    sizes = [group_rows(g, ndev) for g in GROUPS]

    vmem, smem, hbm = pltpu.VMEM, pltpu.SMEM, pl.ANY
    ins = [
        ("images", images, hbm), ("cot", cot, hbm),
        ("reduce_one", reduce_one, vmem), ("spatial_one", spatial_one.reshape(3, 3 * LANES, LANES), vmem),
        ("expand_one", expand_one, vmem), ("shortcut", shortcut, vmem), ("reduce_two", reduce_two, vmem),
        ("spatial_two", spatial_two.reshape(3, 3 * LANES, LANES), vmem), ("expand_two", expand_two, vmem),
        ("mid_gain", mid_gain, vmem), ("mid_bias", mid_bias, vmem),
        ("wide_gain", wide_gain, vmem), ("wide_bias", wide_bias, vmem),
        ("widths", widths.T, smem), ("depth_gate", depth_gate, smem),
    ]
    outs = [
        ("out", cot.shape, BF16, hbm),
        ("images_grad", images.shape, BF16, hbm),
        ("summed0", (sizes[0], LANES), BF16, hbm),
        ("summed1", (sizes[1], LANES), BF16, hbm),
        ("summed2", (sizes[2], LANES), BF16, hbm),
        ("mid_grads", (8, LANES), F32, vmem), ("wide_grads", (6, c_out), F32, vmem),
    ]
    half, quad = (nk, hh, PAD), (2, 2, nk, hh, PAD)
    dma = pltpu.SemaphoreType.DMA
    scratch = [
        ("x_in", vmem(images.shape, BF16)),
        ("spread", vmem((c_in // LANES, 2 * hh, 2 * PAD, LANES), F32)),
        ("x", vmem(quad + (c_in,), BF16)),
        ("z1", vmem(quad + (LANES,), F32)),
        ("s1", vmem(quad + (LANES,), F32)),
        ("q1", vmem(quad + (LANES,), F32)),
        ("dz1", vmem(quad + (LANES,), BF16)),
        ("h1", vmem((2, nk, PAD, LANES), F32)),
        ("even", vmem(half + (3 * LANES,), BF16)),
        ("odd", vmem((nk, hh + 1, PAD, 3 * LANES), BF16)),
        ("dz2", vmem((nk, hh + 1, PAD, 2 * LANES), BF16)),
        ("a4", vmem((nk, hh + 2, PAD, 3 * LANES), BF16)),
        ("dz5", vmem((nk, hh + 2, PAD, 3 * LANES), BF16)),
        ("h2", vmem((nk, PAD, LANES), F32)),
        ("hq2", vmem((nk, PAD, LANES), F32)),
        ("h4", vmem((2, nk, PAD, LANES), F32)),
        ("h5", vmem((2, nk, PAD, LANES), F32)),
        ("hq5", vmem((2, nk, PAD, LANES), F32)),
        ("cot_rows", vmem((nk, hh, wv, c_out), BF16)),
        ("out_rows", vmem((nk, hh, wv, c_out), BF16)),
        ("skip_back", vmem(half + (c_in,), F32)),
        ("back_two", vmem((3, 3 * LANES, LANES), BF16)),
        ("back_here", vmem((2 * LANES, 4 * LANES), BF16)),
        ("back_below", vmem((2 * LANES, 2 * LANES), BF16)),
        ("mask_one", vmem((nk, 1, LANES), F32)),
        ("mask_two", vmem((nk, 1, LANES), F32)),
        ("gates", vmem((nk, 1, c_out), F32)),
    ]
    scratch += [(n, vmem(half + (LANES,), F32)) for n in ("z2", "s2", "q2", "z4", "s4", "q4", "z5", "s5", "q5")]
    scratch += [(n, vmem(half + (c_out,), F32)) for n in ("z3", "zs", "s3", "q3", "z6", "live")]
    scratch += [(n, vmem(half + (LANES,), BF16)) for n in ("a2", "a5", "dz4")]
    scratch += [(n, vmem(half + (c_out,), BF16)) for n in ("hidden", "dz6", "dz3", "dzs")]
    scratch += [
        ("image_sem", dma((nk,))), ("local_sem", dma((3,))),
        ("sum_send", dma((len(ROUND_ROWS),))), ("sum_recv", dma((len(ROUND_ROWS),))),
        ("halo_send", dma((9,))), ("halo_recv", dma((9,))),
        ("cot_send", dma((6, nr))), ("cot_recv", dma((6, nr))),
        ("out_send", dma((6, nr))), ("out_recv", dma((6, nr))),
        ("full_sem", dma((len(GROUPS),))),
        ("grad_send", dma((len(GROUPS), 6))), ("grad_recv", dma((len(GROUPS), 6))),
    ]
    scratch += [(f"sums{i}", vmem((ndev, n, LANES), F32)) for i, n in enumerate(ROUND_ROWS)]
    for g, size in enumerate(sizes):
        levels = (size, size // 2, size // nc, size // ndev)
        for level, n in enumerate((2, nxy, nr)):
            scratch.append((f"part{g}_{level}", vmem((levels[level], LANES), BF16)))
            scratch.append((f"came{g}_{level}", vmem((n - 1, levels[level + 1], LANES), BF16)))
        scratch.append((f"full{g}", vmem((size, LANES), BF16)))
    cfg = SimpleNamespace(
        nr=nr, nc=nc, nk=nk, hh=hh, wv=wv, c_in=c_in, c_out=c_out, group_size=sizes,
        pieces=[(i * hh // 6, (i + 1) * hh // 6) for i in range(6)],
        names=[n for n, *_ in ins] + [n for n, *_ in outs] + [n for n, _ in scratch],
    )

    def body(*refs):
        named = dict(zip(cfg.names, refs))
        named["sums"] = [named[f"sums{i}"] for i in range(len(ROUND_ROWS))]
        named["part"] = [[named[f"part{g}_{j}"] for j in range(3)] for g in range(len(GROUPS))]
        named["came"] = [[named[f"came{g}_{j}"] for j in range(3)] for g in range(len(GROUPS))]
        named["full"] = [named[f"full{g}"] for g in range(len(GROUPS))]
        inner = SimpleNamespace(**vars(cfg))
        inner.names = list(named)
        mega(inner, *named.values())

    result = pl.pallas_call(
        body,
        out_shape=[jax.ShapeDtypeStruct(s, t) for _, s, t, _ in outs],
        in_specs=[pl.BlockSpec(memory_space=m) for _, _, m in ins],
        out_specs=[pl.BlockSpec(memory_space=m) for _, _, _, m in outs],
        scratch_shapes=[s for _, s in scratch],
        compiler_params=pltpu.CompilerParams(
            collective_id=0, has_side_effects=True, vmem_limit_bytes=60 << 20
        ),
    )(*[a for _, a, _ in ins])
    return finished(result, mid_gain.shape, wide_gain.shape)


WEIGHTS = (
    ("reduce_one", (256, 128)),
    ("spatial_one", (3, 3, 128, 128)),
    ("expand_one", (128, 512)),
    ("shortcut", (256, 512)),
    ("reduce_two", (512, 128)),
    ("spatial_two", (3, 3, 128, 128)),
    ("expand_two", (128, 512)),
)


def finish(*refs):
    ins, outs, held = refs[:7], refs[7:20], refs[20:27]
    wide_to, (in_sem, out_sem) = refs[27:38], refs[38:]
    chunks = [(0, i) for i in range(4)] + [(1, i) for i in range(4)]

    def part(ref, which, i):
        n = ref.shape[1 - which] // 4
        return ref.at[:, pl.ds(i * n, n)] if which == 0 else ref.at[pl.ds(i * n, n)]

    small = [pltpu.make_async_copy(ins[i], held[i], in_sem.at[i]) for i in (5, 6, 2, 3, 4)]
    large = [
        pltpu.make_async_copy(part(ins[w], w, i), part(held[w], w, i), in_sem.at[7 + 4 * w + i])
        for w, i in chunks
    ]
    for copy in small + large:
        copy.start()
    leaving = []

    def leave(src, dst):
        copy = pltpu.make_async_copy(src, dst, out_sem.at[len(leaving)])
        copy.start()
        leaving.append(copy)

    for i in range(2):
        small[i].wait()
    mid, wide = held[5], held[6]
    grads = (mid[0:4, :], mid[4:8, :], wide[0:3, :], wide[3:6, :])
    for ref, value, to in zip(wide_to[7:], grads, outs[9:]):
        ref[...] = value
        leave(ref, to)
    names = [name for name, _ in WEIGHTS]
    for g, group in enumerate(GROUPS):
        small[2 + g].wait()
        summed = held[2 + g]
        at = 0
        for name, rows in group:
            which = names.index(name)
            ref = wide_to[which]
            if len(ref.shape) == 4:
                for i in range(9):
                    lo = at + i * LANES
                    ref[i // 3, i % 3] = summed[lo : lo + LANES, :].astype(F32)
            else:
                n = ref.shape[0]
                for q in range(ref.shape[1] // LANES):
                    lo = at + q * n
                    ref[:, q * LANES : (q + 1) * LANES] = summed[lo : lo + n, :].astype(F32)
            leave(ref, outs[2 + which])
            at += rows
    for copy, (w, i) in zip(large, chunks):
        copy.wait()
        leave(part(held[w], w, i), part(outs[w], w, i))
    for copy in leaving:
        copy.wait()


def finished(parts, mid_shape, wide_shape):
    hbm = pl.BlockSpec(memory_space=pl.ANY)
    outs = [jax.ShapeDtypeStruct(p.shape, p.dtype) for p in parts[:2]]
    outs += [jax.ShapeDtypeStruct(s, F32) for _, s in WEIGHTS]
    outs += [jax.ShapeDtypeStruct(s, F32) for s in (mid_shape, mid_shape, wide_shape, wide_shape)]
    dma = pltpu.SemaphoreType.DMA
    return tuple(
        pl.pallas_call(
            finish,
            out_shape=outs,
            in_specs=[hbm] * 7,
            out_specs=[hbm] * 13,
            scratch_shapes=[pltpu.VMEM(p.shape, p.dtype) for p in parts]
            + [pltpu.VMEM(o.shape, o.dtype) for o in outs[2:]]
            + [dma((15,)), dma((19,))],
            compiler_params=pltpu.CompilerParams(vmem_limit_bytes=60 << 20),
        )(*parts)
    )


def solution(mesh):
    nr, nc = mesh.shape["rows"], mesh.shape["crops"]
    whole = P()
    return jax.shard_map(
        functools.partial(on_device, nr, nc),
        mesh=mesh,
        in_specs=(P("crops", "rows", None, None),)
        + (whole,) * 11
        + (P("crops", None), P("crops"), P(("crops", "rows"), None, None, None)),
        out_specs=(P(("crops", "rows"), None, None, None), P("crops", "rows", None, None))
        + (whole,) * 11,
        check_vma=False,
    )
```

```python
import functools
from types import SimpleNamespace

import jax
import jax.numpy as jnp
from jax import lax
from jax.experimental import pallas as pl
from jax.experimental.pallas import tpu as pltpu
from jax.sharding import PartitionSpec as P

MESH = pl.DeviceIdType.MESH
F32 = jnp.float32
BF16 = jnp.bfloat16
epsilon = 1e-05
PAD = 32
LANES = 128

ROUND_ROWS = (4, 2, 8, 2, 2, 8, 8, 2, 2, 12, 2, 2)
WIDE = (2, 5, 6, 9)

GROUPS = (
    (("expand_two", 512),),
    (("spatial_two", 1152),),
    (("reduce_two", 512),),
    (("expand_one", 512), ("shortcut", 1024)),
    (("spatial_one", 1152),),
)


def group_rows(group, devices):
    unit = 16 * devices
    return -(-sum(rows for _, rows in group) // unit) * unit


def split(rows, parts):
    return [(i * rows // parts, (i + 1) * rows // parts) for i in range(parts)]


def dot(a, b):
    return lax.dot_general(a, b, (((1,), (0,)), ((), ())), preferred_element_type=F32)


def dot_nt(a, b):
    return lax.dot_general(a, b, (((1,), (1,)), ((), ())), preferred_element_type=F32)


def dot_tn(a, b):
    return lax.dot_general(a, b, (((0,), (0,)), ((), ())), preferred_element_type=F32)


def half_silu(h, half_mask=0.5):
    t = jnp.tanh(h)
    p = h * t
    return h + p, (half_mask + half_mask * t) * (1.0 + (h - p))


def folded(x):
    return jnp.sum(x.reshape(-1, 8, x.shape[-1]), axis=0)


def row_sum(x):
    return jnp.sum(x, axis=0, keepdims=True)


def flat2(x):
    return x.reshape(-1, x.shape[-1])


def mega(cfg, r):
    nr, nc, nk, hh, wv = cfg.nr, cfg.nc, cfg.nk, cfg.hh, cfg.wv
    ndev, nxy, own = nr * nc, nc // 2, nk // nr
    m_half = hh * PAD
    row = lax.axis_index("rows")
    col = lax.axis_index("crops")
    xy, core = lax.div(col, 2), lax.rem(col, 2)
    me = row * nc + col

    barrier = pltpu.get_barrier_semaphore()

    def place(i):
        return (lax.div(i, nc), lax.rem(i, nc))

    def greet(k, c):
        pl.semaphore_signal(
            barrier, inc=1, device_id=place(lax.rem(me + k, ndev)), device_id_type=MESH
        )
        return c

    lax.fori_loop(1, ndev, greet, 0)

    image_copies = [
        pltpu.make_async_copy(r.images.at[k], r.x_in.at[k], r.image_sem.at[k]) for k in range(nk)
    ]
    weight_copies = {
        name: pltpu.make_async_copy(r.weights[name], r.held[name], r.weight_sem.at[i])
        for i, name in enumerate(cfg.order)
    }
    for i, copy in enumerate(weight_copies.values()):
        copy.start()
        if i == 0:
            for other in image_copies:
                other.start()

    def arrived(*names):
        for name in names:
            weight_copies[name].wait()

    lane = lax.broadcasted_iota(jnp.int32, (1, LANES), 1)
    for k in range(nk):
        gate = (jnp.full((1, LANES), r.depth_gate[k], jnp.int32) > 0).astype(F32)
        r.mask_one[k] = (lane < r.widths[0, k]).astype(F32)
        r.mask_two[k] = (lane < r.widths[1, k]).astype(F32) * gate
        r.gates[k] = jnp.concatenate([gate] * 4, axis=1)
    col_mask = (lax.broadcasted_iota(jnp.int32, (PAD, 1), 0) < wv).astype(F32)
    half_mask = 0.5 * col_mask

    def to_all(copy_to):
        def send(k, c):
            copy_to(lax.rem(me + k, ndev)).start()
            return c

        lax.fori_loop(1, ndev, send, 0)

    def sum_copy(idx, p):
        mine = r.sums[idx].at[me]
        return pltpu.make_async_remote_copy(
            src_ref=mine,
            dst_ref=mine,
            send_sem=r.sum_send.at[idx],
            recv_sem=r.sum_recv.at[idx],
            device_id=place(p),
            device_id_type=MESH,
        )

    def pair_copy(step, src, dst):
        return pltpu.make_async_remote_copy(
            src_ref=src,
            dst_ref=dst,
            send_sem=r.pair_send.at[step],
            recv_sem=r.pair_recv.at[step],
            device_id=(row, xy * 2 + 1 - core),
            device_id_type=MESH,
        )

    def lines(vectors):
        return [v[:, q * LANES : (q + 1) * LANES] for v in vectors for q in range(v.shape[1] // LANES)]

    def send_sums(idx, vectors):
        rows = lines(vectors)
        assert len(rows) == ROUND_ROWS[idx]
        if idx in WIDE:
            half = len(rows) // 2
            both, came = r.both[idx], r.from_pair[idx]
            for at, v in enumerate(rows):
                both[at // half, at % half : at % half + 1, :] = v
            copy = pair_copy(idx, both.at[1 - core], came)
            copy.start()
            copy.wait()
            r.sums[idx][me] = both[core] + came[...]
        else:
            for at, v in enumerate(rows):
                r.sums[idx][me, at : at + 1, :] = v
        to_all(lambda p: sum_copy(idx, p))

    def take_sums(idx, widths):
        buf = r.sums[idx]
        others = buf.at[pl.ds(0, ndev - 1)]
        pltpu.make_async_copy(others, others, r.sum_recv.at[idx]).wait()
        if idx in WIDE:
            half = ROUND_ROWS[idx] // 2
            total = jnp.sum(buf[...].reshape(ndev // 2, 2, half, LANES), axis=0)
            rows = [total[at // half, at % half : at % half + 1, :] for at in range(2 * half)]
        else:
            total = jnp.sum(buf[...], axis=0)
            rows = [total[at : at + 1, :] for at in range(ROUND_ROWS[idx])]
        pltpu.make_async_copy(others, others, r.sum_send.at[idx]).wait()
        result, at = [], 0
        for w in widths:
            parts = rows[at : at + w // LANES]
            at += w // LANES
            result.append(jnp.concatenate(parts, axis=1) if len(parts) > 1 else parts[0])
        return result

    up_ok, down_ok = row > 0, row < nr - 1
    halo_up = (False, False, True, False, True, False, True, True, True)

    def halo(idx):
        return pltpu.make_async_remote_copy(
            src_ref=r.edge[idx],
            dst_ref=r.halo[idx],
            send_sem=r.halo_send.at[idx],
            recv_sem=r.halo_recv.at[idx],
            device_id=(row - 1 if halo_up[idx] else row + 1, col),
            device_id_type=MESH,
        )

    def halo_put(idx, at, rows):
        r.edge[idx][at] = rows.astype(BF16)

    def halo_start(idx):
        @pl.when(up_ok if halo_up[idx] else down_ok)
        def _():
            halo(idx).start()

    def halo_wait(idx):
        @pl.when(up_ok if halo_up[idx] else down_ok)
        def _():
            halo(idx).wait_send()

        @pl.when(down_ok if halo_up[idx] else up_ok)
        def _():
            halo(idx).wait_recv()

    def halo_row(idx, at, k):
        return r.halo[idx][at, k].astype(F32)

    def both_edges(idx, ref):
        halo_put(idx, 0, ref[:, hh - 1])
        halo_put(idx + 1, 0, ref[:, 0])

    chips = nr * nxy
    chip = row * nxy + xy

    def chip_copy(src, dst, to, send_sem, recv_sem):
        return pltpu.make_async_remote_copy(
            src_ref=src,
            dst_ref=dst,
            send_sem=send_sem,
            recv_sem=recv_sem,
            device_id=(lax.div(to, nxy), lax.rem(to, nxy) * 2 + core),
            device_id_type=MESH,
        )

    def to_chips(copy_to):
        def send(k, c):
            copy_to(lax.rem(chip + k, chips)).start()
            return c

        lax.fori_loop(1, chips, send, 0)

    def all_of(ref, n, sem):
        pltpu.make_async_copy(ref.at[pl.ds(0, n)], ref.at[pl.ds(0, n)], sem).wait()

    def skip_send(vectors):
        for at, v in enumerate(lines(vectors)):
            r.pair_rows[at // 4, at % 4 : at % 4 + 1, :] = v
        pair_copy(12, r.pair_rows.at[1 - core], r.pair_came).start()

    def skip_spread():
        pair_copy(12, r.pair_rows.at[1 - core], r.pair_came).wait()
        r.pair_chips[chip] = r.pair_rows[core] + r.pair_came[...]
        mine = r.pair_chips.at[chip]
        to_chips(lambda to: chip_copy(mine, mine, to, r.chip_send.at[0], r.chip_recv.at[0]))

    def skip_return():
        all_of(r.pair_chips, chips - 1, r.chip_recv.at[0])
        all_of(r.pair_chips, chips - 1, r.chip_send.at[0])
        r.pair_total[core] = jnp.sum(r.pair_chips[...], axis=0)
        mine = r.pair_total.at[core]
        pair_copy(13, mine, mine).start()

    def skip_take():
        mine = r.pair_total.at[core]
        pair_copy(13, mine, mine).wait()
        return [
            jnp.concatenate([r.pair_total[i, q : q + 1, :] for q in range(4)], axis=1)
            for i in range(2)
        ]

    axes = (("core", 2), ("xy", nxy), ("rows", nr))
    seat = {"core": core, "xy": xy, "rows": row}

    def device_of(kind, i):
        if kind == "core":
            return (row, xy * 2 + i)
        if kind == "xy":
            return (row, i * 2 + core)
        return (i, col)

    def level_rows(g, level):
        size = cfg.group_size[g]
        for _, n in axes[:level]:
            size //= n
        return size

    def offset(g, level):
        at = 0
        for i, (kind, _) in enumerate(axes[:level]):
            at = at + seat[kind] * level_rows(g, i + 1)
        return pl.multiple_of(at, 16) if level else 0

    def scatter_send(g, level):
        kind, n = axes[level]
        chunk = level_rows(g, level + 1)
        for k in range(1, n):
            p = lax.rem(seat[kind] + k, n)
            pltpu.make_async_remote_copy(
                src_ref=r.part[g][level].at[pl.ds(pl.multiple_of(p * chunk, 16), chunk)],
                dst_ref=r.came[g][level].at[k - 1],
                send_sem=r.grad_send.at[g, level],
                recv_sem=r.grad_recv.at[g, level],
                device_id=device_of(kind, p),
                device_id_type=MESH,
            ).start()

    def scatter_take(g, level):
        kind, n = axes[level]
        chunk = level_rows(g, level + 1)
        came = r.came[g][level]
        pltpu.make_async_copy(came, came, r.grad_recv.at[g, level]).wait()
        mine = pl.ds(pl.multiple_of(seat[kind] * chunk, 16), chunk)
        total = r.part[g][level][mine, :].astype(F32) + jnp.sum(came[...].astype(F32), axis=0)
        pltpu.make_async_copy(came, came, r.grad_send.at[g, level]).wait()
        if level + 1 < len(axes):
            r.part[g][level + 1][...] = total.astype(BF16)
        else:
            r.full[g][pl.ds(offset(g, 3), chunk), :] = total.astype(BF16)

    def gather_send(g, level):
        kind, n = axes[level]
        size = level_rows(g, level + 1)
        region = r.full[g].at[pl.ds(offset(g, level + 1), size)]
        for k in range(1, n):
            p = lax.rem(seat[kind] + k, n)
            pltpu.make_async_remote_copy(
                src_ref=region,
                dst_ref=region,
                send_sem=r.grad_send.at[g, 3 + level],
                recv_sem=r.grad_recv.at[g, 3 + level],
                device_id=device_of(kind, p),
                device_id_type=MESH,
            ).start()

    def gather_take(g, level):
        n = axes[level][1]
        size = level_rows(g, level + 1) * (n - 1)
        bytes_of = r.full[g].at[pl.ds(0, size)]
        pltpu.make_async_copy(bytes_of, bytes_of, r.grad_recv.at[g, 3 + level]).wait()
        pltpu.make_async_copy(bytes_of, bytes_of, r.grad_send.at[g, 3 + level]).wait()

    steps = (
        (scatter_send, 0), (scatter_take, 0), (scatter_send, 1), (scatter_take, 1),
        (scatter_send, 2), (scatter_take, 2), (gather_send, 2), (gather_take, 2),
        (gather_send, 1), (gather_take, 1), (gather_send, 0), (gather_take, 0),
    )

    def advance(g, phase):
        for fn, level in steps[max(0, 2 * phase - 1) : 2 * phase + 1]:
            fn(g, level)

    def stage(g, name, value):
        at = 0
        for other, rows in GROUPS[g]:
            if other == name:
                break
            at += rows
        blocks = value.shape[1] // LANES
        for q in range(blocks):
            n = value.shape[0]
            lo = at + q * n
            r.part[g][0][lo : lo + n, :] = value[:, q * LANES : (q + 1) * LANES].astype(BF16)

    def one_send(value):
        r.one_both[...] = value.reshape(2, chips, -1, LANES)
        pair_copy(14, r.one_both.at[1 - core], r.one_came).start()

    def one_spread():
        pair_copy(14, r.one_both.at[1 - core], r.one_came).wait()
        r.one_half[...] = r.one_both[core] + r.one_came[...]
        to_chips(
            lambda to: chip_copy(
                r.one_half.at[to], r.one_slots.at[chip], to, r.chip_send.at[1], r.chip_recv.at[1]
            )
        )

    def one_gather():
        all_of(r.one_slots, chips - 1, r.chip_recv.at[1])
        r.one_slots[chip] = r.one_half[chip]
        r.one_whole[core, chip] = jnp.sum(r.one_slots[...], axis=0)
        mine = r.one_whole.at[core, chip]
        to_chips(lambda to: chip_copy(mine, mine, to, r.chip_send.at[2], r.chip_recv.at[2]))

    def one_return():
        all_of(r.one_slots, chips - 1, r.chip_send.at[1])
        all_of(r.one_slots, chips - 1, r.chip_recv.at[2])
        all_of(r.one_slots, chips - 1, r.chip_send.at[2])
        pair_copy(15, r.one_whole.at[core], r.one_whole.at[core]).start()

    def one_take():
        pair_copy(15, r.one_whole.at[core], r.one_whole.at[core]).wait()

    def coefficients(total, square, count, gain, bias):
        n = jnp.maximum(count, 1.0)
        mu = total / n
        inv = lax.rsqrt(square / n - mu * mu + epsilon)
        scale = gain * inv
        return SimpleNamespace(n=n, mu=mu, inv=inv, scale=scale, shift=bias - mu * scale)

    def backward(norm, dbias, dz_sum):
        dgain = norm.inv * (dz_sum - norm.mu * dbias)
        c2 = -norm.scale * norm.inv * dgain / norm.n
        c3 = -norm.scale * dbias / norm.n - c2 * norm.mu
        return dgain, (norm.scale, c2, c3)

    def loop(body, init=0):
        return lax.fori_loop(0, nk, body, init)

    def zero8(width, count):
        return tuple(jnp.zeros((8, width), F32) for _ in range(count))

    def row_pieces(src_of, dst_of, send, recv, local):
        pieces = []
        for w, (lo, hi) in enumerate(cfg.pieces):
            for k in range(1, nr):
                p = lax.rem(row + k, nr)
                pieces.append(
                    pltpu.make_async_remote_copy(
                        src_ref=src_of(p, lo, hi - lo),
                        dst_ref=dst_of(lo, hi - lo),
                        send_sem=send,
                        recv_sem=recv,
                        device_id=(p, col),
                        device_id_type=MESH,
                    )
                )
        here = pltpu.make_async_copy(src_of(row, 0, hh), dst_of(0, hh), local)
        return pieces, here

    def wait_pieces(which):
        bytes_of = r.out_rows.at[pl.ds(0, nk - own)]
        pltpu.make_async_copy(bytes_of, bytes_of, r.row_recv.at[which]).wait()
        pltpu.make_async_copy(bytes_of, bytes_of, r.row_send.at[which]).wait()

    def start_pieces(pieces, *which):
        for w in which:
            for copy in pieces[w * (nr - 1) : (w + 1) * (nr - 1)]:
                copy.start()

    cot_copies, cot_local = row_pieces(
        lambda p, lo, n: r.cot.at[:, pl.ds(p * hh + lo, n)],
        lambda lo, n: r.cot_rows.at[pl.ds(row * own, own), pl.ds(lo, n)],
        r.row_send.at[0], r.row_recv.at[0], r.local_sem.at[0],
    )
    out_copies, out_local = row_pieces(
        lambda p, lo, n: r.out_rows.at[pl.ds(p * own, own), pl.ds(lo, n)],
        lambda lo, n: r.out.at[:, pl.ds(row * hh + lo, n)],
        r.row_send.at[1], r.row_recv.at[1], r.local_sem.at[1],
    )
    cot_local.start()

    lane_blocks = cfg.c_in // LANES
    for slot in range(2 * hh):
        for q in range(lane_blocks):
            r.spread[q, slot, 2 * wv : 2 * PAD, :] = jnp.zeros((2 * PAD - 2 * wv, LANES), F32)
    arrived("reduce_one")
    w1 = r.reduce_one[...]
    acc = zero8(LANES, 2)
    for copy in image_copies:
        copy.wait()

    def first(k, acc):
        for i in range(2 * hh):
            for q in range(lane_blocks):
                lanes = slice(q * LANES, (q + 1) * LANES)
                r.spread[q, i, 0 : 2 * wv, :] = r.x_in[k, i, :, lanes].astype(F32)
        m = r.mask_one[k]
        s1, s2 = acc
        for pr in range(2):
            for pc in range(2):
                for i in range(hh):
                    for q in range(lane_blocks):
                        lanes = slice(q * LANES, (q + 1) * LANES)
                        r.x[pr, pc, k, i, :, lanes] = r.spread[
                            q, 2 * i + pr, pl.ds(pc, PAD, stride=2), :
                        ].astype(BF16)
                z = dot(flat2(r.x[pr, pc, k]), w1)
                r.z1[pr, pc, k] = z.reshape(hh, PAD, LANES)
                s1 += m * folded(z)
                s2 += m * folded(z * z)
        return s1, s2

    s1, s2 = loop(first, acc)
    count_one = sum(r.mask_one[k] for k in range(nk))
    count_two = sum(r.mask_two[k] for k in range(nk))
    arrived("shortcut")
    sc = r.shortcut[...]

    def skip(k, acc):
        z = dot(flat2(r.x[0, 0, k]), sc)
        r.zs[k] = z.reshape(hh, PAD, cfg.c_out)
        return acc[0] + folded(z), acc[1] + folded(z * z)

    zs1, zs2 = loop(skip, zero8(cfg.c_out, 2))
    for pc in range(2):
        halo_put(0, pc, r.z1[1, pc, :, hh - 1])
    pl.semaphore_wait(barrier, ndev - 1)
    send_sums(0, [row_sum(s1), row_sum(s2), count_one, count_two])
    halo_start(0)
    skip_send([row_sum(zs1), row_sum(zs2)])
    start_pieces(cot_copies, 0)
    arrived("mid_gain", "mid_bias", "spatial_one")
    t1, t2, active_one, active_two = take_sums(0, [LANES] * 4)
    half_px, full_px = float(hh * wv), float(4 * hh * wv)
    active_gate = active_two[:, 0:1]
    g1, b1 = r.mid_gain[0:1, :], r.mid_bias[0:1, :]
    n1 = coefficients(t1, t2, active_one * full_px, g1, b1)
    halo_wait(0)

    def shifted_right(a):
        return pltpu.roll(a, 1, axis=a.ndim - 2)

    def shifted_left(a):
        return pltpu.roll(a, PAD - 1, axis=a.ndim - 2)

    def affine(norm, m):
        return 0.5 * m * norm.scale, (0.5 * m * norm.shift) * col_mask

    k_one = [r.spatial_one[i] for i in range(3)]

    def second(k, acc):
        m = r.mask_one[k]
        ah, bh = affine(n1, m)
        for pr in range(2):
            for pc in range(2):
                a, s = half_silu(r.z1[pr, pc, k] * ah + bh, half_mask)
                r.s1[pr, pc, k] = s
                dst = r.even if pr == 0 else r.odd
                rows = pl.ds(0, hh) if pr == 0 else pl.ds(1, hh)
                if pc == 0:
                    dst[k, rows, :, LANES : 2 * LANES] = a.astype(BF16)
                else:
                    dst[k, rows, :, 2 * LANES : 3 * LANES] = a.astype(BF16)
                    dst[k, rows, :, 0:LANES] = shifted_right(a).astype(BF16)
        for pc in range(2):
            a, _ = half_silu(halo_row(0, pc, k) * ah + bh)
            a = jnp.where(row > 0, a, 0.0)
            if pc == 0:
                r.odd[k, 0, :, LANES : 2 * LANES] = a.astype(BF16)
            else:
                r.odd[k, 0, :, 2 * LANES : 3 * LANES] = a.astype(BF16)
                r.odd[k, 0, :, 0:LANES] = shifted_right(a).astype(BF16)
        z = dot(flat2(r.even[k]), k_one[1])
        z += dot(flat2(r.odd[k, 1 : hh + 1]), k_one[2])
        z += dot(flat2(r.odd[k, 0:hh]), k_one[0])
        z = z.reshape(hh, PAD, LANES) * col_mask
        r.z2[k] = z
        return acc[0] + m * folded(z), acc[1] + m * folded(z * z)

    s1, s2 = loop(second, zero8(LANES, 2))
    send_sums(1, [row_sum(s1), row_sum(s2)])
    skip_spread()
    start_pieces(cot_copies, 1)

    def early(k, c):
        m = r.mask_one[k]
        for pr in range(2):
            for pc in range(2):
                zhat = (r.z1[pr, pc, k] - n1.mu) * (m * n1.inv)
                r.dz1[pr, pc, k] = zhat.astype(BF16)
        r.dz4[k] = jnp.broadcast_to(m, (hh, PAD, LANES)).astype(BF16)
        return c

    loop(early)
    for name in ("expand_one", "wide_gain", "wide_bias", "reduce_two"):
        arrived(name)
    planes = [(pr, pc) for pr in range(2) for pc in range(2)]
    r.part_z[...] = sum(dot_tn(flat2(r.x[q]), flat2(r.dz1[q])) for q in planes)
    r.part_m[...] = sum(dot_tn(flat2(r.x[q]), flat2(r.dz4[...])) for q in planes)
    t1, t2 = take_sums(1, [LANES] * 2)
    n2 = coefficients(t1, t2, active_one * half_px, r.mid_gain[1:2, :], r.mid_bias[1:2, :])
    e1 = r.expand_one[...]

    def third(k, acc):
        ah, bh = affine(n2, r.mask_one[k])
        a, s = half_silu(r.z2[k] * ah + bh, half_mask)
        r.s2[k] = s
        a = a.astype(BF16)
        r.a2[k] = a
        z = dot(flat2(a), e1)
        r.z3[k] = z.reshape(hh, PAD, cfg.c_out)
        return acc[0] + folded(z), acc[1] + folded(z * z)

    s1, s2 = loop(third, zero8(cfg.c_out, 2))
    send_sums(2, [row_sum(s1), row_sum(s2)])
    start_pieces(cot_copies, 2, 3)
    arrived("spatial_two", "expand_two")
    def tap(ref, i, j):
        return ref[i, j * LANES : (j + 1) * LANES, :].T

    for i in range(3):
        for j in range(3):
            r.back_two[i, j * LANES : (j + 1) * LANES, :] = tap(r.spatial_two, 2 - i, 2 - j)
    zeros = jnp.zeros((LANES, LANES), BF16)
    k1 = r.spatial_one
    here = [[tap(k1, 2, 2), tap(k1, 1, 2), tap(k1, 2, 1), tap(k1, 1, 1)],
            [tap(k1, 2, 0), tap(k1, 1, 0), zeros, zeros]]
    below = [[tap(k1, 0, 2), tap(k1, 0, 1)], [tap(k1, 0, 0), zeros]]
    for ref, blocks in ((r.back_here, here), (r.back_below, below)):
        for i, line in enumerate(blocks):
            for j, block in enumerate(line):
                ref[i * LANES : (i + 1) * LANES, j * LANES : (j + 1) * LANES] = block
    skip_return()
    t1, t2 = take_sums(2, [cfg.c_out] * 2)
    ts1, ts2 = skip_take()
    all_px = float(nk * nc) * float(nr) * half_px
    n3 = coefficients(t1, t2, all_px, r.wide_gain[0:1, :], r.wide_bias[0:1, :])
    ns = coefficients(ts1, ts2, all_px, r.wide_gain[1:2, :], r.wide_bias[1:2, :])
    w2 = r.reduce_two[...]

    def fourth(k, acc):
        a3, as_ = 0.5 * n3.scale, 0.5 * ns.scale
        b3 = (0.5 * (n3.shift + ns.shift)) * col_mask
        for i in range(hh):
            a, s = half_silu(r.z3[k, i] * a3 + r.zs[k, i] * as_ + b3, half_mask)
            r.hidden[k, i] = a.astype(BF16)
            r.s3[k, i] = s
        z = dot(flat2(r.hidden[k]), w2)
        r.z4[k] = z.reshape(hh, PAD, LANES)
        m = r.mask_two[k]
        return acc[0] + m * folded(z), acc[1] + m * folded(z * z)

    s1, s2 = loop(fourth, zero8(LANES, 2))
    send_sums(3, [row_sum(s1), row_sum(s2)])
    both_edges(1, r.z4)
    halo_start(1)
    halo_start(2)
    start_pieces(cot_copies, 4)
    t1, t2 = take_sums(3, [LANES] * 2)
    n4 = coefficients(t1, t2, active_two * half_px, r.mid_gain[2:3, :], r.mid_bias[2:3, :])
    halo_wait(1)
    halo_wait(2)

    def put3(dst, k, rows, a):
        dst[k, rows, :, LANES : 2 * LANES] = a.astype(BF16)
        dst[k, rows, :, 0:LANES] = shifted_right(a).astype(BF16)
        dst[k, rows, :, 2 * LANES : 3 * LANES] = shifted_left(a).astype(BF16)

    k_two = [r.spatial_two[i] for i in range(3)]

    def fifth(k, acc):
        m = r.mask_two[k]
        ah, bh = affine(n4, m)
        a, s = half_silu(r.z4[k] * ah + bh, half_mask)
        r.s4[k] = s
        put3(r.a4, k, pl.ds(1, hh), a)
        a, _ = half_silu(halo_row(1, 0, k) * ah + bh)
        put3(r.a4, k, 0, jnp.where(row > 0, a, 0.0))
        a, _ = half_silu(halo_row(2, 0, k) * ah + bh)
        put3(r.a4, k, hh + 1, jnp.where(row < nr - 1, a, 0.0))
        z = sum(dot(flat2(r.a4[k, i : i + hh]), k_two[i]) for i in range(3))
        z = z.reshape(hh, PAD, LANES) * col_mask
        r.z5[k] = z
        return acc[0] + m * folded(z), acc[1] + m * folded(z * z)

    s1, s2 = loop(fifth, zero8(LANES, 2))
    send_sums(4, [row_sum(s1), row_sum(s2)])
    start_pieces(cot_copies, 5, 6)
    t1, t2 = take_sums(4, [LANES] * 2)
    n5 = coefficients(t1, t2, active_two * half_px, r.mid_gain[3:4, :], r.mid_bias[3:4, :])
    e2 = r.expand_two[...]

    def sixth(k, acc):
        ah, bh = affine(n5, r.mask_two[k])
        a, s = half_silu(r.z5[k] * ah + bh, half_mask)
        r.s5[k] = s
        a = a.astype(BF16)
        r.a5[k] = a
        z = dot(flat2(a), e2)
        r.z6[k] = z.reshape(hh, PAD, cfg.c_out)
        g = r.gates[k]
        return acc[0] + g * folded(z), acc[1] + g * folded(z * z)

    s1, s2 = loop(sixth, zero8(cfg.c_out, 2))
    send_sums(5, [row_sum(s1), row_sum(s2)])
    both_edges(3, r.z5)
    halo_start(3)
    halo_start(4)
    wait_pieces(0)
    cot_local.wait()
    t1, t2 = take_sums(5, [cfg.c_out] * 2)
    gate_count = active_gate * half_px
    n6 = coefficients(t1, t2, gate_count, r.wide_gain[2:3, :], r.wide_bias[2:3, :])
    pad_rows = jnp.zeros((PAD - wv, cfg.c_out), F32)

    def cot_row(k, i):
        return jnp.concatenate([r.cot_rows[k, i].astype(F32), pad_rows], axis=0)

    def seventh(k, acc):
        g = r.gates[k]
        a6, b6 = (0.5 * g) * n6.scale, ((0.5 * g) * n6.shift) * col_mask
        d1, d2 = acc
        for i in range(hh):
            hid = r.hidden[k, i].astype(F32)
            z = r.z6[k, i]
            a, s = half_silu(0.5 * hid + (z * a6 + b6))
            r.out_rows[k, i] = jnp.where(g > 0.0, a, hid)[:wv].astype(BF16)
            live = g * cot_row(k, i) * s
            r.live[k, i] = live
            d1 += folded(live)
            d2 += folded(live * z)
        return d1, d2

    d1, d2 = loop(seventh, zero8(cfg.c_out, 2))
    send_sums(6, [row_sum(d1), row_sum(d2)])

    start_pieces(out_copies, 0, 1)
    out_local.start()
    db6, q6 = take_sums(6, [cfg.c_out] * 2)
    dg6, (c1, c2, c3) = backward(n6, db6, q6)

    def eighth(k, acc, c1=c1, c2=c2, c3=c3):
        g = r.gates[k]
        f1, f2, f3 = g * c1, g * c2, (g * c3) * col_mask
        for i in range(hh):
            r.dz6[k, i] = (r.live[k, i] * f1 + r.z6[k, i] * f2 + f3).astype(BF16)
        q = dot_nt(flat2(r.dz6[k]), e2).reshape(hh, PAD, LANES) * r.s5[k]
        r.q5[k] = q
        m = r.mask_two[k]
        return acc[0] + m * folded(q), acc[1] + m * folded(q * r.z5[k])

    d1, d2 = loop(eighth, zero8(LANES, 2))
    send_sums(7, [row_sum(d1), row_sum(d2)])
    both_edges(5, r.q5)
    halo_start(5)
    halo_start(6)
    start_pieces(out_copies, 2)
    stage(0, "expand_two", dot_tn(flat2(r.a5[...]), flat2(r.dz6[...])))
    advance(0, 0)
    halo_wait(3)
    halo_wait(4)
    db5, q5 = take_sums(7, [LANES] * 2)
    dg5, (c1, c2, c3) = backward(n5, db5, q5)
    halo_wait(5)
    halo_wait(6)

    def ninth(k, acc, c1=c1, c2=c2, c3=c3):
        m = r.mask_two[k]
        f1, f2, f3 = m * c1, m * c2, (m * c3) * col_mask
        put3(r.dz5, k, pl.ds(1, hh), r.q5[k] * f1 + r.z5[k] * f2 + f3)
        d = halo_row(5, 0, k) * f1 + halo_row(3, 0, k) * f2 + f3
        put3(r.dz5, k, 0, jnp.where(row > 0, d, 0.0))
        d = halo_row(6, 0, k) * f1 + halo_row(4, 0, k) * f2 + f3
        put3(r.dz5, k, hh + 1, jnp.where(row < nr - 1, d, 0.0))
        q = sum(dot(flat2(r.dz5[k, i : i + hh]), r.back_two[i]) for i in range(3))
        q = q.reshape(hh, PAD, LANES) * r.s4[k]
        r.q4[k] = q
        return acc[0] + m * folded(q), acc[1] + m * folded(q * r.z4[k])

    d1, d2 = loop(ninth, zero8(LANES, 2))
    send_sums(8, [row_sum(d1), row_sum(d2)])
    start_pieces(out_copies, 3)
    d5 = flat2(r.dz5[:, 1 : hh + 1, :, LANES : 2 * LANES])
    stage(
        1,
        "spatial_two",
        jnp.concatenate([dot_tn(flat2(r.a4[:, i : i + hh]), d5) for i in range(3)], axis=0),
    )
    halo_put(8, 0, r.z2[:, 0])
    halo_start(8)
    advance(0, 1)
    advance(1, 0)
    db4, q4 = take_sums(8, [LANES] * 2)
    dg4, (c1, c2, c3) = backward(n4, db4, q4)

    def tenth(k, acc, c1=c1, c2=c2, c3=c3):
        m, g = r.mask_two[k], r.gates[k]
        f1, f2, f3 = m * c1, m * c2, (m * c3) * col_mask
        r.dz4[k] = (r.q4[k] * f1 + r.z4[k] * f2 + f3).astype(BF16)
        back = dot_nt(flat2(r.dz4[k]), w2).reshape(hh, PAD, cfg.c_out)
        e1_, e2_, e3_ = acc
        for i in range(hh):
            d = back[i] + (1.0 - g) * cot_row(k, i) + r.live[k, i]
            q = d.astype(BF16).astype(F32) * r.s3[k, i]
            r.q3[k, i] = q
            e1_ += folded(q)
            e2_ += folded(q * r.z3[k, i])
            e3_ += folded(q * r.zs[k, i])
        return e1_, e2_, e3_

    d1, d2, d3 = loop(tenth, zero8(cfg.c_out, 3))
    send_sums(9, [row_sum(d1), row_sum(d2), row_sum(d3)])
    start_pieces(out_copies, 4)
    stage(2, "reduce_two", dot_tn(flat2(r.hidden[...]), flat2(r.dz4[...])))
    advance(1, 1)
    advance(0, 2)
    advance(2, 0)
    db3, q3, qs = take_sums(9, [cfg.c_out] * 3)
    dg3, (c1, c2, c3) = backward(n3, db3, q3)
    dgs, (p1, p2, p3) = backward(ns, db3, qs)

    def eleventh(k, acc, c1=c1, c2=c2, c3=c3):
        f3, h3 = c3 * col_mask, p3 * col_mask
        for i in range(hh):
            q = r.q3[k, i]
            r.dz3[k, i] = (q * c1 + r.z3[k, i] * c2 + f3).astype(BF16)
            r.dzs[k, i] = (q * p1 + r.zs[k, i] * p2 + h3).astype(BF16)
        q = dot_nt(flat2(r.dz3[k]), e1).reshape(hh, PAD, LANES) * r.s2[k]
        r.q2[k] = q
        m = r.mask_one[k]
        return acc[0] + m * folded(q), acc[1] + m * folded(q * r.z2[k])

    d1, d2 = loop(eleventh, zero8(LANES, 2))
    send_sums(10, [row_sum(d1), row_sum(d2)])
    halo_put(7, 0, r.q2[:, 0])
    halo_start(7)
    stage(3, "expand_one", dot_tn(flat2(r.a2[...]), flat2(r.dz3[...])))
    stage(3, "shortcut", dot_tn(flat2(r.x[0, 0]), flat2(r.dzs[...])))
    advance(3, 0)
    advance(1, 2)
    advance(2, 1)
    start_pieces(out_copies, 5)
    halo_wait(8)
    db2, q2 = take_sums(10, [LANES] * 2)
    dg2, (c1, c2, c3) = backward(n2, db2, q2)
    halo_wait(7)
    advance(3, 1)

    def twelfth(k, c, c1=c1, c2=c2, c3=c3):
        m = r.mask_one[k]
        f1, f2, f3 = m * c1, m * c2, (m * c3) * col_mask
        d = r.q2[k] * f1 + r.z2[k] * f2 + f3
        r.dz2[k, 0:hh, :, 0:LANES] = d.astype(BF16)
        r.dz2[k, 0:hh, :, LANES : 2 * LANES] = shifted_left(d).astype(BF16)
        d = jnp.where(row < nr - 1, halo_row(7, 0, k) * f1 + halo_row(8, 0, k) * f2 + f3, 0.0)
        r.dz2[k, hh, :, 0:LANES] = d.astype(BF16)
        r.dz2[k, hh, :, LANES : 2 * LANES] = shifted_left(d).astype(BF16)
        return c

    loop(twelfth)
    d2_ = flat2(r.dz2[:, 0:hh, :, 0:LANES])
    inputs = [r.odd[:, 0:hh], r.even[...], r.odd[:, 1 : hh + 1]]
    stage(4, "spatial_one", jnp.concatenate([dot_tn(flat2(a), d2_) for a in inputs], axis=0))
    advance(4, 0)

    def thirteenth(k, acc):
        m = r.mask_one[k]
        u = dot(flat2(r.dz2[k, 0:hh]), r.back_here[...])
        v = dot(flat2(r.dz2[k, 1 : hh + 1]), r.back_below[...])
        s1, s2 = acc
        parts = (
            (1, 1, u[:, 0:LANES] + v[:, 0:LANES]),
            (0, 1, u[:, LANES : 2 * LANES]),
            (1, 0, u[:, 2 * LANES : 3 * LANES] + v[:, LANES : 2 * LANES]),
            (0, 0, u[:, 3 * LANES : 4 * LANES]),
        )
        for pr, pc, q in parts:
            q = q.reshape(hh, PAD, LANES) * r.s1[pr, pc, k]
            r.q1[pr, pc, k] = q
            r.dz1[pr, pc, k] = (m * q).astype(BF16)
            s1 += m * folded(q)
            s2 += m * folded(q * r.z1[pr, pc, k])
        return s1, s2

    d1, d2 = loop(thirteenth, zero8(LANES, 2))
    send_sums(11, [row_sum(d1), row_sum(d2)])
    advance(4, 1)
    advance(0, 3)
    start_pieces(out_copies, 6)
    part_q = sum(dot_tn(flat2(r.x[q]), flat2(r.dz1[q])) for q in planes)
    advance(1, 3)
    advance(2, 2)

    def skip_back(k, c):
        r.skip_back[k] = dot_nt(flat2(r.dzs[k]), sc).reshape(hh, PAD, cfg.c_in)
        return c

    loop(skip_back)
    advance(3, 2)
    db1, q1 = take_sums(11, [LANES] * 2)
    dg1, (c1, c2, c3) = backward(n1, db1, q1)

    total = n1.scale * part_q
    total += (c2 / n1.inv) * r.part_z[...] + (c3 + c2 * n1.mu) * r.part_m[...]
    one_send(total)
    advance(4, 2)
    one_spread()
    advance(3, 3)
    advance(1, 4)
    advance(2, 3)
    advance(0, 4)

    def last(k, acc, c1=c1, c2=c2, c3=c3):
        m = r.mask_one[k]
        f1, f2, f3 = m * c1, m * c2, (m * c3) * col_mask
        for pr in range(2):
            for pc in range(2):
                d = (r.q1[pr, pc, k] * f1 + r.z1[pr, pc, k] * f2 + f3).astype(BF16)
                r.dz1[pr, pc, k] = d
        return acc

    loop(last)

    def images_back(k, c):
        for pr in range(2):
            for pc in range(2):
                g = dot_nt(flat2(r.dz1[pr, pc, k]), w1).reshape(hh, PAD, cfg.c_in)
                if pr == 0 and pc == 0:
                    g += r.skip_back[k]
                for i in range(hh):
                    for q in range(lane_blocks):
                        r.spread[q, 2 * i + pr, pl.ds(pc, PAD, stride=2), :] = g[
                            i, :, q * LANES : (q + 1) * LANES
                        ]
        for i in range(2 * hh):
            for q in range(lane_blocks):
                lanes = slice(q * LANES, (q + 1) * LANES)
                r.x_in[k, i, :, lanes] = r.spread[q, i, 0 : 2 * wv, :].astype(BF16)
        return c

    loop(images_back)
    back_copy = pltpu.make_async_copy(r.x_in, r.images_grad, r.local_sem.at[2])
    back_copy.start()

    for k, v in enumerate((dg1, dg2, dg4, dg5, db1, db2, db4, db5)):
        r.mid_held[k : k + 1, :] = v
    for k, v in enumerate((dg3, dgs, dg6, db3, db3, db6)):
        r.wide_held[k : k + 1, :] = v
    results = []

    def give(src, dst):
        copy = pltpu.make_async_copy(src, dst, r.full_sem.at[len(results)])
        copy.start()
        results.append(copy)

    give(r.mid_held, r.mid_grads)
    give(r.wide_held, r.wide_grads)

    def result(g):
        give(r.full[g], r.summed[g])

    advance(4, 3)
    one_gather()
    advance(3, 4)
    advance(1, 5)
    advance(2, 4)
    advance(0, 5)
    advance(4, 4)
    one_return()
    advance(3, 5)
    advance(1, 6)
    result(1)
    advance(2, 5)
    advance(0, 6)
    result(0)
    advance(4, 5)
    advance(3, 6)
    result(3)
    advance(2, 6)
    result(2)
    one_take()
    give(r.one_whole, r.summed_one)
    advance(4, 6)
    result(4)
    wait_pieces(1)
    out_local.wait()
    back_copy.wait()
    for copy in results:
        copy.wait()


def on_device(nr, nc, *args):
    (images, reduce_one, spatial_one, expand_one, shortcut, reduce_two, spatial_two, expand_two,
     mid_gain, mid_bias, wide_gain, wide_bias, widths, depth_gate, cot) = args
    nk, full_rows, full_cols, c_in = images.shape
    hh, wv, c_out = full_rows // 2, full_cols // 2, expand_one.shape[1]
    own = cot.shape[0]
    ndev, nxy, groups = nr * nc, nc // 2, len(GROUPS)
    sizes = [group_rows(g, ndev) for g in GROUPS]
    chunk = (ndev // 2, c_in // ndev, LANES)
    half, quad = (nk, hh, PAD), (2, 2, nk, hh, PAD)

    def f32(*shape):
        return pltpu.VMEM(shape, F32)

    def bf16(*shape):
        return pltpu.VMEM(shape, BF16)

    def dma(*shape):
        return pltpu.SemaphoreType.DMA(shape)

    def mid():
        return f32(*half, LANES)

    def wide():
        return f32(*half, c_out)

    def low(width):
        return bf16(*half, width)

    weights = dict(
        reduce_one=reduce_one, shortcut=shortcut, mid_gain=mid_gain, mid_bias=mid_bias,
        spatial_one=spatial_one.reshape(3, 3 * LANES, LANES), expand_one=expand_one,
        wide_gain=wide_gain, wide_bias=wide_bias, reduce_two=reduce_two,
        spatial_two=spatial_two.reshape(3, 3 * LANES, LANES), expand_two=expand_two,
    )
    scalars = dict(widths=widths.T, depth_gate=depth_gate)
    ins = dict(images=images, cot=cot, weights=weights)
    outs = dict(
        out=jax.ShapeDtypeStruct(cot.shape, BF16),
        images_grad=jax.ShapeDtypeStruct(images.shape, BF16),
        summed=[jax.ShapeDtypeStruct((size, LANES), BF16) for size in sizes],
        summed_one=jax.ShapeDtypeStruct((2,) + chunk, F32),
        mid_grads=jax.ShapeDtypeStruct((8, LANES), F32),
        wide_grads=jax.ShapeDtypeStruct((6, c_out), F32),
    )
    edges = [bf16(2 if i == 0 else 1, nk, PAD, LANES) for i in range(9)]
    levels = [(n, n // 2, n // nc, n // ndev) for n in sizes]
    halves = {i: ROUND_ROWS[i] // 2 for i in WIDE}
    scratch = dict(
        held={name: pltpu.VMEM(a.shape, a.dtype) for name, a in weights.items()},
        x_in=bf16(*images.shape), spread=f32(c_in // LANES, 2 * hh, 2 * PAD, LANES), x=bf16(*quad, c_in),
        z1=f32(*quad, LANES), s1=f32(*quad, LANES), q1=f32(*quad, LANES), dz1=bf16(*quad, LANES),
        part_z=f32(c_in, LANES), part_m=f32(c_in, LANES),
        one_both=f32(2, *chunk), one_came=f32(*chunk), one_half=f32(*chunk), one_slots=f32(*chunk),
        one_whole=f32(2, *chunk), mid_held=f32(8, LANES), wide_held=f32(6, c_out),
        pair_rows=f32(2, 4, LANES), pair_came=f32(4, LANES), pair_chips=f32(ndev // 2, 4, LANES),
        pair_total=f32(2, 4, LANES),
        even=low(3 * LANES), odd=bf16(nk, hh + 1, PAD, 3 * LANES), dz2=bf16(nk, hh + 1, PAD, 2 * LANES),
        a4=bf16(nk, hh + 2, PAD, 3 * LANES), dz5=bf16(nk, hh + 2, PAD, 3 * LANES),
        cot_rows=bf16(nk, hh, wv, c_out), out_rows=bf16(nk, hh, wv, c_out), skip_back=f32(*half, c_in),
        back_two=bf16(3, 3 * LANES, LANES), back_here=bf16(2 * LANES, 4 * LANES),
        back_below=bf16(2 * LANES, 2 * LANES),
        mask_one=f32(nk, 1, LANES), mask_two=f32(nk, 1, LANES), gates=f32(nk, 1, c_out),
        z2=mid(), s2=mid(), q2=mid(), z4=mid(), s4=mid(), q4=mid(), z5=mid(), s5=mid(), q5=mid(),
        z3=wide(), zs=wide(), s3=wide(), q3=wide(), z6=wide(), live=wide(),
        a2=low(LANES), a5=low(LANES), dz4=low(LANES),
        hidden=low(c_out), dz6=low(c_out), dz3=low(c_out), dzs=low(c_out),
        edge=edges, halo=edges,
        sums=[f32(ndev, halves.get(i, n), LANES) for i, n in enumerate(ROUND_ROWS)],
        both={i: f32(2, n, LANES) for i, n in halves.items()},
        from_pair={i: f32(n, LANES) for i, n in halves.items()},
        part=[[bf16(n[i], LANES) for i in range(3)] for n in levels],
        came=[[bf16(m - 1, n[i + 1], LANES) for i, m in enumerate((2, nxy, nr))] for n in levels],
        full=[bf16(n, LANES) for n in sizes],
        image_sem=dma(nk), local_sem=dma(3), full_sem=dma(groups + 3), weight_sem=dma(len(weights)),
        sum_send=dma(len(ROUND_ROWS)), sum_recv=dma(len(ROUND_ROWS)), halo_send=dma(9), halo_recv=dma(9),
        row_send=dma(2), row_recv=dma(2), pair_send=dma(16), pair_recv=dma(16), chip_send=dma(3),
        chip_recv=dma(3), grad_send=dma(groups, 6), grad_recv=dma(groups, 6),
    )
    cfg = SimpleNamespace(
        nr=nr, nc=nc, nk=nk, hh=hh, wv=wv, c_in=c_in, c_out=c_out, group_size=sizes,
        pieces=split(hh, 7), order=list(weights),
    )
    flat, trees = [], []
    for part in (scalars, ins, outs, scratch):
        leaves, tree = jax.tree.flatten(part)
        flat.append(leaves)
        trees.append(tree)

    def body(*refs):
        named, at = {}, 0
        for leaves, tree in zip(flat, trees):
            named.update(jax.tree.unflatten(tree, refs[at : at + len(leaves)]))
            at += len(leaves)
        mega(cfg, SimpleNamespace(**named, **named["held"]))

    smem, hbm = pl.BlockSpec(memory_space=pltpu.SMEM), pl.BlockSpec(memory_space=pl.ANY)
    result = pl.pallas_call(
        body,
        out_shape=flat[2],
        in_specs=[smem] * len(flat[0]) + [hbm] * len(flat[1]),
        out_specs=[hbm] * len(flat[2]),
        scratch_shapes=flat[3],
        compiler_params=pltpu.CompilerParams(
            collective_id=0, has_side_effects=True, vmem_limit_bytes=60 << 20
        ),
    )(*flat[0], *flat[1])
    made = SimpleNamespace(**jax.tree.unflatten(trees[2], result))
    parts = [made.out, made.images_grad, *made.summed, made.summed_one, made.mid_grads, made.wide_grads]
    return finished(parts, mid_gain.shape, wide_gain.shape)


WEIGHTS = (
    ("reduce_one", (256, 128)),
    ("spatial_one", (3, 3, 128, 128)),
    ("expand_one", (128, 512)),
    ("shortcut", (256, 512)),
    ("reduce_two", (512, 128)),
    ("spatial_two", (3, 3, 128, 128)),
    ("expand_two", (128, 512)),
)


def finish(*refs):
    n = len(GROUPS) + 5
    ins, outs, held = refs[:n], refs[n : n + 13], refs[n + 13 : 2 * n + 13]
    wide_to, (in_sem, out_sem) = refs[2 * n + 13 : 2 * n + 24], refs[2 * n + 24 :]
    chunks = [(0, i) for i in range(4)] + [(1, i) for i in range(4)]

    def part(ref, which, i):
        size = ref.shape[1 - which] // 4
        return ref.at[:, pl.ds(i * size, size)] if which == 0 else ref.at[pl.ds(i * size, size)]

    small = [pltpu.make_async_copy(ins[i], held[i], in_sem.at[i]) for i in (n - 2, n - 1, *range(2, n - 2))]
    large = [
        pltpu.make_async_copy(part(ins[w], w, i), part(held[w], w, i), in_sem.at[n + 4 * w + i])
        for w, i in chunks
    ]
    for copy in small + large:
        copy.start()
    leaving = []

    def leave(src, dst):
        copy = pltpu.make_async_copy(src, dst, out_sem.at[len(leaving)])
        copy.start()
        leaving.append(copy)

    for i in range(2):
        small[i].wait()
    mid, wide = held[n - 2], held[n - 1]
    grads = (mid[0:4, :], mid[4:8, :], wide[0:3, :], wide[3:6, :])
    for ref, value, to in zip(wide_to[7:], grads, outs[9:]):
        ref[...] = value
        leave(ref, to)
    names = [name for name, _ in WEIGHTS]
    for g, group in enumerate(GROUPS):
        small[2 + g].wait()
        summed = held[2 + g]
        at = 0
        for name, rows in group:
            which = names.index(name)
            ref = wide_to[which]
            if len(ref.shape) == 4:
                for i in range(9):
                    lo = at + i * LANES
                    ref[i // 3, i % 3] = summed[lo : lo + LANES, :].astype(F32)
            else:
                height = ref.shape[0]
                for q in range(ref.shape[1] // LANES):
                    lo = at + q * height
                    ref[:, q * LANES : (q + 1) * LANES] = summed[lo : lo + height, :].astype(F32)
            leave(ref, outs[2 + which])
            at += rows
    small[n - 3].wait()
    wide_to[0][...] = held[n - 3][...].reshape(wide_to[0].shape)
    leave(wide_to[0], outs[2])
    for copy, (w, i) in zip(large, chunks):
        copy.wait()
        leave(part(held[w], w, i), part(outs[w], w, i))
    for copy in leaving:
        copy.wait()


def finished(parts, mid_shape, wide_shape):
    hbm = pl.BlockSpec(memory_space=pl.ANY)
    outs = [jax.ShapeDtypeStruct(p.shape, p.dtype) for p in parts[:2]]
    outs += [jax.ShapeDtypeStruct(s, F32) for _, s in WEIGHTS]
    outs += [jax.ShapeDtypeStruct(s, F32) for s in (mid_shape, mid_shape, wide_shape, wide_shape)]
    dma = pltpu.SemaphoreType.DMA
    return tuple(
        pl.pallas_call(
            finish,
            out_shape=outs,
            in_specs=[hbm] * len(parts),
            out_specs=[hbm] * 13,
            scratch_shapes=[pltpu.VMEM(p.shape, p.dtype) for p in parts]
            + [pltpu.VMEM(o.shape, o.dtype) for o in outs[2:]]
            + [dma((len(parts) + 8,)), dma((19,))],
            compiler_params=pltpu.CompilerParams(vmem_limit_bytes=60 << 20),
        )(*parts)
    )


def solution(mesh):
    nr, nc = mesh.shape["rows"], mesh.shape["crops"]
    whole = P()
    return jax.shard_map(
        functools.partial(on_device, nr, nc),
        mesh=mesh,
        in_specs=(P("crops", "rows", None, None),)
        + (whole,) * 11
        + (P("crops", None), P("crops"), P(("crops", "rows"), None, None, None)),
        out_specs=(P(("crops", "rows"), None, None, None), P("crops", "rows", None, None))
        + (whole,) * 11,
        check_vma=False,
    )
```

```python
import functools
from types import SimpleNamespace

import jax
import jax.numpy as jnp
from jax import lax
from jax.experimental import pallas as pl
from jax.experimental.pallas import tpu as pltpu
from jax.sharding import PartitionSpec as P

MESH = pl.DeviceIdType.MESH
F32 = jnp.float32
BF16 = jnp.bfloat16
epsilon = 1e-05
COT_AT = ((0,), (1,), (2, 3), (4,), (5, 6))
OUT_AT = ((0, 1), (2,), (3, 4), (5,), (6,), ())
PAD = 32
LANES = 128

ROUND_ROWS = (4, 2, 8, 2, 2, 10, 8, 2, 2, 14, 2)
WIDE = (2, 5, 6, 9)


GROUPS = (
    (("expand_two", 512), ("spatial_two", 1152)),
    (("reduce_two", 512),),
    (("expand_one", 512), ("shortcut", 1024)),
    (("spatial_one", 1152),),
    (("slope", 128), ("slope_z", 128)),
)
GROUP_TYPES = (BF16, BF16, BF16, BF16, F32)


def group_rows(g, devices):
    group, unit = GROUPS[g], (16 if GROUP_TYPES[g] == BF16 else 8) * devices
    return -(-sum(rows for _, rows in group) // unit) * unit


def split(rows, parts):
    return [(i * rows // parts, (i + 1) * rows // parts) for i in range(parts)]


def dot(a, b):
    return lax.dot_general(a, b, (((1,), (0,)), ((), ())), preferred_element_type=F32)


def dot_nt(a, b):
    return lax.dot_general(a, b, (((1,), (1,)), ((), ())), preferred_element_type=F32)


def dot_tn(a, b):
    return lax.dot_general(a, b, (((0,), (0,)), ((), ())), preferred_element_type=F32)


def two_terms(x):
    high = x.astype(BF16)
    return high, (x - high.astype(F32)).astype(BF16)


def half_silu(h, half_mask=0.5):
    t = jnp.tanh(h)
    p = h * t
    return h + p, (half_mask + half_mask * t) * (1.0 + (h - p))


def folded(x):
    return jnp.sum(x.reshape(-1, 8, x.shape[-1]), axis=0)


def row_sum(x):
    return jnp.sum(x, axis=0, keepdims=True)


def flat2(x):
    return x.reshape(-1, x.shape[-1])


def mega(cfg, r):
    nr, nc, nk, hh, wv = cfg.nr, cfg.nc, cfg.nk, cfg.hh, cfg.wv
    ndev, nxy, own = nr * nc, nc // 2, nk // nr
    m_half = hh * PAD
    row = lax.axis_index("rows")
    col = lax.axis_index("crops")
    xy, core = lax.div(col, 2), lax.rem(col, 2)
    me = row * nc + col

    barrier = pltpu.get_barrier_semaphore()

    def place(i):
        return (lax.div(i, nc), lax.rem(i, nc))

    def greet(k, c):
        pl.semaphore_signal(
            barrier, inc=1, device_id=place(lax.rem(me + k, ndev)), device_id_type=MESH
        )
        return c

    lax.fori_loop(1, ndev, greet, 0)

    image_copies = [
        pltpu.make_async_copy(r.images.at[k], r.x_in.at[k], r.image_sem.at[k]) for k in range(nk)
    ]
    weight_copies = {
        name: pltpu.make_async_copy(r.weights[name], r.held[name], r.weight_sem.at[i])
        for i, name in enumerate(cfg.order)
    }
    for i, copy in enumerate(weight_copies.values()):
        copy.start()
        if i == 0:
            for other in image_copies:
                other.start()

    def arrived(*names):
        for name in names:
            weight_copies[name].wait()

    lane = lax.broadcasted_iota(jnp.int32, (1, LANES), 1)
    for k in range(nk):
        gate = (jnp.full((1, LANES), r.depth_gate[k], jnp.int32) > 0).astype(F32)
        r.mask_one[k] = (lane < r.widths[0, k]).astype(F32)
        r.mask_two[k] = (lane < r.widths[1, k]).astype(F32) * gate
        r.gates[k] = jnp.concatenate([gate] * 4, axis=1)
    col_mask = (lax.broadcasted_iota(jnp.int32, (PAD, 1), 0) < wv).astype(F32)
    half_mask = 0.5 * col_mask

    chips = nr * nxy
    chip = row * nxy + xy

    def chip_copy(src, dst, to, send_sem, recv_sem):
        return pltpu.make_async_remote_copy(
            src_ref=src,
            dst_ref=dst,
            send_sem=send_sem,
            recv_sem=recv_sem,
            device_id=(lax.div(to, nxy), lax.rem(to, nxy) * 2 + core),
            device_id_type=MESH,
        )

    def to_chips(copy_to):
        def send(k, c):
            copy_to(lax.rem(chip + k, chips)).start()
            return c

        lax.fori_loop(1, chips, send, 0)

    def all_of(ref, n, sem):
        pltpu.make_async_copy(ref.at[pl.ds(0, n)], ref.at[pl.ds(0, n)], sem).wait()

    def to_all(copy_to):
        def send(k, c):
            copy_to(lax.rem(me + k, ndev)).start()
            return c

        lax.fori_loop(1, ndev, send, 0)

    def sum_copy(idx, p):
        mine = r.sums[idx].at[me]
        return pltpu.make_async_remote_copy(
            src_ref=mine,
            dst_ref=mine,
            send_sem=r.sum_send.at[idx],
            recv_sem=r.sum_recv.at[idx],
            device_id=place(p),
            device_id_type=MESH,
        )

    def pair_copy(step, src, dst):
        return pltpu.make_async_remote_copy(
            src_ref=src,
            dst_ref=dst,
            send_sem=r.pair_send.at[step],
            recv_sem=r.pair_recv.at[step],
            device_id=(row, xy * 2 + 1 - core),
            device_id_type=MESH,
        )

    def lines(vectors):
        return [v[:, q * LANES : (q + 1) * LANES] for v in vectors for q in range(v.shape[1] // LANES)]

    def send_sums(idx, vectors):
        rows = lines(vectors)
        assert len(rows) == ROUND_ROWS[idx]
        slots = r.sums[idx]
        if idx in WIDE:
            half = len(rows) // 2
            both, came = r.both[idx], r.from_pair[idx]
            for at, v in enumerate(rows):
                both[at // half, at % half : at % half + 1, :] = v
            copy = pair_copy(idx, both.at[1 - core], came)
            copy.start()
            copy.wait()
            slots[chip] = both[core] + came[...]
        else:
            for at, v in enumerate(rows):
                slots[me, at : at + 1, :] = v
        if idx in WIDE:
            mine = slots.at[chip]
            to_chips(lambda to: chip_copy(mine, mine, to, r.sum_send.at[idx], r.sum_recv.at[idx]))
        else:
            to_all(lambda p: sum_copy(idx, p))

    def take_sums(idx, widths):
        slots = r.sums[idx]
        others = slots.shape[0] - 1
        all_of(slots, others, r.sum_recv.at[idx])
        if idx in WIDE:
            totals = r.totals[idx]
            totals[core] = jnp.sum(slots[...], axis=0)
            mine = totals.at[core]
            copy = pair_copy(14 + WIDE.index(idx), mine, mine)
            copy.start()
            copy.wait()
            half = ROUND_ROWS[idx] // 2
            rows = [totals[at // half, at % half : at % half + 1, :] for at in range(2 * half)]
        else:
            total = jnp.sum(slots[...], axis=0)
            rows = [total[at : at + 1, :] for at in range(ROUND_ROWS[idx])]
        all_of(slots, others, r.sum_send.at[idx])
        result, at = [], 0
        for w in widths:
            parts = rows[at : at + w // LANES]
            at += w // LANES
            result.append(jnp.concatenate(parts, axis=1) if len(parts) > 1 else parts[0])
        return result

    up_ok, down_ok = row > 0, row < nr - 1
    halo_up = (False, False, True, False, True, False, True, True, True)

    def halo(idx):
        return pltpu.make_async_remote_copy(
            src_ref=r.edge[idx],
            dst_ref=r.halo[idx],
            send_sem=r.halo_send.at[idx],
            recv_sem=r.halo_recv.at[idx],
            device_id=(row - 1 if halo_up[idx] else row + 1, col),
            device_id_type=MESH,
        )

    def halo_put(idx, at, rows):
        r.edge[idx][at] = rows.astype(BF16)

    def halo_start(idx):
        @pl.when(up_ok if halo_up[idx] else down_ok)
        def _():
            halo(idx).start()

    def halo_wait(idx):
        @pl.when(up_ok if halo_up[idx] else down_ok)
        def _():
            halo(idx).wait_send()

        @pl.when(down_ok if halo_up[idx] else up_ok)
        def _():
            halo(idx).wait_recv()

    def halo_row(idx, at, k):
        return r.halo[idx][at, k].astype(F32)

    def both_edges(idx, ref):
        halo_put(idx, 0, ref[:, hh - 1])
        halo_put(idx + 1, 0, ref[:, 0])

    def skip_send(vectors):
        for at, v in enumerate(lines(vectors)):
            r.pair_rows[at // 4, at % 4 : at % 4 + 1, :] = v
        pair_copy(12, r.pair_rows.at[1 - core], r.pair_came).start()

    def skip_spread():
        pair_copy(12, r.pair_rows.at[1 - core], r.pair_came).wait()
        r.pair_chips[chip] = r.pair_rows[core] + r.pair_came[...]
        mine = r.pair_chips.at[chip]
        to_chips(lambda to: chip_copy(mine, mine, to, r.chip_send.at[0], r.chip_recv.at[0]))

    def skip_return():
        all_of(r.pair_chips, chips - 1, r.chip_recv.at[0])
        all_of(r.pair_chips, chips - 1, r.chip_send.at[0])
        r.pair_total[core] = jnp.sum(r.pair_chips[...], axis=0)
        mine = r.pair_total.at[core]
        pair_copy(13, mine, mine).start()

    def skip_take():
        mine = r.pair_total.at[core]
        pair_copy(13, mine, mine).wait()
        return [
            jnp.concatenate([r.pair_total[i, q : q + 1, :] for q in range(4)], axis=1)
            for i in range(2)
        ]

    axes = (("core", 2), ("xy", nxy), ("rows", nr))
    seat = {"core": core, "xy": xy, "rows": row}

    def device_of(kind, i):
        if kind == "core":
            return (row, xy * 2 + i)
        if kind == "xy":
            return (row, i * 2 + core)
        return (i, col)

    def level_rows(g, level):
        size = cfg.group_size[g]
        for _, n in axes[:level]:
            size //= n
        return size

    def offset(g, level):
        at = 0
        for i, (kind, _) in enumerate(axes[:level]):
            at = at + seat[kind] * level_rows(g, i + 1)
        return pl.multiple_of(at, 8) if level else 0

    def scatter_send(g, level):
        kind, n = axes[level]
        chunk = level_rows(g, level + 1)
        for k in range(1, n):
            p = lax.rem(seat[kind] + k, n)
            pltpu.make_async_remote_copy(
                src_ref=r.part[g][level].at[pl.ds(pl.multiple_of(p * chunk, 8), chunk)],
                dst_ref=r.came[g][level].at[k - 1],
                send_sem=r.grad_send.at[g, level],
                recv_sem=r.grad_recv.at[g, level],
                device_id=device_of(kind, p),
                device_id_type=MESH,
            ).start()

    def scatter_take(g, level):
        kind, n = axes[level]
        chunk = level_rows(g, level + 1)
        came = r.came[g][level]
        pltpu.make_async_copy(came, came, r.grad_recv.at[g, level]).wait()
        mine = pl.ds(pl.multiple_of(seat[kind] * chunk, 8), chunk)
        total = r.part[g][level][mine, :].astype(F32) + jnp.sum(came[...].astype(F32), axis=0)
        pltpu.make_async_copy(came, came, r.grad_send.at[g, level]).wait()
        if level + 1 < len(axes):
            r.part[g][level + 1][...] = total.astype(GROUP_TYPES[g])
        else:
            r.full[g][pl.ds(offset(g, 3), chunk), :] = total.astype(GROUP_TYPES[g])

    def gather_send(g, level):
        kind, n = axes[level]
        size = level_rows(g, level + 1)
        region = r.full[g].at[pl.ds(offset(g, level + 1), size)]
        for k in range(1, n):
            p = lax.rem(seat[kind] + k, n)
            pltpu.make_async_remote_copy(
                src_ref=region,
                dst_ref=region,
                send_sem=r.grad_send.at[g, 3 + level],
                recv_sem=r.grad_recv.at[g, 3 + level],
                device_id=device_of(kind, p),
                device_id_type=MESH,
            ).start()

    def gather_take(g, level):
        n = axes[level][1]
        size = level_rows(g, level + 1) * (n - 1)
        bytes_of = r.full[g].at[pl.ds(0, size)]
        pltpu.make_async_copy(bytes_of, bytes_of, r.grad_recv.at[g, 3 + level]).wait()
        pltpu.make_async_copy(bytes_of, bytes_of, r.grad_send.at[g, 3 + level]).wait()

    steps = (
        (scatter_send, 0), (scatter_take, 0), (scatter_send, 1), (scatter_take, 1),
        (scatter_send, 2), (scatter_take, 2), (gather_send, 2), (gather_take, 2),
        (gather_send, 1), (gather_take, 1), (gather_send, 0), (gather_take, 0),
    )

    def advance(g, phase):
        for fn, level in steps[max(0, 2 * phase - 1) : 2 * phase + 1]:
            fn(g, level)

    def stage(g, name, value):
        at = 0
        for other, rows in GROUPS[g]:
            if other == name:
                break
            at += rows
        blocks = value.shape[1] // LANES
        for q in range(blocks):
            n = value.shape[0]
            lo = at + q * n
            r.part[g][0][lo : lo + n, :] = value[:, q * LANES : (q + 1) * LANES].astype(GROUP_TYPES[g])

    def one_send(value):
        r.one_both[...] = value.reshape(2, chips, -1, LANES)
        pair_copy(18, r.one_both.at[1 - core], r.one_came).start()

    def one_spread():
        pair_copy(18, r.one_both.at[1 - core], r.one_came).wait()
        half, slots = r.one_half, r.one_slots
        half[...] = r.one_both[core] + r.one_came[...]
        sems = (r.chip_send.at[1], r.chip_recv.at[1])
        to_chips(lambda to: chip_copy(half.at[to], slots.at[chip], to, *sems))

    def one_gather():
        slots = r.one_slots
        all_of(slots, chips - 1, r.chip_recv.at[1])
        slots[chip] = r.one_half[chip]
        r.one_whole[core, chip] = jnp.sum(slots[...], axis=0)
        mine = r.one_whole.at[core, chip]
        sems = (r.chip_send.at[2], r.chip_recv.at[2])
        to_chips(lambda to: chip_copy(mine, mine, to, *sems))

    def one_return():
        slots = r.one_slots
        all_of(slots, chips - 1, r.chip_send.at[1])
        all_of(slots, chips - 1, r.chip_recv.at[2])
        all_of(slots, chips - 1, r.chip_send.at[2])
        mine = r.one_whole.at[core]
        pair_copy(19, mine, mine).start()

    def one_take():
        mine = r.one_whole.at[core]
        pair_copy(19, mine, mine).wait()

    def coefficients(total, square, count, gain, bias):
        n = jnp.maximum(count, 1.0)
        mu = total / n
        inv = lax.rsqrt(square / n - mu * mu + epsilon)
        scale = gain * inv
        return SimpleNamespace(n=n, mu=mu, inv=inv, scale=scale, shift=bias - mu * scale)

    def factors(norm, dbias, dgain):
        c2 = -norm.scale * norm.inv * dgain / norm.n
        c3 = -norm.scale * dbias / norm.n - c2 * norm.mu
        return norm.scale, c2, c3

    def gain_sum(norm, total, z_total):
        return norm.inv * (z_total - norm.mu * total)

    def slope_sums(mask, slope, z, a, norm):
        def scaled(k, c):
            t = mask[k] * slope[k]
            r.dz4[k] = t.astype(BF16)
            r.slope_z[k] = (t * ((z[k] - norm.mu) * norm.inv)).astype(BF16)
            return c

        loop(scaled)
        flat_a = flat2(a[...])
        stage(4, "slope", dot_tn(flat_a, flat2(r.dz4[...])))
        stage(4, "slope_z", dot_tn(flat_a, flat2(r.slope_z[...])))

    def through(weight, c2, c3):
        high, low = two_terms(weight.astype(F32) * c2)
        b = dot_nt(high, weight) + dot_nt(low, weight)
        v = sum(dot_nt(jnp.broadcast_to(c, (16, c.shape[1])), weight) for c in two_terms(c3))
        return b, v[0:1]

    def chained(norm, u_sum, uz_sum, t_sum, tz_sum, b, v):
        k1, k2 = r.full[4][0:LANES, :], r.full[4][LANES : 2 * LANES, :]
        dbias = u_sum + row_sum(k1 * b) + t_sum * v
        dgain = gain_sum(norm, u_sum, uz_sum) + row_sum(k2 * b) + gain_sum(norm, t_sum, tz_sum) * v
        return dbias, dgain

    def loop(body, init=0):
        for k in range(nk):
            init = body(k, init)
        return init

    def zero8(width, count):
        return tuple(jnp.zeros((8, width), F32) for _ in range(count))

    def row_pieces(src_of, dst_of, send, recv, local):
        pieces = []
        for w, (lo, hi) in enumerate(cfg.pieces):
            for k in range(1, nr):
                p = lax.rem(row + k, nr)
                pieces.append(
                    pltpu.make_async_remote_copy(
                        src_ref=src_of(p, lo, hi - lo),
                        dst_ref=dst_of(lo, hi - lo),
                        send_sem=send,
                        recv_sem=recv,
                        device_id=(p, col),
                        device_id_type=MESH,
                    )
                )
        here = pltpu.make_async_copy(src_of(row, 0, hh), dst_of(0, hh), local)
        return pieces, here

    def wait_pieces(which):
        bytes_of = r.out_rows.at[pl.ds(0, nk - own)]
        pltpu.make_async_copy(bytes_of, bytes_of, r.row_recv.at[which]).wait()
        pltpu.make_async_copy(bytes_of, bytes_of, r.row_send.at[which]).wait()

    def start_pieces(pieces, *which):
        for w in which:
            for copy in pieces[w * (nr - 1) : (w + 1) * (nr - 1)]:
                copy.start()

    cot_copies, cot_local = row_pieces(
        lambda p, lo, n: r.cot.at[:, pl.ds(p * hh + lo, n)],
        lambda lo, n: r.cot_rows.at[pl.ds(row * own, own), pl.ds(lo, n)],
        r.row_send.at[0], r.row_recv.at[0], r.local_sem.at[0],
    )
    out_copies, out_local = row_pieces(
        lambda p, lo, n: r.out_rows.at[pl.ds(p * own, own), pl.ds(lo, n)],
        lambda lo, n: r.out.at[:, pl.ds(row * hh + lo, n)],
        r.row_send.at[1], r.row_recv.at[1], r.local_sem.at[1],
    )
    cot_local.start()

    lane_blocks = cfg.c_in // LANES
    for slot in range(2 * hh):
        for q in range(lane_blocks):
            r.spread[q, slot, 2 * wv : 2 * PAD, :] = jnp.zeros((2 * PAD - 2 * wv, LANES), F32)
    arrived("reduce_one")
    w1 = r.reduce_one[...]
    acc = zero8(LANES, 2)
    for copy in image_copies:
        copy.wait()

    def first(k, acc):
        for i in range(2 * hh):
            for q in range(lane_blocks):
                lanes = slice(q * LANES, (q + 1) * LANES)
                r.spread[q, i, 0 : 2 * wv, :] = r.x_in[k, i, :, lanes].astype(F32)
        m = r.mask_one[k]
        s1, s2 = acc
        for pr in range(2):
            for pc in range(2):
                for i in range(hh):
                    for q in range(lane_blocks):
                        lanes = slice(q * LANES, (q + 1) * LANES)
                        r.x[pr, pc, k, i, :, lanes] = r.spread[
                            q, 2 * i + pr, pl.ds(pc, PAD, stride=2), :
                        ].astype(BF16)
                z = dot(flat2(r.x[pr, pc, k]), w1)
                r.z1[pr, pc, k] = z.reshape(hh, PAD, LANES)
                s1 += m * folded(z)
                s2 += m * folded(z * z)
        return s1, s2

    s1, s2 = loop(first, acc)
    count_one = sum(r.mask_one[k] for k in range(nk))
    count_two = sum(r.mask_two[k] for k in range(nk))
    arrived("shortcut")
    sc = r.shortcut[...]

    def skip(k, acc):
        z = dot(flat2(r.x[0, 0, k]), sc)
        r.zs[k] = z.reshape(hh, PAD, cfg.c_out)
        return acc[0] + folded(z), acc[1] + folded(z * z)

    zs1, zs2 = loop(skip, zero8(cfg.c_out, 2))
    for pc in range(2):
        halo_put(0, pc, r.z1[1, pc, :, hh - 1])
    pl.semaphore_wait(barrier, ndev - 1)
    send_sums(0, [row_sum(s1), row_sum(s2), count_one, count_two])
    halo_start(0)
    skip_send([row_sum(zs1), row_sum(zs2)])
    start_pieces(cot_copies, *COT_AT[0])
    arrived("mid_gain", "mid_bias", "spatial_one")
    t1, t2, active_one, active_two = take_sums(0, [LANES] * 4)
    half_px, full_px = float(hh * wv), float(4 * hh * wv)
    active_gate = active_two[:, 0:1]
    g1, b1 = r.mid_gain[0:1, :], r.mid_bias[0:1, :]
    n1 = coefficients(t1, t2, active_one * full_px, g1, b1)
    halo_wait(0)

    def shifted_right(a):
        return pltpu.roll(a, 1, axis=a.ndim - 2)

    def shifted_left(a):
        return pltpu.roll(a, PAD - 1, axis=a.ndim - 2)

    def affine(norm, m):
        return 0.5 * m * norm.scale, (0.5 * m * norm.shift) * col_mask

    k_one = [r.spatial_one[i] for i in range(3)]

    def second(k, acc):
        m = r.mask_one[k]
        ah, bh = affine(n1, m)
        for pr in range(2):
            for pc in range(2):
                a, s = half_silu(r.z1[pr, pc, k] * ah + bh, half_mask)
                r.s1[pr, pc, k] = s
                dst = r.even if pr == 0 else r.odd
                rows = pl.ds(0, hh) if pr == 0 else pl.ds(1, hh)
                if pc == 0:
                    dst[k, rows, :, LANES : 2 * LANES] = a.astype(BF16)
                else:
                    dst[k, rows, :, 2 * LANES : 3 * LANES] = a.astype(BF16)
                    dst[k, rows, :, 0:LANES] = shifted_right(a).astype(BF16)
        for pc in range(2):
            a, _ = half_silu(halo_row(0, pc, k) * ah + bh)
            a = jnp.where(row > 0, a, 0.0)
            if pc == 0:
                r.odd[k, 0, :, LANES : 2 * LANES] = a.astype(BF16)
            else:
                r.odd[k, 0, :, 2 * LANES : 3 * LANES] = a.astype(BF16)
                r.odd[k, 0, :, 0:LANES] = shifted_right(a).astype(BF16)
        z = dot(flat2(r.even[k]), k_one[1])
        z += dot(flat2(r.odd[k, 1 : hh + 1]), k_one[2])
        z += dot(flat2(r.odd[k, 0:hh]), k_one[0])
        z = z.reshape(hh, PAD, LANES) * col_mask
        r.z2[k] = z
        return acc[0] + m * folded(z), acc[1] + m * folded(z * z)

    s1, s2 = loop(second, zero8(LANES, 2))
    send_sums(1, [row_sum(s1), row_sum(s2)])
    skip_spread()

    def early(k, c):
        m = r.mask_one[k]
        for pr in range(2):
            for pc in range(2):
                zhat = (r.z1[pr, pc, k] - n1.mu) * (m * n1.inv)
                r.dz1[pr, pc, k] = zhat.astype(BF16)
        r.dz4[k] = jnp.broadcast_to(m, (hh, PAD, LANES)).astype(BF16)
        return c

    loop(early)
    for name in ("expand_one", "wide_gain", "wide_bias", "reduce_two"):
        arrived(name)
    planes = [(pr, pc) for pr in range(2) for pc in range(2)]
    r.part_z[...] = sum(dot_tn(flat2(r.x[q]), flat2(r.dz1[q])) for q in planes)
    r.part_m[...] = sum(dot_tn(flat2(r.x[q]), flat2(r.dz4[...])) for q in planes)
    start_pieces(cot_copies, *COT_AT[1])
    t1, t2 = take_sums(1, [LANES] * 2)
    n2 = coefficients(t1, t2, active_one * half_px, r.mid_gain[1:2, :], r.mid_bias[1:2, :])
    e1 = r.expand_one[...]

    def third(k, acc):
        ah, bh = affine(n2, r.mask_one[k])
        a, s = half_silu(r.z2[k] * ah + bh, half_mask)
        r.s2[k] = s
        a = a.astype(BF16)
        r.a2[k] = a
        z = dot(flat2(a), e1)
        r.z3[k] = z.reshape(hh, PAD, cfg.c_out)
        t = r.mask_one[k] * s
        return (
            acc[0] + folded(z), acc[1] + folded(z * z), acc[2] + folded(t), acc[3] + folded(t * r.z2[k])
        )

    s1, s2, t2_sum, t2z_sum = loop(third, zero8(cfg.c_out, 2) + zero8(LANES, 2))
    send_sums(2, [row_sum(s1), row_sum(s2)])
    slope_sums(r.mask_one, r.s2, r.z2, r.a2, n2)
    advance(4, 0)
    arrived("spatial_two", "expand_two")
    def tap(ref, i, j):
        return ref[i, j * LANES : (j + 1) * LANES, :].T

    for i in range(3):
        for j in range(3):
            r.back_two[i, j * LANES : (j + 1) * LANES, :] = tap(r.spatial_two, 2 - i, 2 - j)
    zeros = jnp.zeros((LANES, LANES), BF16)
    k1 = r.spatial_one
    here = [[tap(k1, 2, 2), tap(k1, 1, 2), tap(k1, 2, 1), tap(k1, 1, 1)],
            [tap(k1, 2, 0), tap(k1, 1, 0), zeros, zeros]]
    below = [[tap(k1, 0, 2), tap(k1, 0, 1)], [tap(k1, 0, 0), zeros]]
    for ref, blocks in ((r.back_here, here), (r.back_below, below)):
        for i, line in enumerate(blocks):
            for j, block in enumerate(line):
                ref[i * LANES : (i + 1) * LANES, j * LANES : (j + 1) * LANES] = block
    skip_return()
    start_pieces(cot_copies, *COT_AT[2])
    t1, t2 = take_sums(2, [cfg.c_out] * 2)
    ts1, ts2 = skip_take()
    all_px = float(nk * nc) * float(nr) * half_px
    n3 = coefficients(t1, t2, all_px, r.wide_gain[0:1, :], r.wide_bias[0:1, :])
    ns = coefficients(ts1, ts2, all_px, r.wide_gain[1:2, :], r.wide_bias[1:2, :])
    w2 = r.reduce_two[...]

    def fourth(k, acc):
        a3, as_ = 0.5 * n3.scale, 0.5 * ns.scale
        b3 = (0.5 * (n3.shift + ns.shift)) * col_mask
        for i in range(hh):
            a, s = half_silu(r.z3[k, i] * a3 + r.zs[k, i] * as_ + b3, half_mask)
            r.hidden[k, i] = a.astype(BF16)
            r.s3[k, i] = s
        z = dot(flat2(r.hidden[k]), w2)
        r.z4[k] = z.reshape(hh, PAD, LANES)
        m = r.mask_two[k]
        return acc[0] + m * folded(z), acc[1] + m * folded(z * z)

    s1, s2 = loop(fourth, zero8(LANES, 2))
    send_sums(3, [row_sum(s1), row_sum(s2)])
    both_edges(1, r.z4)
    halo_start(1)
    halo_start(2)

    def hats(k, c):
        for i in range(hh):
            r.dz3[k, i] = ((r.z3[k, i] - n3.mu) * n3.inv).astype(BF16)
            r.dzs[k, i] = ((r.zs[k, i] - ns.mu) * ns.inv).astype(BF16)
        return c

    advance(4, 1)
    loop(hats)
    ones = jnp.ones((nk * m_half, LANES), BF16)
    r.expand_z[...] = dot_tn(flat2(r.a2[...]), flat2(r.dz3[...]))
    r.expand_m[...] = dot_tn(flat2(r.a2[...]), ones)
    r.skip_z[...] = dot_tn(flat2(r.x[0, 0]), flat2(r.dzs[...]))
    r.skip_m[...] = dot_tn(flat2(r.x[0, 0]), ones)
    start_pieces(cot_copies, *COT_AT[3])
    t1, t2 = take_sums(3, [LANES] * 2)
    n4 = coefficients(t1, t2, active_two * half_px, r.mid_gain[2:3, :], r.mid_bias[2:3, :])
    halo_wait(1)
    halo_wait(2)

    def put3(dst, k, rows, a):
        dst[k, rows, :, LANES : 2 * LANES] = a.astype(BF16)
        dst[k, rows, :, 0:LANES] = shifted_right(a).astype(BF16)
        dst[k, rows, :, 2 * LANES : 3 * LANES] = shifted_left(a).astype(BF16)

    k_two = [r.spatial_two[i] for i in range(3)]

    def fifth(k, acc):
        m = r.mask_two[k]
        ah, bh = affine(n4, m)
        a, s = half_silu(r.z4[k] * ah + bh, half_mask)
        r.s4[k] = s
        put3(r.a4, k, pl.ds(1, hh), a)
        a, _ = half_silu(halo_row(1, 0, k) * ah + bh)
        put3(r.a4, k, 0, jnp.where(row > 0, a, 0.0))
        a, _ = half_silu(halo_row(2, 0, k) * ah + bh)
        put3(r.a4, k, hh + 1, jnp.where(row < nr - 1, a, 0.0))
        z = sum(dot(flat2(r.a4[k, i : i + hh]), k_two[i]) for i in range(3))
        z = z.reshape(hh, PAD, LANES) * col_mask
        r.z5[k] = z
        return acc[0] + m * folded(z), acc[1] + m * folded(z * z)

    s1, s2 = loop(fifth, zero8(LANES, 2))
    send_sums(4, [row_sum(s1), row_sum(s2)])
    advance(4, 2)
    start_pieces(cot_copies, *COT_AT[4])
    t1, t2 = take_sums(4, [LANES] * 2)
    n5 = coefficients(t1, t2, active_two * half_px, r.mid_gain[3:4, :], r.mid_bias[3:4, :])
    e2 = r.expand_two[...]

    def sixth(k, acc):
        ah, bh = affine(n5, r.mask_two[k])
        a, s = half_silu(r.z5[k] * ah + bh, half_mask)
        r.s5[k] = s
        a = a.astype(BF16)
        r.a5[k] = a
        z = dot(flat2(a), e2)
        r.z6[k] = z.reshape(hh, PAD, cfg.c_out)
        g = r.gates[k]
        return acc[0] + g * folded(z), acc[1] + g * folded(z * z)

    s1, s2 = loop(sixth, zero8(cfg.c_out, 2))
    send_sums(5, [row_sum(v) for v in (s1, s2, t2_sum, t2z_sum)])
    both_edges(3, r.z5)
    halo_start(3)
    halo_start(4)
    advance(4, 3)
    wait_pieces(0)
    cot_local.wait()
    t1, t2, t2_sum, t2z_sum = take_sums(5, [cfg.c_out] * 2 + [LANES] * 2)
    gate_count = active_gate * half_px
    n6 = coefficients(t1, t2, gate_count, r.wide_gain[2:3, :], r.wide_bias[2:3, :])
    pad_rows = jnp.zeros((PAD - wv, cfg.c_out), F32)

    def cot_row(k, i):
        return jnp.concatenate([r.cot_rows[k, i].astype(F32), pad_rows], axis=0)

    def seventh(k, acc):
        g = r.gates[k]
        a6, b6 = (0.5 * g) * n6.scale, ((0.5 * g) * n6.shift) * col_mask
        d1, d2 = acc
        for i in range(hh):
            hid = r.hidden[k, i].astype(F32)
            z = r.z6[k, i]
            a, s = half_silu(0.5 * hid + (z * a6 + b6))
            r.out_rows[k, i] = jnp.where(g > 0.0, a, hid)[:wv].astype(BF16)
            live = g * cot_row(k, i) * s
            r.live[k, i] = live
            d1 += folded(live)
            d2 += folded(live * z)
        return d1, d2

    sums = loop(seventh, zero8(cfg.c_out, 2))
    send_sums(6, [row_sum(v) for v in sums])

    advance(4, 4)
    start_pieces(out_copies, *OUT_AT[0])
    out_local.start()
    db6, q6 = take_sums(6, [cfg.c_out] * 2)
    dg6 = gain_sum(n6, db6, q6)
    c1, c2, c3 = factors(n6, db6, dg6)

    def eighth(k, acc, c1=c1, c2=c2, c3=c3):
        g = r.gates[k]
        f1, f2, f3 = g * c1, g * c2, (g * c3) * col_mask
        for i in range(hh):
            r.dz6[k, i] = (r.live[k, i] * f1 + r.z6[k, i] * f2 + f3).astype(BF16)
        q = dot_nt(flat2(r.dz6[k]), e2).reshape(hh, PAD, LANES) * r.s5[k]
        r.q5[k] = q
        m = r.mask_two[k]
        return acc[0] + m * folded(q), acc[1] + m * folded(q * r.z5[k])

    d1, d2 = loop(eighth, zero8(LANES, 2))
    send_sums(7, [row_sum(d1), row_sum(d2)])
    both_edges(5, r.q5)
    halo_start(5)
    halo_start(6)
    stage(0, "expand_two", dot_tn(flat2(r.a5[...]), flat2(r.dz6[...])))
    halo_wait(3)
    halo_wait(4)
    advance(4, 5)
    start_pieces(out_copies, *OUT_AT[1])
    db5, q5 = take_sums(7, [LANES] * 2)
    dg5 = gain_sum(n5, db5, q5)
    c1, c2, c3 = factors(n5, db5, dg5)
    halo_wait(5)
    halo_wait(6)

    def ninth(k, acc, c1=c1, c2=c2, c3=c3):
        m = r.mask_two[k]
        f1, f2, f3 = m * c1, m * c2, (m * c3) * col_mask
        put3(r.dz5, k, pl.ds(1, hh), r.q5[k] * f1 + r.z5[k] * f2 + f3)
        d = halo_row(5, 0, k) * f1 + halo_row(3, 0, k) * f2 + f3
        put3(r.dz5, k, 0, jnp.where(row > 0, d, 0.0))
        d = halo_row(6, 0, k) * f1 + halo_row(4, 0, k) * f2 + f3
        put3(r.dz5, k, hh + 1, jnp.where(row < nr - 1, d, 0.0))
        q = sum(dot(flat2(r.dz5[k, i : i + hh]), r.back_two[i]) for i in range(3))
        q = q.reshape(hh, PAD, LANES) * r.s4[k]
        r.q4[k] = q
        return acc[0] + m * folded(q), acc[1] + m * folded(q * r.z4[k])

    d1, d2 = loop(ninth, zero8(LANES, 2))
    send_sums(8, [row_sum(d1), row_sum(d2)])
    halo_put(8, 0, r.z2[:, 0])
    halo_start(8)

    d5 = flat2(r.dz5[:, 1 : hh + 1, :, LANES : 2 * LANES])
    stage(
        0,
        "spatial_two",
        jnp.concatenate([dot_tn(flat2(r.a4[:, i : i + hh]), d5) for i in range(3)], axis=0),
    )
    advance(4, 6)
    advance(0, 0)
    start_pieces(out_copies, *OUT_AT[2])
    db4, q4 = take_sums(8, [LANES] * 2)
    advance(0, 1)
    dg4 = gain_sum(n4, db4, q4)
    c1, c2, c3 = factors(n4, db4, dg4)

    def tenth(k, acc, c1=c1, c2=c2, c3=c3):
        m, g = r.mask_two[k], r.gates[k]
        f1, f2, f3 = m * c1, m * c2, (m * c3) * col_mask
        r.dz4[k] = (r.q4[k] * f1 + r.z4[k] * f2 + f3).astype(BF16)
        back = dot_nt(flat2(r.dz4[k]), w2).reshape(hh, PAD, cfg.c_out)
        e1_, e2_, e3_, u1, u2 = acc
        for i in range(hh):
            d = back[i] + (1.0 - g) * cot_row(k, i) + r.live[k, i]
            q = d.astype(BF16).astype(F32) * r.s3[k, i]
            r.q3[k, i] = q
            r.dz3[k, i] = (q * n3.scale).astype(BF16)
            e1_ += folded(q)
            e2_ += folded(q * r.z3[k, i])
            e3_ += folded(q * r.zs[k, i])
        u = dot_nt(flat2(r.dz3[k]), e1).reshape(hh, PAD, LANES)
        r.q2[k] = u
        ut = (r.mask_one[k] * u) * r.s2[k]
        return e1_, e2_, e3_, u1 + folded(ut), u2 + folded(ut * r.z2[k])

    sums = loop(tenth, zero8(cfg.c_out, 3) + zero8(LANES, 2))
    send_sums(9, [row_sum(v) for v in sums])
    halo_put(7, 0, r.q2[:, 0])
    halo_start(7)
    stage(1, "reduce_two", dot_tn(flat2(r.hidden[...]), flat2(r.dz4[...])))
    advance(1, 0)
    expand_q = dot_tn(flat2(r.a2[...]), flat2(r.dz3[...]))
    skip_q = dot_tn(flat2(r.x[0, 0]), flat2(r.dz3[...]))
    halo_wait(8)

    def edge_slope(k, c):
        ah, bh = affine(n2, r.mask_one[k])
        a, t = half_silu(halo_row(8, 0, k) * ah + bh, half_mask)
        r.edge_a[k] = a.astype(BF16)
        r.edge_t[k] = t
        return c

    loop(edge_slope)
    advance(1, 1)
    advance(0, 2)
    start_pieces(out_copies, *OUT_AT[3])
    db3, q3, qs, u_sum, uz_sum = take_sums(9, [cfg.c_out] * 3 + [LANES] * 2)
    dg3, dgs = gain_sum(n3, db3, q3), gain_sum(ns, db3, qs)
    f3_, fs_ = factors(n3, db3, dg3), factors(ns, db3, dgs)
    b, v2 = through(e1, *f3_[1:])
    db2, dg2 = chained(n2, u_sum, uz_sum, t2_sum, t2z_sum, b, v2)
    c1, c2, c3 = factors(n2, db2, dg2)
    b2 = two_terms(b)

    def four(x):
        return jnp.concatenate([x] * (cfg.c_out // LANES), axis=1)

    def by_parts(q_part, z_part, m_part, norm, fs):
        total = q_part + (fs[1] / norm.inv) * z_part[...]
        return total + (fs[2] + fs[1] * norm.mu) * four(m_part[...])

    stage(2, "expand_one", by_parts(expand_q, r.expand_z, r.expand_m, n3, f3_))
    stage(2, "shortcut", by_parts(skip_q * (ns.scale / n3.scale), r.skip_z, r.skip_m, ns, fs_))
    advance(2, 0)
    halo_wait(7)
    edge_ab = sum(dot(flat2(r.edge_a[...]), t) for t in b2).reshape(nk, PAD, LANES)

    def twelfth(k, c, c1=c1, c2=c2, c3=c3):
        m = r.mask_one[k]
        f1, f2, f3 = m * c1, m * c2, (m * c3) * col_mask
        ab = sum(dot(flat2(r.a2[k]), t) for t in b2).reshape(hh, PAD, LANES)
        q = (r.q2[k] + ab + v2) * r.s2[k]
        d = q * f1 + r.z2[k] * f2 + f3
        r.dz2[k, 0:hh, :, 0:LANES] = d.astype(BF16)
        r.dz2[k, 0:hh, :, LANES : 2 * LANES] = shifted_left(d).astype(BF16)
        q = (halo_row(7, 0, k) + edge_ab[k] + v2) * r.edge_t[k]
        d = jnp.where(row < nr - 1, q * f1 + halo_row(8, 0, k) * f2 + f3, 0.0)
        r.dz2[k, hh, :, 0:LANES] = d.astype(BF16)
        r.dz2[k, hh, :, LANES : 2 * LANES] = shifted_left(d).astype(BF16)
        return c

    loop(twelfth)
    d2_ = flat2(r.dz2[:, 0:hh, :, 0:LANES])
    inputs = [r.odd[:, 0:hh], r.even[...], r.odd[:, 1 : hh + 1]]
    stage(3, "spatial_one", jnp.concatenate([dot_tn(flat2(a), d2_) for a in inputs], axis=0))


    advance(3, 0)
    advance(2, 1)

    def thirteenth(k, acc):
        m = r.mask_one[k]
        u = dot(flat2(r.dz2[k, 0:hh]), r.back_here[...])
        v = dot(flat2(r.dz2[k, 1 : hh + 1]), r.back_below[...])
        s1, s2 = acc
        parts = (
            (1, 1, u[:, 0:LANES] + v[:, 0:LANES]),
            (0, 1, u[:, LANES : 2 * LANES]),
            (1, 0, u[:, 2 * LANES : 3 * LANES] + v[:, LANES : 2 * LANES]),
            (0, 0, u[:, 3 * LANES : 4 * LANES]),
        )
        for pr, pc, q in parts:
            q = q.reshape(hh, PAD, LANES) * r.s1[pr, pc, k]
            r.q1[pr, pc, k] = q
            r.dz1[pr, pc, k] = (m * q).astype(BF16)
            s1 += m * folded(q)
            s2 += m * folded(q * r.z1[pr, pc, k])
        return s1, s2

    d1, d2 = loop(thirteenth, zero8(LANES, 2))
    send_sums(10, [row_sum(d1), row_sum(d2)])
    advance(3, 1)
    advance(0, 3)
    advance(1, 2)
    part_q = sum(dot_tn(flat2(r.x[q]), flat2(r.dz1[q])) for q in planes)

    def skip_back(k, c):
        h3 = fs_[2] * col_mask
        for i in range(hh):
            r.dzs[k, i] = (r.q3[k, i] * fs_[0] + r.zs[k, i] * fs_[1] + h3).astype(BF16)
        r.skip_back[k] = dot_nt(flat2(r.dzs[k]), sc).reshape(hh, PAD, cfg.c_in)
        return c

    loop(skip_back)
    start_pieces(out_copies, *OUT_AT[4])
    advance(2, 2)
    db1, q1 = take_sums(10, [LANES] * 2)
    dg1 = gain_sum(n1, db1, q1)
    c1, c2, c3 = factors(n1, db1, dg1)

    total = n1.scale * part_q
    total += (c2 / n1.inv) * r.part_z[...] + (c3 + c2 * n1.mu) * r.part_m[...]
    one_send(total)
    one_spread()
    advance(3, 2)
    advance(0, 4)
    advance(1, 3)
    start_pieces(out_copies, *OUT_AT[5])

    def last(k, acc, c1=c1, c2=c2, c3=c3):
        m = r.mask_one[k]
        f1, f2, f3 = m * c1, m * c2, (m * c3) * col_mask
        for pr in range(2):
            for pc in range(2):
                d = (r.q1[pr, pc, k] * f1 + r.z1[pr, pc, k] * f2 + f3).astype(BF16)
                r.dz1[pr, pc, k] = d
        return acc

    loop(last)

    def images_back(k, c):
        for pr in range(2):
            for pc in range(2):
                g = dot_nt(flat2(r.dz1[pr, pc, k]), w1).reshape(hh, PAD, cfg.c_in)
                if pr == 0 and pc == 0:
                    g += r.skip_back[k]
                for i in range(hh):
                    for q in range(lane_blocks):
                        r.spread[q, 2 * i + pr, pl.ds(pc, PAD, stride=2), :] = g[
                            i, :, q * LANES : (q + 1) * LANES
                        ]
        for i in range(2 * hh):
            for q in range(lane_blocks):
                lanes = slice(q * LANES, (q + 1) * LANES)
                r.x_in[k, i, :, lanes] = r.spread[q, i, 0 : 2 * wv, :].astype(BF16)
        return c

    loop(images_back)
    back_copy = pltpu.make_async_copy(r.x_in, r.images_grad, r.local_sem.at[2])
    back_copy.start()

    for k, v in enumerate((dg1, dg2, dg4, dg5, db1, db2, db4, db5)):
        r.mid_held[k : k + 1, :] = v
    for k, v in enumerate((dg3, dgs, dg6, db3, db3, db6)):
        r.wide_held[k : k + 1, :] = v
    results = []

    def give(src, dst):
        copy = pltpu.make_async_copy(src, dst, r.full_sem.at[len(results)])
        copy.start()
        results.append(copy)

    give(r.mid_held, r.mid_grads)
    give(r.wide_held, r.wide_grads)

    def result(g):
        give(r.full[g], r.summed[g])

    advance(2, 3)
    advance(3, 3)
    one_gather()
    advance(0, 5)
    advance(1, 4)
    advance(2, 4)
    advance(3, 4)
    one_return()
    advance(0, 6)
    result(0)
    advance(1, 5)
    advance(2, 5)
    advance(3, 5)
    one_take()
    give(r.one_whole, r.summed_one)
    advance(1, 6)
    result(1)
    advance(2, 6)
    result(2)
    advance(3, 6)
    result(3)
    wait_pieces(1)
    out_local.wait()
    back_copy.wait()
    for copy in results:
        copy.wait()


def on_device(nr, nc, *args):
    (images, reduce_one, spatial_one, expand_one, shortcut, reduce_two, spatial_two, expand_two,
     mid_gain, mid_bias, wide_gain, wide_bias, widths, depth_gate, cot) = args
    nk, full_rows, full_cols, c_in = images.shape
    hh, wv, c_out = full_rows // 2, full_cols // 2, expand_one.shape[1]
    own = cot.shape[0]
    ndev, nxy, groups = nr * nc, nc // 2, len(GROUPS)
    sizes = [group_rows(g, ndev) for g in range(groups)]
    chunk = (ndev // 2, c_in // ndev, LANES)
    half, quad = (nk, hh, PAD), (2, 2, nk, hh, PAD)

    def f32(*shape):
        return pltpu.VMEM(shape, F32)

    def bf16(*shape):
        return pltpu.VMEM(shape, BF16)

    def dma(*shape):
        return pltpu.SemaphoreType.DMA(shape)

    def mid():
        return f32(*half, LANES)

    def wide():
        return f32(*half, c_out)

    def low(width):
        return bf16(*half, width)

    weights = dict(
        reduce_one=reduce_one, shortcut=shortcut, mid_gain=mid_gain, mid_bias=mid_bias,
        spatial_one=spatial_one.reshape(3, 3 * LANES, LANES), expand_one=expand_one,
        wide_gain=wide_gain, wide_bias=wide_bias, reduce_two=reduce_two,
        spatial_two=spatial_two.reshape(3, 3 * LANES, LANES), expand_two=expand_two,
    )
    scalars = dict(widths=widths.T, depth_gate=depth_gate)
    ins = dict(images=images, cot=cot, weights=weights)
    outs = dict(
        out=jax.ShapeDtypeStruct(cot.shape, BF16),
        images_grad=jax.ShapeDtypeStruct(images.shape, BF16),
        summed=[jax.ShapeDtypeStruct((size, LANES), BF16) for size in sizes[:4]],
        summed_one=jax.ShapeDtypeStruct((2,) + chunk, F32),
        mid_grads=jax.ShapeDtypeStruct((8, LANES), F32),
        wide_grads=jax.ShapeDtypeStruct((6, c_out), F32),
    )
    edges = [bf16(2 if i == 0 else 1, nk, PAD, LANES) for i in range(9)]
    levels = [(n, n // 2, n // nc, n // ndev) for n in sizes]
    halves = {i: ROUND_ROWS[i] // 2 for i in WIDE}
    scratch = dict(
        held={name: pltpu.VMEM(a.shape, a.dtype) for name, a in weights.items()},
        x_in=bf16(*images.shape), spread=f32(c_in // LANES, 2 * hh, 2 * PAD, LANES), x=bf16(*quad, c_in),
        z1=f32(*quad, LANES), s1=f32(*quad, LANES), q1=f32(*quad, LANES), dz1=bf16(*quad, LANES),
        part_z=f32(c_in, LANES), part_m=f32(c_in, LANES),
        one_both=f32(2, *chunk), one_came=f32(*chunk), one_half=f32(*chunk), one_slots=f32(*chunk),
        one_whole=f32(2, *chunk), slope_z=low(LANES),
        edge_a=bf16(nk, PAD, LANES), edge_t=f32(nk, PAD, LANES),
        expand_z=f32(LANES, c_out), expand_m=f32(LANES, LANES), skip_z=f32(c_in, c_out),
        skip_m=f32(c_in, LANES), mid_held=f32(8, LANES), wide_held=f32(6, c_out),
        pair_rows=f32(2, 4, LANES), pair_came=f32(4, LANES), pair_chips=f32(ndev // 2, 4, LANES),
        pair_total=f32(2, 4, LANES),
        even=low(3 * LANES), odd=bf16(nk, hh + 1, PAD, 3 * LANES), dz2=bf16(nk, hh + 1, PAD, 2 * LANES),
        a4=bf16(nk, hh + 2, PAD, 3 * LANES), dz5=bf16(nk, hh + 2, PAD, 3 * LANES),
        cot_rows=bf16(nk, hh, wv, c_out), out_rows=bf16(nk, hh, wv, c_out), skip_back=f32(*half, c_in),
        back_two=bf16(3, 3 * LANES, LANES), back_here=bf16(2 * LANES, 4 * LANES),
        back_below=bf16(2 * LANES, 2 * LANES),
        mask_one=f32(nk, 1, LANES), mask_two=f32(nk, 1, LANES), gates=f32(nk, 1, c_out),
        z2=mid(), s2=mid(), q2=mid(), z4=mid(), s4=mid(), q4=mid(), z5=mid(), s5=mid(), q5=mid(),
        z3=wide(), zs=wide(), s3=wide(), q3=wide(), z6=wide(), live=wide(),
        a2=low(LANES), a5=low(LANES), dz4=low(LANES),
        hidden=low(c_out), dz6=low(c_out), dz3=low(c_out), dzs=low(c_out),
        edge=edges, halo=edges,
        sums=[
            f32(ndev // 2 if i in WIDE else ndev, halves.get(i, n), LANES)
            for i, n in enumerate(ROUND_ROWS)
        ],
        both={i: f32(2, n, LANES) for i, n in halves.items()},
        totals={i: f32(2, n, LANES) for i, n in halves.items()},
        from_pair={i: f32(n, LANES) for i, n in halves.items()},
        part=[[pltpu.VMEM((n[i], LANES), t) for i in range(3)] for n, t in zip(levels, GROUP_TYPES)],
        came=[
            [pltpu.VMEM((m - 1, n[i + 1], LANES), t) for i, m in enumerate((2, nxy, nr))]
            for n, t in zip(levels, GROUP_TYPES)
        ],
        full=[pltpu.VMEM((n, LANES), t) for n, t in zip(sizes, GROUP_TYPES)],
        image_sem=dma(nk), local_sem=dma(3), full_sem=dma(groups + 3), weight_sem=dma(len(weights)),
        sum_send=dma(len(ROUND_ROWS)), sum_recv=dma(len(ROUND_ROWS)), halo_send=dma(9), halo_recv=dma(9),
        row_send=dma(2), row_recv=dma(2), pair_send=dma(20), pair_recv=dma(20), chip_send=dma(3),
        chip_recv=dma(3), grad_send=dma(groups, 6), grad_recv=dma(groups, 6),
    )
    cfg = SimpleNamespace(
        nr=nr, nc=nc, nk=nk, hh=hh, wv=wv, c_in=c_in, c_out=c_out, group_size=sizes,
        pieces=split(hh, 7), order=list(weights),
    )
    flat, trees = [], []
    for part in (scalars, ins, outs, scratch):
        leaves, tree = jax.tree.flatten(part)
        flat.append(leaves)
        trees.append(tree)

    def body(*refs):
        named, at = {}, 0
        for leaves, tree in zip(flat, trees):
            named.update(jax.tree.unflatten(tree, refs[at : at + len(leaves)]))
            at += len(leaves)
        mega(cfg, SimpleNamespace(**named, **named["held"]))

    smem, hbm = pl.BlockSpec(memory_space=pltpu.SMEM), pl.BlockSpec(memory_space=pl.ANY)
    result = pl.pallas_call(
        body,
        out_shape=flat[2],
        in_specs=[smem] * len(flat[0]) + [hbm] * len(flat[1]),
        out_specs=[hbm] * len(flat[2]),
        scratch_shapes=flat[3],
        compiler_params=pltpu.CompilerParams(
            collective_id=0, has_side_effects=True, vmem_limit_bytes=60 << 20
        ),
    )(*flat[0], *flat[1])
    made = SimpleNamespace(**jax.tree.unflatten(trees[2], result))
    parts = [made.out, made.images_grad, *made.summed, made.summed_one, made.mid_grads, made.wide_grads]
    return finished(parts, mid_gain.shape, wide_gain.shape)


WEIGHTS = (
    ("reduce_one", (256, 128)),
    ("spatial_one", (3, 3, 128, 128)),
    ("expand_one", (128, 512)),
    ("shortcut", (256, 512)),
    ("reduce_two", (512, 128)),
    ("spatial_two", (3, 3, 128, 128)),
    ("expand_two", (128, 512)),
)


def finish(*refs):
    n = len(GROUPS) + 4
    ins, outs, held = refs[:n], refs[n : n + 13], refs[n + 13 : 2 * n + 13]
    wide_to, (in_sem, out_sem) = refs[2 * n + 13 : 2 * n + 24], refs[2 * n + 24 :]
    chunks = [(0, i) for i in range(4)] + [(1, i) for i in range(4)]

    def part(ref, which, i):
        size = ref.shape[1 - which] // 4
        return ref.at[:, pl.ds(i * size, size)] if which == 0 else ref.at[pl.ds(i * size, size)]

    small = [pltpu.make_async_copy(ins[i], held[i], in_sem.at[i]) for i in (n - 2, n - 1, *range(2, n - 2))]
    large = [
        pltpu.make_async_copy(part(ins[w], w, i), part(held[w], w, i), in_sem.at[n + 4 * w + i])
        for w, i in chunks
    ]
    for copy in small + large:
        copy.start()
    leaving = []

    def leave(src, dst):
        copy = pltpu.make_async_copy(src, dst, out_sem.at[len(leaving)])
        copy.start()
        leaving.append(copy)

    for i in range(2):
        small[i].wait()
    mid, wide = held[n - 2], held[n - 1]
    grads = (mid[0:4, :], mid[4:8, :], wide[0:3, :], wide[3:6, :])
    for ref, value, to in zip(wide_to[7:], grads, outs[9:]):
        ref[...] = value
        leave(ref, to)
    names = [name for name, _ in WEIGHTS]
    for g, group in enumerate(GROUPS[:4]):
        small[2 + g].wait()
        summed = held[2 + g]
        at = 0
        for name, rows in group:
            which = names.index(name)
            ref = wide_to[which]
            if len(ref.shape) == 4:
                for i in range(9):
                    lo = at + i * LANES
                    ref[i // 3, i % 3] = summed[lo : lo + LANES, :].astype(F32)
            else:
                height = ref.shape[0]
                for q in range(ref.shape[1] // LANES):
                    lo = at + q * height
                    ref[:, q * LANES : (q + 1) * LANES] = summed[lo : lo + height, :].astype(F32)
            leave(ref, outs[2 + which])
            at += rows
    small[n - 3].wait()
    wide_to[0][...] = held[n - 3][...].reshape(wide_to[0].shape)
    leave(wide_to[0], outs[2])
    for copy, (w, i) in zip(large, chunks):
        copy.wait()
        leave(part(held[w], w, i), part(outs[w], w, i))
    for copy in leaving:
        copy.wait()


def finished(parts, mid_shape, wide_shape):
    hbm = pl.BlockSpec(memory_space=pl.ANY)
    outs = [jax.ShapeDtypeStruct(p.shape, p.dtype) for p in parts[:2]]
    outs += [jax.ShapeDtypeStruct(s, F32) for _, s in WEIGHTS]
    outs += [jax.ShapeDtypeStruct(s, F32) for s in (mid_shape, mid_shape, wide_shape, wide_shape)]
    dma = pltpu.SemaphoreType.DMA
    return tuple(
        pl.pallas_call(
            finish,
            out_shape=outs,
            in_specs=[hbm] * len(parts),
            out_specs=[hbm] * 13,
            scratch_shapes=[pltpu.VMEM(p.shape, p.dtype) for p in parts]
            + [pltpu.VMEM(o.shape, o.dtype) for o in outs[2:]]
            + [dma((len(parts) + 8,)), dma((19,))],
            compiler_params=pltpu.CompilerParams(vmem_limit_bytes=60 << 20),
        )(*parts)
    )


def solution(mesh):
    nr, nc = mesh.shape["rows"], mesh.shape["crops"]
    whole = P()
    return jax.shard_map(
        functools.partial(on_device, nr, nc),
        mesh=mesh,
        in_specs=(P("crops", "rows", None, None),)
        + (whole,) * 11
        + (P("crops", None), P("crops"), P(("crops", "rows"), None, None, None)),
        out_specs=(P(("crops", "rows"), None, None, None), P("crops", "rows", None, None))
        + (whole,) * 11,
        check_vma=False,
    )
```

```python
import functools
from types import SimpleNamespace

import jax
import jax.numpy as jnp
from jax import lax
from jax.experimental import pallas as pl
from jax.experimental.pallas import tpu as pltpu
from jax.sharding import PartitionSpec as P

MESH = pl.DeviceIdType.MESH
F32 = jnp.float32
BF16 = jnp.bfloat16
epsilon = 1e-05
COT_AT = ((0,), (1,), (2, 3), (4,), (5, 6))
OUT_AT = ((0, 1), (2,), (3, 4), (5,), (6,), ())
PAD = 32
LANES = 128

ROUND_ROWS = (4, 2, 8, 2, 2, 10, 8, 2, 2, 14, 2)
WIDE = (2, 5, 6, 9)


GROUPS = (
    (("expand_two", 384), ("spatial_two", 1152)),
    (("reduce_two", 512),),
    (("expand_one", 512), ("shortcut", 1024)),
    (("spatial_one", 1152), ("expand_rest", 128)),
    (("slope", 128), ("slope_z", 128)),
)
GROUP_TYPES = (BF16, BF16, BF16, BF16, F32)


def group_rows(g, devices):
    group, unit = GROUPS[g], (16 if GROUP_TYPES[g] == BF16 else 8) * devices
    return -(-sum(rows for _, rows in group) // unit) * unit


def split(rows, parts):
    return [(i * rows // parts, (i + 1) * rows // parts) for i in range(parts)]


def dot(a, b):
    return lax.dot_general(a, b, (((1,), (0,)), ((), ())), preferred_element_type=F32)


def dot_nt(a, b):
    return lax.dot_general(a, b, (((1,), (1,)), ((), ())), preferred_element_type=F32)


def dot_tn(a, b):
    return lax.dot_general(a, b, (((0,), (0,)), ((), ())), preferred_element_type=F32)


def two_terms(x):
    high = x.astype(BF16)
    return high, (x - high.astype(F32)).astype(BF16)


def half_act(h):
    return h + h * jnp.tanh(h)


def half_silu(h, half_mask=0.5):
    t = jnp.tanh(h)
    p = h * t
    return h + p, (half_mask + half_mask * t) * (1.0 + (h - p))


def folded(x):
    return jnp.sum(x.reshape(-1, 8, x.shape[-1]), axis=0)


def row_sum(x):
    return jnp.sum(x, axis=0, keepdims=True)


def flat2(x):
    return x.reshape(-1, x.shape[-1])


def mega(cfg, r):
    nr, nc, nk, hh, wv = cfg.nr, cfg.nc, cfg.nk, cfg.hh, cfg.wv
    ndev, nxy, own = nr * nc, nc // 2, nk // nr
    m_half = hh * PAD
    row = lax.axis_index("rows")
    col = lax.axis_index("crops")
    xy, core = lax.div(col, 2), lax.rem(col, 2)
    me = row * nc + col

    barrier = pltpu.get_barrier_semaphore()

    def place(i):
        return (lax.div(i, nc), lax.rem(i, nc))

    def greet(k, c):
        pl.semaphore_signal(
            barrier, inc=1, device_id=place(lax.rem(me + k, ndev)), device_id_type=MESH
        )
        return c

    lax.fori_loop(1, ndev, greet, 0)

    image_copies = [
        pltpu.make_async_copy(r.images.at[k], r.x_in.at[k], r.image_sem.at[k]) for k in range(nk)
    ]
    weight_copies = {
        name: pltpu.make_async_copy(r.weights[name], r.held[name], r.weight_sem.at[i])
        for i, name in enumerate(cfg.order)
    }
    for i, copy in enumerate(weight_copies.values()):
        copy.start()
        if i == 0:
            for other in image_copies:
                other.start()

    def arrived(*names):
        for name in names:
            weight_copies[name].wait()

    lane = lax.broadcasted_iota(jnp.int32, (1, LANES), 1)
    for k in range(nk):
        gate = (jnp.full((1, LANES), r.depth_gate[k], jnp.int32) > 0).astype(F32)
        r.mask_one[k] = (lane < r.widths[0, k]).astype(F32)
        r.mask_two[k] = (lane < r.widths[1, k]).astype(F32) * gate
        r.gates[k] = jnp.concatenate([gate] * 4, axis=1)
    col_mask = (lax.broadcasted_iota(jnp.int32, (PAD, 1), 0) < wv).astype(F32)
    half_mask = 0.5 * col_mask

    chips = nr * nxy
    chip = row * nxy + xy

    def chip_copy(src, dst, to, send_sem, recv_sem):
        return pltpu.make_async_remote_copy(
            src_ref=src,
            dst_ref=dst,
            send_sem=send_sem,
            recv_sem=recv_sem,
            device_id=(lax.div(to, nxy), lax.rem(to, nxy) * 2 + core),
            device_id_type=MESH,
        )

    def to_chips(copy_to):
        def send(k, c):
            copy_to(lax.rem(chip + k, chips)).start()
            return c

        lax.fori_loop(1, chips, send, 0)

    def all_of(ref, n, sem):
        pltpu.make_async_copy(ref.at[pl.ds(0, n)], ref.at[pl.ds(0, n)], sem).wait()

    def to_all(copy_to):
        def send(k, c):
            copy_to(lax.rem(me + k, ndev)).start()
            return c

        lax.fori_loop(1, ndev, send, 0)

    def sum_copy(idx, p):
        mine = r.sums[idx].at[me]
        return pltpu.make_async_remote_copy(
            src_ref=mine,
            dst_ref=mine,
            send_sem=r.sum_send,
            recv_sem=r.sum_recv.at[idx],
            device_id=place(p),
            device_id_type=MESH,
        )

    def pair_copy(step, src, dst):
        return pltpu.make_async_remote_copy(
            src_ref=src,
            dst_ref=dst,
            send_sem=r.pair_send.at[step],
            recv_sem=r.pair_recv.at[step],
            device_id=(row, xy * 2 + 1 - core),
            device_id_type=MESH,
        )

    def lines(vectors):
        return [v[:, q * LANES : (q + 1) * LANES] for v in vectors for q in range(v.shape[1] // LANES)]

    def send_sums(idx, vectors):
        rows = lines(vectors)
        assert len(rows) == ROUND_ROWS[idx]
        slots = r.sums[idx]
        if idx in WIDE:
            half = len(rows) // 2
            both, came = r.both[idx], r.from_pair[idx]
            for at, v in enumerate(rows):
                both[at // half, at % half : at % half + 1, :] = v
            copy = pair_copy(WIDE.index(idx), both.at[1 - core], came)
            copy.start()
            copy.wait()
            slots[chip] = both[core] + came[...]
        else:
            for at, v in enumerate(rows):
                slots[me, at : at + 1, :] = v
        if idx in WIDE:
            mine = slots.at[chip]
            to_chips(lambda to: chip_copy(mine, mine, to, r.sum_send, r.sum_recv.at[idx]))
        else:
            to_all(lambda p: sum_copy(idx, p))

    def take_sums(idx, widths):
        slots = r.sums[idx]
        others = slots.shape[0] - 1
        all_of(slots, others, r.sum_recv.at[idx])
        if idx in WIDE:
            totals = r.totals[idx]
            totals[core] = jnp.sum(slots[...], axis=0)
            mine = totals.at[core]
            copy = pair_copy(4 + WIDE.index(idx), mine, mine)
            copy.start()
            copy.wait()
            half = ROUND_ROWS[idx] // 2
            rows = [totals[at // half, at % half : at % half + 1, :] for at in range(2 * half)]
        else:
            total = jnp.sum(slots[...], axis=0)
            rows = [total[at : at + 1, :] for at in range(ROUND_ROWS[idx])]
        all_of(slots, others, r.sum_send)
        result, at = [], 0
        for w in widths:
            parts = rows[at : at + w // LANES]
            at += w // LANES
            result.append(jnp.concatenate(parts, axis=1) if len(parts) > 1 else parts[0])
        return result

    up_ok, down_ok = row > 0, row < nr - 1
    halo_up = (False, False, True, False, True, False, True, True, True)

    def halo(idx):
        return pltpu.make_async_remote_copy(
            src_ref=r.edge[idx],
            dst_ref=r.halo[idx],
            send_sem=r.halo_send.at[idx],
            recv_sem=r.halo_recv.at[idx],
            device_id=(row - 1 if halo_up[idx] else row + 1, col),
            device_id_type=MESH,
        )

    def halo_put(idx, at, rows):
        r.edge[idx][at] = rows.astype(BF16)

    def halo_start(idx):
        @pl.when(up_ok if halo_up[idx] else down_ok)
        def _():
            halo(idx).start()

    def halo_wait(idx):
        @pl.when(up_ok if halo_up[idx] else down_ok)
        def _():
            halo(idx).wait_send()

        @pl.when(down_ok if halo_up[idx] else up_ok)
        def _():
            halo(idx).wait_recv()

    def halo_row(idx, at, k):
        return r.halo[idx][at, k].astype(F32)

    def both_edges(idx, ref):
        halo_put(idx, 0, ref[:, hh - 1])
        halo_put(idx + 1, 0, ref[:, 0])

    def skip_send(vectors):
        for at, v in enumerate(lines(vectors)):
            r.pair_rows[at // 4, at % 4 : at % 4 + 1, :] = v
        pair_copy(8, r.pair_rows.at[1 - core], r.pair_came).start()

    def skip_spread():
        pair_copy(8, r.pair_rows.at[1 - core], r.pair_came).wait()
        r.pair_chips[chip] = r.pair_rows[core] + r.pair_came[...]
        mine = r.pair_chips.at[chip]
        to_chips(lambda to: chip_copy(mine, mine, to, r.chip_send.at[0], r.chip_recv.at[0]))

    def skip_return():
        all_of(r.pair_chips, chips - 1, r.chip_recv.at[0])
        all_of(r.pair_chips, chips - 1, r.chip_send.at[0])
        r.pair_total[core] = jnp.sum(r.pair_chips[...], axis=0)
        mine = r.pair_total.at[core]
        pair_copy(9, mine, mine).start()

    def skip_take():
        mine = r.pair_total.at[core]
        pair_copy(9, mine, mine).wait()
        return [
            jnp.concatenate([r.pair_total[i, q : q + 1, :] for q in range(4)], axis=1)
            for i in range(2)
        ]

    axes = (("core", 2), ("xy", nxy), ("rows", nr))
    seat = {"core": core, "xy": xy, "rows": row}

    def device_of(kind, i):
        if kind == "core":
            return (row, xy * 2 + i)
        if kind == "xy":
            return (row, i * 2 + core)
        return (i, col)

    def level_rows(g, level):
        size = cfg.group_size[g]
        for _, n in axes[:level]:
            size //= n
        return size

    def offset(g, level):
        at = 0
        for i, (kind, _) in enumerate(axes[:level]):
            at = at + seat[kind] * level_rows(g, i + 1)
        return pl.multiple_of(at, 8) if level else 0

    def scatter_send(g, level):
        kind, n = axes[level]
        chunk = level_rows(g, level + 1)
        for k in range(1, n):
            p = lax.rem(seat[kind] + k, n)
            pltpu.make_async_remote_copy(
                src_ref=r.part[g][level].at[pl.ds(pl.multiple_of(p * chunk, 8), chunk)],
                dst_ref=r.came[g][level].at[k - 1],
                send_sem=r.grad_send.at[g],
                recv_sem=r.grad_recv.at[g, level],
                device_id=device_of(kind, p),
                device_id_type=MESH,
            ).start()

    def scatter_take(g, level):
        kind, n = axes[level]
        chunk = level_rows(g, level + 1)
        came = r.came[g][level]
        pltpu.make_async_copy(came, came, r.grad_recv.at[g, level]).wait()
        mine = pl.ds(pl.multiple_of(seat[kind] * chunk, 8), chunk)
        total = r.part[g][level][mine, :].astype(F32) + jnp.sum(came[...].astype(F32), axis=0)
        pltpu.make_async_copy(came, came, r.grad_send.at[g]).wait()
        if level + 1 < len(axes):
            r.part[g][level + 1][...] = total.astype(GROUP_TYPES[g])
        else:
            r.full[g][pl.ds(offset(g, 3), chunk), :] = total.astype(GROUP_TYPES[g])

    def gather_send(g, level):
        kind, n = axes[level]
        size = level_rows(g, level + 1)
        region = r.full[g].at[pl.ds(offset(g, level + 1), size)]
        for k in range(1, n):
            p = lax.rem(seat[kind] + k, n)
            pltpu.make_async_remote_copy(
                src_ref=region,
                dst_ref=region,
                send_sem=r.grad_send.at[g],
                recv_sem=r.grad_recv.at[g, 3 + level],
                device_id=device_of(kind, p),
                device_id_type=MESH,
            ).start()

    def gather_take(g, level):
        n = axes[level][1]
        size = level_rows(g, level + 1) * (n - 1)
        bytes_of = r.full[g].at[pl.ds(0, size)]
        pltpu.make_async_copy(bytes_of, bytes_of, r.grad_recv.at[g, 3 + level]).wait()
        pltpu.make_async_copy(bytes_of, bytes_of, r.grad_send.at[g]).wait()

    steps = (
        (scatter_send, 0), (scatter_take, 0), (scatter_send, 1), (scatter_take, 1),
        (scatter_send, 2), (scatter_take, 2), (gather_send, 2), (gather_take, 2),
        (gather_send, 1), (gather_take, 1), (gather_send, 0), (gather_take, 0),
    )

    def advance(g, phase):
        for fn, level in steps[max(0, 2 * phase - 1) : 2 * phase + 1]:
            fn(g, level)

    def stage(g, name, value):
        at = 0
        for other, rows in GROUPS[g]:
            if other == name:
                break
            at += rows
        blocks = value.shape[1] // LANES
        for q in range(blocks):
            n = value.shape[0]
            lo = at + q * n
            r.part[g][0][lo : lo + n, :] = value[:, q * LANES : (q + 1) * LANES].astype(GROUP_TYPES[g])

    def one_send(value):
        r.one_both[...] = value.reshape(2, chips, -1, LANES)
        pair_copy(10, r.one_both.at[1 - core], r.one_came).start()

    def one_spread():
        pair_copy(10, r.one_both.at[1 - core], r.one_came).wait()
        half, slots = r.one_half, r.one_slots
        half[...] = r.one_both[core] + r.one_came[...]
        sems = (r.chip_send.at[1], r.chip_recv.at[1])
        to_chips(lambda to: chip_copy(half.at[to], slots.at[chip], to, *sems))

    def one_gather():
        slots = r.one_slots
        all_of(slots, chips - 1, r.chip_recv.at[1])
        slots[chip] = r.one_half[chip]
        r.one_whole[core, chip] = jnp.sum(slots[...], axis=0)
        mine = r.one_whole.at[core, chip]
        sems = (r.chip_send.at[2], r.chip_recv.at[2])
        to_chips(lambda to: chip_copy(mine, mine, to, *sems))

    def one_return():
        slots = r.one_slots
        all_of(slots, chips - 1, r.chip_send.at[1])
        all_of(slots, chips - 1, r.chip_recv.at[2])
        all_of(slots, chips - 1, r.chip_send.at[2])
        mine = r.one_whole.at[core]
        pair_copy(11, mine, mine).start()

    def one_take():
        mine = r.one_whole.at[core]
        pair_copy(11, mine, mine).wait()

    def coefficients(total, square, count, gain, bias):
        n = jnp.maximum(count, 1.0)
        mu = total / n
        inv = lax.rsqrt(square / n - mu * mu + epsilon)
        scale = gain * inv
        return SimpleNamespace(n=n, mu=mu, inv=inv, scale=scale, shift=bias - mu * scale)

    def factors(norm, dbias, dgain):
        c2 = -norm.scale * norm.inv * dgain / norm.n
        c3 = -norm.scale * dbias / norm.n - c2 * norm.mu
        return norm.scale, c2, c3

    def gain_sum(norm, total, z_total):
        return norm.inv * (z_total - norm.mu * total)

    def slope_sums(mask, slope, z, a, norm):
        def scaled(k, c):
            t = mask[k] * slope[k]
            r.dz4[k] = t.astype(BF16)
            r.slope_z[k] = (t * ((z[k] - norm.mu) * norm.inv)).astype(BF16)
            return c

        loop(scaled)
        flat_a = flat2(a[...])
        stage(4, "slope", dot_tn(flat_a, flat2(r.dz4[...])))
        stage(4, "slope_z", dot_tn(flat_a, flat2(r.slope_z[...])))

    def through(weight, c2, c3):
        high, low = two_terms(weight.astype(F32) * c2)
        b = dot_nt(high, weight) + dot_nt(low, weight)
        v = sum(dot_nt(jnp.broadcast_to(c, (16, c.shape[1])), weight) for c in two_terms(c3))
        return b, v[0:1]

    def chained(norm, u_sum, uz_sum, t_sum, tz_sum, b, v):
        k1, k2 = r.full[4][0:LANES, :], r.full[4][LANES : 2 * LANES, :]
        dbias = u_sum + row_sum(k1 * b) + t_sum * v
        dgain = gain_sum(norm, u_sum, uz_sum) + row_sum(k2 * b) + gain_sum(norm, t_sum, tz_sum) * v
        return dbias, dgain

    def loop(body, init=0):
        for k in range(nk):
            init = body(k, init)
        return init

    def zero8(width, count):
        return tuple(jnp.zeros((8, width), F32) for _ in range(count))

    def row_pieces(src_of, dst_of, send, recv, local):
        pieces = []
        for w, (lo, hi) in enumerate(cfg.pieces):
            for k in range(1, nr):
                p = lax.rem(row + k, nr)
                pieces.append(
                    pltpu.make_async_remote_copy(
                        src_ref=src_of(p, lo, hi - lo),
                        dst_ref=dst_of(lo, hi - lo),
                        send_sem=send,
                        recv_sem=recv,
                        device_id=(p, col),
                        device_id_type=MESH,
                    )
                )
        here = pltpu.make_async_copy(src_of(row, 0, hh), dst_of(0, hh), local)
        return pieces, here

    def wait_pieces(which):
        bytes_of = r.out_rows.at[pl.ds(0, nk - own)]
        pltpu.make_async_copy(bytes_of, bytes_of, r.row_recv.at[which]).wait()
        pltpu.make_async_copy(bytes_of, bytes_of, r.row_send.at[which]).wait()

    def start_pieces(pieces, *which):
        for w in which:
            for copy in pieces[w * (nr - 1) : (w + 1) * (nr - 1)]:
                copy.start()

    cot_copies, cot_local = row_pieces(
        lambda p, lo, n: r.cot.at[:, pl.ds(p * hh + lo, n)],
        lambda lo, n: r.cot_rows.at[pl.ds(row * own, own), pl.ds(lo, n)],
        r.row_send.at[0], r.row_recv.at[0], r.local_sem.at[0],
    )
    out_copies, out_local = row_pieces(
        lambda p, lo, n: r.out_rows.at[pl.ds(p * own, own), pl.ds(lo, n)],
        lambda lo, n: r.out.at[:, pl.ds(row * hh + lo, n)],
        r.row_send.at[1], r.row_recv.at[1], r.local_sem.at[1],
    )
    cot_local.start()

    lane_blocks = cfg.c_in // LANES
    for slot in range(2 * hh):
        for q in range(lane_blocks):
            r.spread[q, slot, 2 * wv : 2 * PAD, :] = jnp.zeros((2 * PAD - 2 * wv, LANES), F32)
    arrived("reduce_one")
    w1 = r.reduce_one[...]
    acc = zero8(LANES, 2)
    for copy in image_copies:
        copy.wait()

    def first(k, acc):
        for i in range(2 * hh):
            for q in range(lane_blocks):
                lanes = slice(q * LANES, (q + 1) * LANES)
                r.spread[q, i, 0 : 2 * wv, :] = r.x_in[k, i, :, lanes].astype(F32)
        m = r.mask_one[k]
        s1, s2 = acc
        for pr in range(2):
            for pc in range(2):
                for i in range(hh):
                    for q in range(lane_blocks):
                        lanes = slice(q * LANES, (q + 1) * LANES)
                        r.x[pr, pc, k, i, :, lanes] = r.spread[
                            q, 2 * i + pr, pl.ds(pc, PAD, stride=2), :
                        ].astype(BF16)
                z = dot(flat2(r.x[pr, pc, k]), w1)
                r.z1[pr, pc, k] = z.reshape(hh, PAD, LANES)
                s1 += m * folded(z)
                s2 += m * folded(z * z)
        return s1, s2

    s1, s2 = loop(first, acc)
    count_one = sum(r.mask_one[k] for k in range(nk))
    count_two = sum(r.mask_two[k] for k in range(nk))
    arrived("shortcut")
    sc = r.shortcut[...]

    def skip(k, acc):
        z = dot(flat2(r.x[0, 0, k]), sc)
        r.zs[k] = z.reshape(hh, PAD, cfg.c_out)
        return acc[0] + folded(z), acc[1] + folded(z * z)

    zs1, zs2 = loop(skip, zero8(cfg.c_out, 2))
    for pc in range(2):
        halo_put(0, pc, r.z1[1, pc, :, hh - 1])
    pl.semaphore_wait(barrier, ndev - 1)
    send_sums(0, [row_sum(s1), row_sum(s2), count_one, count_two])
    halo_start(0)
    skip_send([row_sum(zs1), row_sum(zs2)])
    start_pieces(cot_copies, *COT_AT[0])
    arrived("mid_gain", "mid_bias", "spatial_one")
    t1, t2, active_one, active_two = take_sums(0, [LANES] * 4)
    half_px, full_px = float(hh * wv), float(4 * hh * wv)
    active_gate = active_two[:, 0:1]
    g1, b1 = r.mid_gain[0:1, :], r.mid_bias[0:1, :]
    n1 = coefficients(t1, t2, active_one * full_px, g1, b1)
    halo_wait(0)

    def shifted_right(a):
        return pltpu.roll(a, 1, axis=a.ndim - 2)

    def shifted_left(a):
        return pltpu.roll(a, PAD - 1, axis=a.ndim - 2)

    def affine(norm, m):
        return 0.5 * m * norm.scale, (0.5 * m * norm.shift) * col_mask

    k_one = [r.spatial_one[i] for i in range(3)]

    def second(k, acc):
        m = r.mask_one[k]
        ah, bh = affine(n1, m)
        for pr in range(2):
            for pc in range(2):
                a = half_act(r.z1[pr, pc, k] * ah + bh)
                dst = r.even if pr == 0 else r.odd
                rows = pl.ds(0, hh) if pr == 0 else pl.ds(1, hh)
                if pc == 0:
                    dst[k, rows, :, LANES : 2 * LANES] = a.astype(BF16)
                else:
                    dst[k, rows, :, 2 * LANES : 3 * LANES] = a.astype(BF16)
                    dst[k, rows, :, 0:LANES] = shifted_right(a).astype(BF16)
        for pc in range(2):
            a = half_act(halo_row(0, pc, k) * ah + bh)
            a = jnp.where(row > 0, a, 0.0)
            if pc == 0:
                r.odd[k, 0, :, LANES : 2 * LANES] = a.astype(BF16)
            else:
                r.odd[k, 0, :, 2 * LANES : 3 * LANES] = a.astype(BF16)
                r.odd[k, 0, :, 0:LANES] = shifted_right(a).astype(BF16)
        z = dot(flat2(r.even[k]), k_one[1])
        z += dot(flat2(r.odd[k, 1 : hh + 1]), k_one[2])
        z += dot(flat2(r.odd[k, 0:hh]), k_one[0])
        z = z.reshape(hh, PAD, LANES) * col_mask
        r.z2[k] = z
        return acc[0] + m * folded(z), acc[1] + m * folded(z * z)

    s1, s2 = loop(second, zero8(LANES, 2))
    send_sums(1, [row_sum(s1), row_sum(s2)])
    skip_spread()

    def early(k, c):
        m = r.mask_one[k]
        ah, bh = affine(n1, m)
        for pr in range(2):
            for pc in range(2):
                zhat = (r.z1[pr, pc, k] - n1.mu) * (m * n1.inv)
                r.dz1[pr, pc, k] = zhat.astype(BF16)
                _, r.s1[pr, pc, k] = half_silu(r.z1[pr, pc, k] * ah + bh, half_mask)
        r.dz4[k] = jnp.broadcast_to(m, (hh, PAD, LANES)).astype(BF16)
        return c

    loop(early)
    for name in ("expand_one", "wide_gain", "wide_bias", "reduce_two"):
        arrived(name)
    planes = [(pr, pc) for pr in range(2) for pc in range(2)]
    r.part_z[...] = sum(dot_tn(flat2(r.x[q]), flat2(r.dz1[q])) for q in planes)
    r.part_m[...] = sum(dot_tn(flat2(r.x[q]), flat2(r.dz4[...])) for q in planes)
    start_pieces(cot_copies, *COT_AT[1])
    t1, t2 = take_sums(1, [LANES] * 2)
    n2 = coefficients(t1, t2, active_one * half_px, r.mid_gain[1:2, :], r.mid_bias[1:2, :])
    e1 = r.expand_one[...]

    def third(k, acc):
        ah, bh = affine(n2, r.mask_one[k])
        a, s = half_silu(r.z2[k] * ah + bh, half_mask)
        r.s2[k] = s
        a = a.astype(BF16)
        r.a2[k] = a
        z = dot(flat2(a), e1)
        r.z3[k] = z.reshape(hh, PAD, cfg.c_out)
        t = r.mask_one[k] * s
        return (
            acc[0] + folded(z), acc[1] + folded(z * z), acc[2] + folded(t), acc[3] + folded(t * r.z2[k])
        )

    s1, s2, t2_sum, t2z_sum = loop(third, zero8(cfg.c_out, 2) + zero8(LANES, 2))
    send_sums(2, [row_sum(s1), row_sum(s2)])
    slope_sums(r.mask_one, r.s2, r.z2, r.a2, n2)
    advance(4, 0)
    arrived("spatial_two", "expand_two")
    def tap(ref, i, j):
        return ref[i, j * LANES : (j + 1) * LANES, :].T

    for i in range(3):
        for j in range(3):
            r.back_two[i, j * LANES : (j + 1) * LANES, :] = tap(r.spatial_two, 2 - i, 2 - j)
    zeros = jnp.zeros((LANES, LANES), BF16)
    k1 = r.spatial_one
    here = [[tap(k1, 2, 2), tap(k1, 1, 2), tap(k1, 2, 1), tap(k1, 1, 1)],
            [tap(k1, 2, 0), tap(k1, 1, 0), zeros, zeros]]
    below = [[tap(k1, 0, 2), tap(k1, 0, 1)], [tap(k1, 0, 0), zeros]]
    for ref, blocks in ((r.back_here, here), (r.back_below, below)):
        for i, line in enumerate(blocks):
            for j, block in enumerate(line):
                ref[i * LANES : (i + 1) * LANES, j * LANES : (j + 1) * LANES] = block
    skip_return()
    start_pieces(cot_copies, *COT_AT[2])
    t1, t2 = take_sums(2, [cfg.c_out] * 2)
    ts1, ts2 = skip_take()
    all_px = float(nk * nc) * float(nr) * half_px
    n3 = coefficients(t1, t2, all_px, r.wide_gain[0:1, :], r.wide_bias[0:1, :])
    ns = coefficients(ts1, ts2, all_px, r.wide_gain[1:2, :], r.wide_bias[1:2, :])
    w2 = r.reduce_two[...]

    a3, as_ = 0.5 * n3.scale, 0.5 * ns.scale
    b3 = (0.5 * (n3.shift + ns.shift)) * col_mask

    def fourth(k, acc):
        for i in range(hh):
            h = r.z3[k, i] * a3 + r.zs[k, i] * as_ + b3
            r.hidden[k, i] = half_act(h).astype(BF16)
        z = dot(flat2(r.hidden[k]), w2)
        r.z4[k] = z.reshape(hh, PAD, LANES)
        m = r.mask_two[k]
        return acc[0] + m * folded(z), acc[1] + m * folded(z * z)

    s1, s2 = loop(fourth, zero8(LANES, 2))
    send_sums(3, [row_sum(s1), row_sum(s2)])
    both_edges(1, r.z4)
    halo_start(1)
    halo_start(2)

    def hats(k, c):
        for i in range(hh):
            r.dz3[k, i] = ((r.z3[k, i] - n3.mu) * n3.inv).astype(BF16)
            r.dzs[k, i] = ((r.zs[k, i] - ns.mu) * ns.inv).astype(BF16)
            _, r.s3[k, i] = half_silu(r.z3[k, i] * a3 + r.zs[k, i] * as_ + b3, half_mask)
        return c

    advance(4, 1)
    loop(hats)
    ones = jnp.ones((nk * m_half, LANES), BF16)
    r.expand_z[...] = dot_tn(flat2(r.a2[...]), flat2(r.dz3[...]))
    r.expand_m[...] = dot_tn(flat2(r.a2[...]), ones)
    r.skip_z[...] = dot_tn(flat2(r.x[0, 0]), flat2(r.dzs[...]))
    r.skip_m[...] = dot_tn(flat2(r.x[0, 0]), ones)
    start_pieces(cot_copies, *COT_AT[3])
    t1, t2 = take_sums(3, [LANES] * 2)
    n4 = coefficients(t1, t2, active_two * half_px, r.mid_gain[2:3, :], r.mid_bias[2:3, :])
    halo_wait(1)
    halo_wait(2)

    def put3(dst, k, rows, a):
        dst[k, rows, :, LANES : 2 * LANES] = a.astype(BF16)
        dst[k, rows, :, 0:LANES] = shifted_right(a).astype(BF16)
        dst[k, rows, :, 2 * LANES : 3 * LANES] = shifted_left(a).astype(BF16)

    k_two = [r.spatial_two[i] for i in range(3)]

    def fifth(k, acc):
        m = r.mask_two[k]
        ah, bh = affine(n4, m)
        put3(r.a4, k, pl.ds(1, hh), half_act(r.z4[k] * ah + bh))
        a = half_act(halo_row(1, 0, k) * ah + bh)
        put3(r.a4, k, 0, jnp.where(row > 0, a, 0.0))
        a = half_act(halo_row(2, 0, k) * ah + bh)
        put3(r.a4, k, hh + 1, jnp.where(row < nr - 1, a, 0.0))
        z = sum(dot(flat2(r.a4[k, i : i + hh]), k_two[i]) for i in range(3))
        z = z.reshape(hh, PAD, LANES) * col_mask
        r.z5[k] = z
        return acc[0] + m * folded(z), acc[1] + m * folded(z * z)

    s1, s2 = loop(fifth, zero8(LANES, 2))
    send_sums(4, [row_sum(s1), row_sum(s2)])
    advance(4, 2)
    start_pieces(cot_copies, *COT_AT[4])

    def slope_four(k, c):
        ah, bh = affine(n4, r.mask_two[k])
        _, r.s4[k] = half_silu(r.z4[k] * ah + bh, half_mask)
        return c

    loop(slope_four)
    t1, t2 = take_sums(4, [LANES] * 2)
    n5 = coefficients(t1, t2, active_two * half_px, r.mid_gain[3:4, :], r.mid_bias[3:4, :])
    e2 = r.expand_two[...]

    def sixth(k, acc):
        ah, bh = affine(n5, r.mask_two[k])
        a = half_act(r.z5[k] * ah + bh).astype(BF16)
        r.a5[k] = a
        z = dot(flat2(a), e2)
        r.z6[k] = z.reshape(hh, PAD, cfg.c_out)
        g = r.gates[k]
        return acc[0] + g * folded(z), acc[1] + g * folded(z * z)

    s1, s2 = loop(sixth, zero8(cfg.c_out, 2))
    send_sums(5, [row_sum(v) for v in (s1, s2, t2_sum, t2z_sum)])
    def slope_five(k, c):
        ah, bh = affine(n5, r.mask_two[k])
        _, r.s5[k] = half_silu(r.z5[k] * ah + bh, half_mask)
        return c

    loop(slope_five)
    both_edges(3, r.z5)
    halo_start(3)
    halo_start(4)
    advance(4, 3)
    wait_pieces(0)
    cot_local.wait()
    t1, t2, t2_sum, t2z_sum = take_sums(5, [cfg.c_out] * 2 + [LANES] * 2)
    gate_count = active_gate * half_px
    n6 = coefficients(t1, t2, gate_count, r.wide_gain[2:3, :], r.wide_bias[2:3, :])
    pad_rows = jnp.zeros((PAD - wv, cfg.c_out), F32)

    def cot_row(k, i):
        return jnp.concatenate([r.cot_rows[k, i].astype(F32), pad_rows], axis=0)

    def seventh(k, acc):
        g = r.gates[k]
        a6, b6 = (0.5 * g) * n6.scale, ((0.5 * g) * n6.shift) * col_mask
        d1, d2 = acc
        for i in range(hh):
            hid = r.hidden[k, i].astype(F32)
            z = r.z6[k, i]
            a, s = half_silu(0.5 * hid + (z * a6 + b6))
            r.out_rows[k, i] = jnp.where(g > 0.0, a, hid)[:wv].astype(BF16)
            live = g * cot_row(k, i) * s
            r.live[k, i] = live
            d1 += folded(live)
            d2 += folded(live * z)
        return d1, d2

    sums = loop(seventh, zero8(cfg.c_out, 2))
    send_sums(6, [row_sum(v) for v in sums])

    advance(4, 4)
    start_pieces(out_copies, *OUT_AT[0])
    out_local.start()
    db6, q6 = take_sums(6, [cfg.c_out] * 2)
    dg6 = gain_sum(n6, db6, q6)
    c1, c2, c3 = factors(n6, db6, dg6)

    def eighth(k, acc, c1=c1, c2=c2, c3=c3):
        g = r.gates[k]
        f1, f2, f3 = g * c1, g * c2, (g * c3) * col_mask
        for i in range(hh):
            r.dz6[k, i] = (r.live[k, i] * f1 + r.z6[k, i] * f2 + f3).astype(BF16)
        q = dot_nt(flat2(r.dz6[k]), e2).reshape(hh, PAD, LANES) * r.s5[k]
        r.q5[k] = q
        m = r.mask_two[k]
        return acc[0] + m * folded(q), acc[1] + m * folded(q * r.z5[k])

    d1, d2 = loop(eighth, zero8(LANES, 2))
    send_sums(7, [row_sum(d1), row_sum(d2)])
    both_edges(5, r.q5)
    halo_start(5)
    halo_start(6)
    expand_grad = dot_tn(flat2(r.a5[...]), flat2(r.dz6[...]))
    stage(0, "expand_two", expand_grad[:, : 3 * LANES])
    stage(3, "expand_rest", expand_grad[:, 3 * LANES :])
    halo_wait(3)
    halo_wait(4)
    advance(4, 5)
    start_pieces(out_copies, *OUT_AT[1])
    db5, q5 = take_sums(7, [LANES] * 2)
    dg5 = gain_sum(n5, db5, q5)
    c1, c2, c3 = factors(n5, db5, dg5)
    halo_wait(5)
    halo_wait(6)

    def ninth(k, acc, c1=c1, c2=c2, c3=c3):
        m = r.mask_two[k]
        f1, f2, f3 = m * c1, m * c2, (m * c3) * col_mask
        put3(r.dz5, k, pl.ds(1, hh), r.q5[k] * f1 + r.z5[k] * f2 + f3)
        d = halo_row(5, 0, k) * f1 + halo_row(3, 0, k) * f2 + f3
        put3(r.dz5, k, 0, jnp.where(row > 0, d, 0.0))
        d = halo_row(6, 0, k) * f1 + halo_row(4, 0, k) * f2 + f3
        put3(r.dz5, k, hh + 1, jnp.where(row < nr - 1, d, 0.0))
        q = sum(dot(flat2(r.dz5[k, i : i + hh]), r.back_two[i]) for i in range(3))
        q = q.reshape(hh, PAD, LANES) * r.s4[k]
        r.q4[k] = q
        return acc[0] + m * folded(q), acc[1] + m * folded(q * r.z4[k])

    d1, d2 = loop(ninth, zero8(LANES, 2))
    send_sums(8, [row_sum(d1), row_sum(d2)])
    halo_put(8, 0, r.z2[:, 0])
    halo_start(8)

    d5 = flat2(r.dz5[:, 1 : hh + 1, :, LANES : 2 * LANES])
    stage(
        0,
        "spatial_two",
        jnp.concatenate([dot_tn(flat2(r.a4[:, i : i + hh]), d5) for i in range(3)], axis=0),
    )
    advance(4, 6)
    advance(0, 0)
    start_pieces(out_copies, *OUT_AT[2])
    db4, q4 = take_sums(8, [LANES] * 2)
    advance(0, 1)
    dg4 = gain_sum(n4, db4, q4)
    c1, c2, c3 = factors(n4, db4, dg4)

    def tenth(k, acc, c1=c1, c2=c2, c3=c3):
        m, g = r.mask_two[k], r.gates[k]
        f1, f2, f3 = m * c1, m * c2, (m * c3) * col_mask
        r.dz4[k] = (r.q4[k] * f1 + r.z4[k] * f2 + f3).astype(BF16)
        back = dot_nt(flat2(r.dz4[k]), w2).reshape(hh, PAD, cfg.c_out)
        e1_, e2_, e3_, u1, u2 = acc
        for i in range(hh):
            d = back[i] + (1.0 - g) * cot_row(k, i) + r.live[k, i]
            q = d.astype(BF16).astype(F32) * r.s3[k, i]
            r.q3[k, i] = q
            r.dz3[k, i] = (q * n3.scale).astype(BF16)
            e1_ += folded(q)
            e2_ += folded(q * r.z3[k, i])
            e3_ += folded(q * r.zs[k, i])
        u = dot_nt(flat2(r.dz3[k]), e1).reshape(hh, PAD, LANES)
        r.q2[k] = u
        ut = (r.mask_one[k] * u) * r.s2[k]
        return e1_, e2_, e3_, u1 + folded(ut), u2 + folded(ut * r.z2[k])

    sums = loop(tenth, zero8(cfg.c_out, 3) + zero8(LANES, 2))
    send_sums(9, [row_sum(v) for v in sums])
    halo_put(7, 0, r.q2[:, 0])
    halo_start(7)
    stage(1, "reduce_two", dot_tn(flat2(r.hidden[...]), flat2(r.dz4[...])))
    advance(1, 0)
    expand_q = dot_tn(flat2(r.a2[...]), flat2(r.dz3[...]))
    skip_q = dot_tn(flat2(r.x[0, 0]), flat2(r.dz3[...]))
    halo_wait(8)

    def edge_slope(k, c):
        ah, bh = affine(n2, r.mask_one[k])
        a, t = half_silu(halo_row(8, 0, k) * ah + bh, half_mask)
        r.edge_a[k] = a.astype(BF16)
        r.edge_t[k] = t
        return c

    loop(edge_slope)
    advance(1, 1)
    advance(0, 2)
    start_pieces(out_copies, *OUT_AT[3])
    db3, q3, qs, u_sum, uz_sum = take_sums(9, [cfg.c_out] * 3 + [LANES] * 2)
    dg3, dgs = gain_sum(n3, db3, q3), gain_sum(ns, db3, qs)
    f3_, fs_ = factors(n3, db3, dg3), factors(ns, db3, dgs)
    b, v2 = through(e1, *f3_[1:])
    db2, dg2 = chained(n2, u_sum, uz_sum, t2_sum, t2z_sum, b, v2)
    c1, c2, c3 = factors(n2, db2, dg2)
    b2 = two_terms(b)

    def four(x):
        return jnp.concatenate([x] * (cfg.c_out // LANES), axis=1)

    def by_parts(q_part, z_part, m_part, norm, fs):
        total = q_part + (fs[1] / norm.inv) * z_part[...]
        return total + (fs[2] + fs[1] * norm.mu) * four(m_part[...])

    stage(2, "expand_one", by_parts(expand_q, r.expand_z, r.expand_m, n3, f3_))
    stage(2, "shortcut", by_parts(skip_q * (ns.scale / n3.scale), r.skip_z, r.skip_m, ns, fs_))
    advance(2, 0)
    halo_wait(7)
    edge_ab = sum(dot(flat2(r.edge_a[...]), t) for t in b2).reshape(nk, PAD, LANES)

    def twelfth(k, c, c1=c1, c2=c2, c3=c3):
        m = r.mask_one[k]
        f1, f2, f3 = m * c1, m * c2, (m * c3) * col_mask
        ab = sum(dot(flat2(r.a2[k]), t) for t in b2).reshape(hh, PAD, LANES)
        q = (r.q2[k] + ab + v2) * r.s2[k]
        d = q * f1 + r.z2[k] * f2 + f3
        r.dz2[k, 0:hh, :, 0:LANES] = d.astype(BF16)
        r.dz2[k, 0:hh, :, LANES : 2 * LANES] = shifted_left(d).astype(BF16)
        q = (halo_row(7, 0, k) + edge_ab[k] + v2) * r.edge_t[k]
        d = jnp.where(row < nr - 1, q * f1 + halo_row(8, 0, k) * f2 + f3, 0.0)
        r.dz2[k, hh, :, 0:LANES] = d.astype(BF16)
        r.dz2[k, hh, :, LANES : 2 * LANES] = shifted_left(d).astype(BF16)
        return c

    loop(twelfth)
    d2_ = flat2(r.dz2[:, 0:hh, :, 0:LANES])
    inputs = [r.odd[:, 0:hh], r.even[...], r.odd[:, 1 : hh + 1]]
    stage(3, "spatial_one", jnp.concatenate([dot_tn(flat2(a), d2_) for a in inputs], axis=0))


    advance(3, 0)
    advance(2, 1)

    def thirteenth(k, acc):
        m = r.mask_one[k]
        u = dot(flat2(r.dz2[k, 0:hh]), r.back_here[...])
        v = dot(flat2(r.dz2[k, 1 : hh + 1]), r.back_below[...])
        s1, s2 = acc
        parts = (
            (1, 1, u[:, 0:LANES] + v[:, 0:LANES]),
            (0, 1, u[:, LANES : 2 * LANES]),
            (1, 0, u[:, 2 * LANES : 3 * LANES] + v[:, LANES : 2 * LANES]),
            (0, 0, u[:, 3 * LANES : 4 * LANES]),
        )
        for pr, pc, q in parts:
            q = q.reshape(hh, PAD, LANES) * r.s1[pr, pc, k]
            r.q1[pr, pc, k] = q
            r.dz1[pr, pc, k] = (m * q).astype(BF16)
            s1 += m * folded(q)
            s2 += m * folded(q * r.z1[pr, pc, k])
        return s1, s2

    d1, d2 = loop(thirteenth, zero8(LANES, 2))
    send_sums(10, [row_sum(d1), row_sum(d2)])
    advance(3, 1)
    advance(0, 3)
    advance(1, 2)
    part_q = sum(dot_tn(flat2(r.x[q]), flat2(r.dz1[q])) for q in planes)

    def skip_back(k, c):
        h3 = fs_[2] * col_mask
        for i in range(hh):
            r.dzs[k, i] = (r.q3[k, i] * fs_[0] + r.zs[k, i] * fs_[1] + h3).astype(BF16)
        r.skip_back[k] = dot_nt(flat2(r.dzs[k]), sc).reshape(hh, PAD, cfg.c_in)
        return c

    loop(skip_back)
    start_pieces(out_copies, *OUT_AT[4])
    advance(2, 2)
    db1, q1 = take_sums(10, [LANES] * 2)
    dg1 = gain_sum(n1, db1, q1)
    c1, c2, c3 = factors(n1, db1, dg1)

    total = n1.scale * part_q
    total += (c2 / n1.inv) * r.part_z[...] + (c3 + c2 * n1.mu) * r.part_m[...]
    one_send(total)
    one_spread()
    advance(3, 2)
    advance(0, 4)
    advance(1, 3)
    start_pieces(out_copies, *OUT_AT[5])

    def last(k, acc, c1=c1, c2=c2, c3=c3):
        m = r.mask_one[k]
        f1, f2, f3 = m * c1, m * c2, (m * c3) * col_mask
        for pr in range(2):
            for pc in range(2):
                d = (r.q1[pr, pc, k] * f1 + r.z1[pr, pc, k] * f2 + f3).astype(BF16)
                r.dz1[pr, pc, k] = d
        return acc

    loop(last)

    def images_back(k, c):
        for pr in range(2):
            for pc in range(2):
                g = dot_nt(flat2(r.dz1[pr, pc, k]), w1).reshape(hh, PAD, cfg.c_in)
                if pr == 0 and pc == 0:
                    g += r.skip_back[k]
                for i in range(hh):
                    for q in range(lane_blocks):
                        r.spread[q, 2 * i + pr, pl.ds(pc, PAD, stride=2), :] = g[
                            i, :, q * LANES : (q + 1) * LANES
                        ]
        for i in range(2 * hh):
            for q in range(lane_blocks):
                lanes = slice(q * LANES, (q + 1) * LANES)
                r.x_in[k, i, :, lanes] = r.spread[q, i, 0 : 2 * wv, :].astype(BF16)
        return c

    loop(images_back)
    back_copy = pltpu.make_async_copy(r.x_in, r.images_grad, r.local_sem.at[2])
    back_copy.start()

    for k, v in enumerate((dg1, dg2, dg4, dg5, db1, db2, db4, db5)):
        r.mid_held[k : k + 1, :] = v
    for k, v in enumerate((dg3, dgs, dg6, db3, db3, db6)):
        r.wide_held[k : k + 1, :] = v
    results = []

    def give(src, dst):
        copy = pltpu.make_async_copy(src, dst, r.full_sem.at[len(results)])
        copy.start()
        results.append(copy)

    give(r.mid_held, r.mid_grads)
    give(r.wide_held, r.wide_grads)

    def result(g):
        give(r.full[g], r.summed[g])

    advance(2, 3)
    advance(3, 3)
    one_gather()
    advance(0, 5)
    advance(1, 4)
    advance(2, 4)
    advance(3, 4)
    one_return()
    advance(0, 6)
    result(0)
    advance(1, 5)
    advance(2, 5)
    advance(3, 5)
    one_take()
    give(r.one_whole, r.summed_one)
    advance(1, 6)
    result(1)
    advance(2, 6)
    result(2)
    advance(3, 6)
    result(3)
    wait_pieces(1)
    out_local.wait()
    back_copy.wait()
    for copy in results:
        copy.wait()


def on_device(nr, nc, *args):
    (images, reduce_one, spatial_one, expand_one, shortcut, reduce_two, spatial_two, expand_two,
     mid_gain, mid_bias, wide_gain, wide_bias, widths, depth_gate, cot) = args
    nk, full_rows, full_cols, c_in = images.shape
    hh, wv, c_out = full_rows // 2, full_cols // 2, expand_one.shape[1]
    own = cot.shape[0]
    ndev, nxy, groups = nr * nc, nc // 2, len(GROUPS)
    sizes = [group_rows(g, ndev) for g in range(groups)]
    chunk = (ndev // 2, c_in // ndev, LANES)
    half, quad = (nk, hh, PAD), (2, 2, nk, hh, PAD)

    def f32(*shape):
        return pltpu.VMEM(shape, F32)

    def bf16(*shape):
        return pltpu.VMEM(shape, BF16)

    def dma(*shape):
        return pltpu.SemaphoreType.DMA(shape)

    def mid():
        return f32(*half, LANES)

    def wide():
        return f32(*half, c_out)

    def low(width):
        return bf16(*half, width)

    weights = dict(
        reduce_one=reduce_one, shortcut=shortcut, mid_gain=mid_gain, mid_bias=mid_bias,
        spatial_one=spatial_one.reshape(3, 3 * LANES, LANES), expand_one=expand_one,
        wide_gain=wide_gain, wide_bias=wide_bias, reduce_two=reduce_two,
        spatial_two=spatial_two.reshape(3, 3 * LANES, LANES), expand_two=expand_two,
    )
    scalars = dict(widths=widths.T, depth_gate=depth_gate)
    ins = dict(images=images, cot=cot, weights=weights)
    outs = dict(
        out=jax.ShapeDtypeStruct(cot.shape, BF16),
        images_grad=jax.ShapeDtypeStruct(images.shape, BF16),
        summed=[jax.ShapeDtypeStruct((size, LANES), BF16) for size in sizes[:4]],
        summed_one=jax.ShapeDtypeStruct((2,) + chunk, F32),
        mid_grads=jax.ShapeDtypeStruct((8, LANES), F32),
        wide_grads=jax.ShapeDtypeStruct((6, c_out), F32),
    )
    edges = [bf16(2 if i == 0 else 1, nk, PAD, LANES) for i in range(9)]
    levels = [(n, n // 2, n // nc, n // ndev) for n in sizes]
    halves = {i: ROUND_ROWS[i] // 2 for i in WIDE}
    scratch = dict(
        held={name: pltpu.VMEM(a.shape, a.dtype) for name, a in weights.items()},
        x_in=bf16(*images.shape), spread=f32(c_in // LANES, 2 * hh, 2 * PAD, LANES), x=bf16(*quad, c_in),
        z1=f32(*quad, LANES), s1=f32(*quad, LANES), q1=f32(*quad, LANES), dz1=bf16(*quad, LANES),
        part_z=f32(c_in, LANES), part_m=f32(c_in, LANES),
        one_both=f32(2, *chunk), one_came=f32(*chunk), one_half=f32(*chunk), one_slots=f32(*chunk),
        one_whole=f32(2, *chunk), slope_z=low(LANES),
        edge_a=bf16(nk, PAD, LANES), edge_t=f32(nk, PAD, LANES),
        expand_z=f32(LANES, c_out), expand_m=f32(LANES, LANES), skip_z=f32(c_in, c_out),
        skip_m=f32(c_in, LANES), mid_held=f32(8, LANES), wide_held=f32(6, c_out),
        pair_rows=f32(2, 4, LANES), pair_came=f32(4, LANES), pair_chips=f32(ndev // 2, 4, LANES),
        pair_total=f32(2, 4, LANES),
        even=low(3 * LANES), odd=bf16(nk, hh + 1, PAD, 3 * LANES), dz2=bf16(nk, hh + 1, PAD, 2 * LANES),
        a4=bf16(nk, hh + 2, PAD, 3 * LANES), dz5=bf16(nk, hh + 2, PAD, 3 * LANES),
        cot_rows=bf16(nk, hh, wv, c_out), out_rows=bf16(nk, hh, wv, c_out), skip_back=f32(*half, c_in),
        back_two=bf16(3, 3 * LANES, LANES), back_here=bf16(2 * LANES, 4 * LANES),
        back_below=bf16(2 * LANES, 2 * LANES),
        mask_one=f32(nk, 1, LANES), mask_two=f32(nk, 1, LANES), gates=f32(nk, 1, c_out),
        z2=mid(), s2=mid(), q2=mid(), z4=mid(), s4=mid(), q4=mid(), z5=mid(), s5=mid(), q5=mid(),
        z3=wide(), zs=wide(), s3=wide(), q3=wide(), z6=wide(), live=wide(),
        a2=low(LANES), a5=low(LANES), dz4=low(LANES),
        hidden=low(c_out), dz6=low(c_out), dz3=low(c_out), dzs=low(c_out),
        edge=edges, halo=edges,
        sums=[
            f32(ndev // 2 if i in WIDE else ndev, halves.get(i, n), LANES)
            for i, n in enumerate(ROUND_ROWS)
        ],
        both={i: f32(2, n, LANES) for i, n in halves.items()},
        totals={i: f32(2, n, LANES) for i, n in halves.items()},
        from_pair={i: f32(n, LANES) for i, n in halves.items()},
        part=[[pltpu.VMEM((n[i], LANES), t) for i in range(3)] for n, t in zip(levels, GROUP_TYPES)],
        came=[
            [pltpu.VMEM((m - 1, n[i + 1], LANES), t) for i, m in enumerate((2, nxy, nr))]
            for n, t in zip(levels, GROUP_TYPES)
        ],
        full=[pltpu.VMEM((n, LANES), t) for n, t in zip(sizes, GROUP_TYPES)],
        image_sem=dma(nk), local_sem=dma(3), full_sem=dma(groups + 3), weight_sem=dma(len(weights)),
        sum_send=pltpu.SemaphoreType.DMA, sum_recv=dma(len(ROUND_ROWS)), halo_send=dma(9), halo_recv=dma(9),
        row_send=dma(2), row_recv=dma(2), pair_send=dma(12), pair_recv=dma(12), chip_send=dma(3),
        chip_recv=dma(3), grad_send=dma(groups), grad_recv=dma(groups, 6),
    )
    cfg = SimpleNamespace(
        nr=nr, nc=nc, nk=nk, hh=hh, wv=wv, c_in=c_in, c_out=c_out, group_size=sizes,
        pieces=split(hh, 7), order=list(weights),
    )
    flat, trees = [], []
    for part in (scalars, ins, outs, scratch):
        leaves, tree = jax.tree.flatten(part)
        flat.append(leaves)
        trees.append(tree)

    def body(*refs):
        named, at = {}, 0
        for leaves, tree in zip(flat, trees):
            named.update(jax.tree.unflatten(tree, refs[at : at + len(leaves)]))
            at += len(leaves)
        mega(cfg, SimpleNamespace(**named, **named["held"]))

    smem, hbm = pl.BlockSpec(memory_space=pltpu.SMEM), pl.BlockSpec(memory_space=pl.ANY)
    result = pl.pallas_call(
        body,
        out_shape=flat[2],
        in_specs=[smem] * len(flat[0]) + [hbm] * len(flat[1]),
        out_specs=[hbm] * len(flat[2]),
        scratch_shapes=flat[3],
        compiler_params=pltpu.CompilerParams(
            collective_id=0, has_side_effects=True, vmem_limit_bytes=60 << 20
        ),
    )(*flat[0], *flat[1])
    made = SimpleNamespace(**jax.tree.unflatten(trees[2], result))
    parts = [made.out, made.images_grad, *made.summed, made.summed_one, made.mid_grads, made.wide_grads]
    return finished(parts, mid_gain.shape, wide_gain.shape)


WEIGHTS = (
    ("reduce_one", (256, 128)),
    ("spatial_one", (3, 3, 128, 128)),
    ("expand_one", (128, 512)),
    ("shortcut", (256, 512)),
    ("reduce_two", (512, 128)),
    ("spatial_two", (3, 3, 128, 128)),
    ("expand_two", (128, 512)),
)


def finish(*refs):
    n = len(GROUPS) + 4
    ins, outs, held = refs[:n], refs[n : n + 13], refs[n + 13 : 2 * n + 13]
    wide_to, (in_sem, out_sem) = refs[2 * n + 13 : 2 * n + 24], refs[2 * n + 24 :]
    chunks = [(0, i) for i in range(4)] + [(1, i) for i in range(4)]

    def part(ref, which, i):
        size = ref.shape[1 - which] // 4
        return ref.at[:, pl.ds(i * size, size)] if which == 0 else ref.at[pl.ds(i * size, size)]

    small = [pltpu.make_async_copy(ins[i], held[i], in_sem.at[i]) for i in (n - 2, n - 1, *range(2, n - 2))]
    large = [
        pltpu.make_async_copy(part(ins[w], w, i), part(held[w], w, i), in_sem.at[n + 4 * w + i])
        for w, i in chunks
    ]
    for copy in small + large:
        copy.start()
    leaving = []

    def leave(src, dst):
        copy = pltpu.make_async_copy(src, dst, out_sem.at[len(leaving)])
        copy.start()
        leaving.append(copy)

    for i in range(2):
        small[i].wait()
    mid, wide = held[n - 2], held[n - 1]
    grads = (mid[0:4, :], mid[4:8, :], wide[0:3, :], wide[3:6, :])
    for ref, value, to in zip(wide_to[7:], grads, outs[9:]):
        ref[...] = value
        leave(ref, to)
    names = [name for name, _ in WEIGHTS]
    for g, group in enumerate(GROUPS[:4]):
        small[2 + g].wait()
        summed = held[2 + g]
        at = 0
        for name, rows in group:
            rest = name not in names
            which = names.index("expand_two" if rest else name)
            ref = wide_to[which]
            if len(ref.shape) == 4:
                for i in range(9):
                    lo = at + i * LANES
                    ref[i // 3, i % 3] = summed[lo : lo + LANES, :].astype(F32)
            else:
                height = ref.shape[0]
                first = ref.shape[1] // LANES - 1 if rest else 0
                for q in range(rows // height):
                    lo, to = at + q * height, (first + q) * LANES
                    ref[:, to : to + LANES] = summed[lo : lo + height, :].astype(F32)
            if rest or name != "expand_two":
                leave(ref, outs[2 + which])
            at += rows
    small[n - 3].wait()
    wide_to[0][...] = held[n - 3][...].reshape(wide_to[0].shape)
    leave(wide_to[0], outs[2])
    for copy, (w, i) in zip(large, chunks):
        copy.wait()
        leave(part(held[w], w, i), part(outs[w], w, i))
    for copy in leaving:
        copy.wait()


def finished(parts, mid_shape, wide_shape):
    hbm = pl.BlockSpec(memory_space=pl.ANY)
    outs = [jax.ShapeDtypeStruct(p.shape, p.dtype) for p in parts[:2]]
    outs += [jax.ShapeDtypeStruct(s, F32) for _, s in WEIGHTS]
    outs += [jax.ShapeDtypeStruct(s, F32) for s in (mid_shape, mid_shape, wide_shape, wide_shape)]
    dma = pltpu.SemaphoreType.DMA
    return tuple(
        pl.pallas_call(
            finish,
            out_shape=outs,
            in_specs=[hbm] * len(parts),
            out_specs=[hbm] * 13,
            scratch_shapes=[pltpu.VMEM(p.shape, p.dtype) for p in parts]
            + [pltpu.VMEM(o.shape, o.dtype) for o in outs[2:]]
            + [dma((len(parts) + 8,)), dma((19,))],
            compiler_params=pltpu.CompilerParams(vmem_limit_bytes=60 << 20),
        )(*parts)
    )


def solution(mesh):
    nr, nc = mesh.shape["rows"], mesh.shape["crops"]
    whole = P()
    return jax.shard_map(
        functools.partial(on_device, nr, nc),
        mesh=mesh,
        in_specs=(P("crops", "rows", None, None),)
        + (whole,) * 11
        + (P("crops", None), P("crops"), P(("crops", "rows"), None, None, None)),
        out_specs=(P(("crops", "rows"), None, None, None), P("crops", "rows", None, None))
        + (whole,) * 11,
        check_vma=False,
    )
```

```python
import functools
from types import SimpleNamespace

import jax
import jax.numpy as jnp
from jax import lax
from jax.experimental import pallas as pl
from jax.experimental.pallas import tpu as pltpu
from jax.sharding import PartitionSpec as P

MESH = pl.DeviceIdType.MESH
F32 = jnp.float32
BF16 = jnp.bfloat16
epsilon = 1e-05
COT_AT = ((0,), (1,), (2, 3), (4,), (5, 6), ())
OUT_AT = ((0, 1), (2,), (3, 4), (5, 6), (), ())
PAD = 32
LANES = 128

ROUND_ROWS = (4, 2, 8, 2, 2, 10, 8, 2, 2, 14, 2)
WIDE = (2, 5, 6, 9)


GROUPS = (
    (("expand_two", 384), ("spatial_two", 1152)),
    (("reduce_two", 512),),
    (("expand_one", 512), ("shortcut", 1024)),
    (("spatial_one", 1152), ("expand_rest", 128)),
    (("slope", 128), ("slope_z", 128)),
)
GROUP_TYPES = (BF16, BF16, BF16, BF16, F32)


def group_rows(g, devices):
    group, unit = GROUPS[g], (16 if GROUP_TYPES[g] == BF16 else 8) * devices
    return -(-sum(rows for _, rows in group) // unit) * unit


def split(rows, parts):
    return [(i * rows // parts, (i + 1) * rows // parts) for i in range(parts)]


def dot(a, b):
    return lax.dot_general(a, b, (((1,), (0,)), ((), ())), preferred_element_type=F32)


def dot_nt(a, b):
    return lax.dot_general(a, b, (((1,), (1,)), ((), ())), preferred_element_type=F32)


def dot_tn(a, b):
    return lax.dot_general(a, b, (((0,), (0,)), ((), ())), preferred_element_type=F32)


def two_terms(x):
    high = x.astype(BF16)
    return high, (x - high.astype(F32)).astype(BF16)


def half_act(h):
    return h + h * jnp.tanh(h)


def half_silu(h, half_mask=0.5):
    t = jnp.tanh(h)
    p = h * t
    return h + p, (half_mask + half_mask * t) * (1.0 + (h - p))


def folded(x):
    return jnp.sum(x.reshape(-1, 8, x.shape[-1]), axis=0)


def row_sum(x):
    return jnp.sum(x, axis=0, keepdims=True)


def flat2(x):
    return x.reshape(-1, x.shape[-1])


def mega(cfg, r):
    nr, nc, nk, hh, wv = cfg.nr, cfg.nc, cfg.nk, cfg.hh, cfg.wv
    ndev, nxy, own = nr * nc, nc // 2, nk // nr
    m_half = hh * PAD
    row = lax.axis_index("rows")
    col = lax.axis_index("crops")
    xy, core = lax.div(col, 2), lax.rem(col, 2)
    me = row * nc + col

    barrier = pltpu.get_barrier_semaphore()

    def place(i):
        return (lax.div(i, nc), lax.rem(i, nc))

    def greet(k, c):
        pl.semaphore_signal(
            barrier, inc=1, device_id=place(lax.rem(me + k, ndev)), device_id_type=MESH
        )
        return c

    lax.fori_loop(1, ndev, greet, 0)

    image_copies = [
        pltpu.make_async_copy(r.images.at[k], r.x_in.at[k], r.image_sem.at[k]) for k in range(nk)
    ]
    weight_copies = {
        name: pltpu.make_async_copy(r.weights[name], r.held[name], r.weight_sem.at[i])
        for i, name in enumerate(cfg.order)
    }
    for i, copy in enumerate(weight_copies.values()):
        copy.start()
        if i == 0:
            for other in image_copies:
                other.start()

    def arrived(*names):
        for name in names:
            weight_copies[name].wait()

    lane = lax.broadcasted_iota(jnp.int32, (1, LANES), 1)
    for k in range(nk):
        gate = (jnp.full((1, LANES), r.depth_gate[k], jnp.int32) > 0).astype(F32)
        r.mask_one[k] = (lane < r.widths[0, k]).astype(F32)
        r.mask_two[k] = (lane < r.widths[1, k]).astype(F32) * gate
        r.gates[k] = jnp.concatenate([gate] * 4, axis=1)
    col_mask = (lax.broadcasted_iota(jnp.int32, (PAD, 1), 0) < wv).astype(F32)
    half_mask = 0.5 * col_mask

    chips = nr * nxy
    chip = row * nxy + xy

    def chip_copy(src, dst, to, send_sem, recv_sem):
        return pltpu.make_async_remote_copy(
            src_ref=src,
            dst_ref=dst,
            send_sem=send_sem,
            recv_sem=recv_sem,
            device_id=(lax.div(to, nxy), lax.rem(to, nxy) * 2 + core),
            device_id_type=MESH,
        )

    def to_chips(copy_to):
        def send(k, c):
            copy_to(lax.rem(chip + k, chips)).start()
            return c

        lax.fori_loop(1, chips, send, 0)

    def all_of(ref, n, sem):
        pltpu.make_async_copy(ref.at[pl.ds(0, n)], ref.at[pl.ds(0, n)], sem).wait()

    def to_all(copy_to):
        def send(k, c):
            copy_to(lax.rem(me + k, ndev)).start()
            return c

        lax.fori_loop(1, ndev, send, 0)

    def sum_copy(idx, p):
        mine = r.sums[idx].at[me]
        return pltpu.make_async_remote_copy(
            src_ref=mine,
            dst_ref=mine,
            send_sem=r.sum_send,
            recv_sem=r.sum_recv.at[idx],
            device_id=place(p),
            device_id_type=MESH,
        )

    def pair_copy(step, src, dst):
        return pltpu.make_async_remote_copy(
            src_ref=src,
            dst_ref=dst,
            send_sem=r.pair_send.at[step],
            recv_sem=r.pair_recv.at[step],
            device_id=(row, xy * 2 + 1 - core),
            device_id_type=MESH,
        )

    def lines(vectors):
        return [v[:, q * LANES : (q + 1) * LANES] for v in vectors for q in range(v.shape[1] // LANES)]

    def send_sums(idx, vectors):
        rows = lines(vectors)
        assert len(rows) == ROUND_ROWS[idx]
        slots = r.sums[idx]
        if idx in WIDE:
            half = len(rows) // 2
            both, came = r.both[idx], r.from_pair[idx]
            for at, v in enumerate(rows):
                both[at // half, at % half : at % half + 1, :] = v
            copy = pair_copy(WIDE.index(idx), both.at[1 - core], came)
            copy.start()
            copy.wait()
            slots[chip] = both[core] + came[...]
        else:
            for at, v in enumerate(rows):
                slots[me, at : at + 1, :] = v
        if idx in WIDE:
            mine = slots.at[chip]
            to_chips(lambda to: chip_copy(mine, mine, to, r.sum_send, r.sum_recv.at[idx]))
        else:
            to_all(lambda p: sum_copy(idx, p))

    def take_sums(idx, widths):
        slots = r.sums[idx]
        others = slots.shape[0] - 1
        all_of(slots, others, r.sum_recv.at[idx])
        if idx in WIDE:
            totals = r.totals[idx]
            totals[core] = jnp.sum(slots[...], axis=0)
            mine = totals.at[core]
            copy = pair_copy(4 + WIDE.index(idx), mine, mine)
            copy.start()
            copy.wait()
            half = ROUND_ROWS[idx] // 2
            rows = [totals[at // half, at % half : at % half + 1, :] for at in range(2 * half)]
        else:
            total = jnp.sum(slots[...], axis=0)
            rows = [total[at : at + 1, :] for at in range(ROUND_ROWS[idx])]
        all_of(slots, others, r.sum_send)
        result, at = [], 0
        for w in widths:
            parts = rows[at : at + w // LANES]
            at += w // LANES
            result.append(jnp.concatenate(parts, axis=1) if len(parts) > 1 else parts[0])
        return result

    up_ok, down_ok = row > 0, row < nr - 1
    halo_up = (False, False, True, False, True, False, True, True, True)

    def halo(idx):
        return pltpu.make_async_remote_copy(
            src_ref=r.edge[idx],
            dst_ref=r.halo[idx],
            send_sem=r.halo_send.at[idx],
            recv_sem=r.halo_recv.at[idx],
            device_id=(row - 1 if halo_up[idx] else row + 1, col),
            device_id_type=MESH,
        )

    def halo_put(idx, at, rows):
        r.edge[idx][at] = rows.astype(BF16)

    def halo_start(idx):
        @pl.when(up_ok if halo_up[idx] else down_ok)
        def _():
            halo(idx).start()

    def halo_wait(idx):
        @pl.when(up_ok if halo_up[idx] else down_ok)
        def _():
            halo(idx).wait_send()

        @pl.when(down_ok if halo_up[idx] else up_ok)
        def _():
            halo(idx).wait_recv()

    def halo_row(idx, at, k):
        return r.halo[idx][at, k].astype(F32)

    def both_edges(idx, ref):
        halo_put(idx, 0, ref[:, hh - 1])
        halo_put(idx + 1, 0, ref[:, 0])

    def skip_send(vectors):
        for at, v in enumerate(lines(vectors)):
            r.pair_rows[at // 4, at % 4 : at % 4 + 1, :] = v
        pair_copy(8, r.pair_rows.at[1 - core], r.pair_came).start()

    def skip_spread():
        pair_copy(8, r.pair_rows.at[1 - core], r.pair_came).wait()
        r.pair_chips[chip] = r.pair_rows[core] + r.pair_came[...]
        mine = r.pair_chips.at[chip]
        to_chips(lambda to: chip_copy(mine, mine, to, r.chip_send.at[0], r.chip_recv.at[0]))

    def skip_return():
        all_of(r.pair_chips, chips - 1, r.chip_recv.at[0])
        all_of(r.pair_chips, chips - 1, r.chip_send.at[0])
        r.pair_total[core] = jnp.sum(r.pair_chips[...], axis=0)
        mine = r.pair_total.at[core]
        pair_copy(9, mine, mine).start()

    def skip_take():
        mine = r.pair_total.at[core]
        pair_copy(9, mine, mine).wait()
        return [
            jnp.concatenate([r.pair_total[i, q : q + 1, :] for q in range(4)], axis=1)
            for i in range(2)
        ]

    axes = (("core", 2), ("xy", nxy), ("rows", nr))
    seat = {"core": core, "xy": xy, "rows": row}

    def device_of(kind, i):
        if kind == "core":
            return (row, xy * 2 + i)
        if kind == "xy":
            return (row, i * 2 + core)
        return (i, col)

    def level_rows(g, level):
        size = cfg.group_size[g]
        for _, n in axes[:level]:
            size //= n
        return size

    def offset(g, level):
        at = 0
        for i, (kind, _) in enumerate(axes[:level]):
            at = at + seat[kind] * level_rows(g, i + 1)
        return pl.multiple_of(at, 8) if level else 0

    def scatter_send(g, level):
        kind, n = axes[level]
        chunk = level_rows(g, level + 1)
        for k in range(1, n):
            p = lax.rem(seat[kind] + k, n)
            pltpu.make_async_remote_copy(
                src_ref=r.part[g][level].at[pl.ds(pl.multiple_of(p * chunk, 8), chunk)],
                dst_ref=r.came[g][level].at[k - 1],
                send_sem=r.grad_send.at[g],
                recv_sem=r.grad_recv.at[g, level],
                device_id=device_of(kind, p),
                device_id_type=MESH,
            ).start()

    def scatter_take(g, level):
        kind, n = axes[level]
        chunk = level_rows(g, level + 1)
        came = r.came[g][level]
        pltpu.make_async_copy(came, came, r.grad_recv.at[g, level]).wait()
        mine = pl.ds(pl.multiple_of(seat[kind] * chunk, 8), chunk)
        total = r.part[g][level][mine, :].astype(F32) + jnp.sum(came[...].astype(F32), axis=0)
        pltpu.make_async_copy(came, came, r.grad_send.at[g]).wait()
        if level + 1 < len(axes):
            r.part[g][level + 1][...] = total.astype(GROUP_TYPES[g])
        else:
            r.full[g][pl.ds(offset(g, 3), chunk), :] = total.astype(GROUP_TYPES[g])

    def gather_send(g, level):
        kind, n = axes[level]
        size = level_rows(g, level + 1)
        region = r.full[g].at[pl.ds(offset(g, level + 1), size)]
        for k in range(1, n):
            p = lax.rem(seat[kind] + k, n)
            pltpu.make_async_remote_copy(
                src_ref=region,
                dst_ref=region,
                send_sem=r.grad_send.at[g],
                recv_sem=r.grad_recv.at[g, 3 + level],
                device_id=device_of(kind, p),
                device_id_type=MESH,
            ).start()

    def gather_take(g, level):
        n = axes[level][1]
        size = level_rows(g, level + 1) * (n - 1)
        bytes_of = r.full[g].at[pl.ds(0, size)]
        pltpu.make_async_copy(bytes_of, bytes_of, r.grad_recv.at[g, 3 + level]).wait()
        pltpu.make_async_copy(bytes_of, bytes_of, r.grad_send.at[g]).wait()

    steps = (
        (scatter_send, 0), (scatter_take, 0), (scatter_send, 1), (scatter_take, 1),
        (scatter_send, 2), (scatter_take, 2), (gather_send, 2), (gather_take, 2),
        (gather_send, 1), (gather_take, 1), (gather_send, 0), (gather_take, 0),
    )

    def advance(g, phase):
        for fn, level in steps[max(0, 2 * phase - 1) : 2 * phase + 1]:
            fn(g, level)

    def stage(g, name, value):
        at = 0
        for other, rows in GROUPS[g]:
            if other == name:
                break
            at += rows
        blocks = value.shape[1] // LANES
        for q in range(blocks):
            n = value.shape[0]
            lo = at + q * n
            r.part[g][0][lo : lo + n, :] = value[:, q * LANES : (q + 1) * LANES].astype(GROUP_TYPES[g])

    def one_send(value):
        r.one_both[...] = value.reshape(2, chips, -1, LANES)
        pair_copy(10, r.one_both.at[1 - core], r.one_came).start()

    def one_spread():
        pair_copy(10, r.one_both.at[1 - core], r.one_came).wait()
        half, slots = r.one_half, r.one_slots
        half[...] = r.one_both[core] + r.one_came[...]
        sems = (r.chip_send.at[1], r.chip_recv.at[1])
        to_chips(lambda to: chip_copy(half.at[to], slots.at[chip], to, *sems))

    def one_gather():
        slots = r.one_slots
        all_of(slots, chips - 1, r.chip_recv.at[1])
        slots[chip] = r.one_half[chip]
        r.one_whole[core, chip] = jnp.sum(slots[...], axis=0)
        mine = r.one_whole.at[core, chip]
        sems = (r.chip_send.at[2], r.chip_recv.at[2])
        to_chips(lambda to: chip_copy(mine, mine, to, *sems))

    def one_return():
        slots = r.one_slots
        all_of(slots, chips - 1, r.chip_send.at[1])
        all_of(slots, chips - 1, r.chip_recv.at[2])
        all_of(slots, chips - 1, r.chip_send.at[2])
        mine = r.one_whole.at[core]
        pair_copy(11, mine, mine).start()

    def one_take():
        mine = r.one_whole.at[core]
        pair_copy(11, mine, mine).wait()

    def coefficients(total, square, count, gain, bias):
        n = jnp.maximum(count, 1.0)
        mu = total / n
        inv = lax.rsqrt(square / n - mu * mu + epsilon)
        scale = gain * inv
        return SimpleNamespace(n=n, mu=mu, inv=inv, scale=scale, shift=bias - mu * scale)

    def factors(norm, dbias, dgain):
        c2 = -norm.scale * norm.inv * dgain / norm.n
        c3 = -norm.scale * dbias / norm.n - c2 * norm.mu
        return norm.scale, c2, c3

    def gain_sum(norm, total, z_total):
        return norm.inv * (z_total - norm.mu * total)

    def slope_sums(mask, slope, z, a, norm):
        def scaled(k, c):
            t = mask[k] * slope[k]
            r.dz4[k] = t.astype(BF16)
            r.slope_z[k] = (t * ((z[k] - norm.mu) * norm.inv)).astype(BF16)
            return c

        loop(scaled)
        flat_a = flat2(a[...])
        stage(4, "slope", dot_tn(flat_a, flat2(r.dz4[...])))
        stage(4, "slope_z", dot_tn(flat_a, flat2(r.slope_z[...])))

    def through(weight, c2, c3):
        high, low = two_terms(weight.astype(F32) * c2)
        b = dot_nt(high, weight) + dot_nt(low, weight)
        v = sum(dot_nt(jnp.broadcast_to(c, (16, c.shape[1])), weight) for c in two_terms(c3))
        return b, v[0:1]

    def chained(norm, u_sum, uz_sum, t_sum, tz_sum, b, v):
        k1, k2 = r.full[4][0:LANES, :], r.full[4][LANES : 2 * LANES, :]
        dbias = u_sum + row_sum(k1 * b) + t_sum * v
        dgain = gain_sum(norm, u_sum, uz_sum) + row_sum(k2 * b) + gain_sum(norm, t_sum, tz_sum) * v
        return dbias, dgain

    def loop(body, init=0):
        for k in range(nk):
            init = body(k, init)
        return init

    def zero8(width, count):
        return tuple(jnp.zeros((8, width), F32) for _ in range(count))

    def row_pieces(src_of, dst_of, send, recv, local):
        pieces = []
        for w, (lo, hi) in enumerate(cfg.pieces):
            for k in range(1, nr):
                p = lax.rem(row + k, nr)
                pieces.append(
                    pltpu.make_async_remote_copy(
                        src_ref=src_of(p, lo, hi - lo),
                        dst_ref=dst_of(lo, hi - lo),
                        send_sem=send,
                        recv_sem=recv,
                        device_id=(p, col),
                        device_id_type=MESH,
                    )
                )
        here = pltpu.make_async_copy(src_of(row, 0, hh), dst_of(0, hh), local)
        return pieces, here

    def wait_pieces(which):
        bytes_of = r.out_rows.at[pl.ds(0, nk - own)]
        pltpu.make_async_copy(bytes_of, bytes_of, r.row_recv.at[which]).wait()
        pltpu.make_async_copy(bytes_of, bytes_of, r.row_send.at[which]).wait()

    def start_pieces(pieces, *which):
        for w in which:
            for copy in pieces[w * (nr - 1) : (w + 1) * (nr - 1)]:
                copy.start()

    cot_copies, cot_local = row_pieces(
        lambda p, lo, n: r.cot.at[:, pl.ds(p * hh + lo, n)],
        lambda lo, n: r.cot_rows.at[pl.ds(row * own, own), pl.ds(lo, n)],
        r.row_send.at[0], r.row_recv.at[0], r.local_sem.at[0],
    )
    out_copies, out_local = row_pieces(
        lambda p, lo, n: r.out_rows.at[pl.ds(p * own, own), pl.ds(lo, n)],
        lambda lo, n: r.out.at[:, pl.ds(row * hh + lo, n)],
        r.row_send.at[1], r.row_recv.at[1], r.local_sem.at[1],
    )
    cot_local.start()

    lane_blocks = cfg.c_in // LANES
    for slot in range(2 * hh):
        for q in range(lane_blocks):
            r.spread[q, slot, 2 * wv : 2 * PAD, :] = jnp.zeros((2 * PAD - 2 * wv, LANES), F32)
    arrived("reduce_one")
    w1 = r.reduce_one[...]
    acc = zero8(LANES, 2)
    for copy in image_copies:
        copy.wait()

    def first(k, acc):
        for i in range(2 * hh):
            for q in range(lane_blocks):
                lanes = slice(q * LANES, (q + 1) * LANES)
                r.spread[q, i, 0 : 2 * wv, :] = r.x_in[k, i, :, lanes].astype(F32)
        m = r.mask_one[k]
        s1, s2 = acc
        for pr in range(2):
            for pc in range(2):
                for i in range(hh):
                    for q in range(lane_blocks):
                        lanes = slice(q * LANES, (q + 1) * LANES)
                        r.x[pr, pc, k, i, :, lanes] = r.spread[
                            q, 2 * i + pr, pl.ds(pc, PAD, stride=2), :
                        ].astype(BF16)
                z = dot(flat2(r.x[pr, pc, k]), w1)
                r.z1[pr, pc, k] = z.reshape(hh, PAD, LANES)
                s1 += m * folded(z)
                s2 += m * folded(z * z)
        return s1, s2

    s1, s2 = loop(first, acc)
    count_one = sum(r.mask_one[k] for k in range(nk))
    count_two = sum(r.mask_two[k] for k in range(nk))
    arrived("shortcut")
    sc = r.shortcut[...]

    def skip(k, acc):
        z = dot(flat2(r.x[0, 0, k]), sc)
        r.zs[k] = z.reshape(hh, PAD, cfg.c_out)
        return acc[0] + folded(z), acc[1] + folded(z * z)

    zs1, zs2 = loop(skip, zero8(cfg.c_out, 2))
    for pc in range(2):
        halo_put(0, pc, r.z1[1, pc, :, hh - 1])
    pl.semaphore_wait(barrier, ndev - 1)
    send_sums(0, [row_sum(s1), row_sum(s2), count_one, count_two])
    halo_start(0)
    skip_send([row_sum(zs1), row_sum(zs2)])
    arrived("mid_gain", "mid_bias", "spatial_one")
    arrived("spatial_two", "expand_two")
    def tap(ref, i, j):
        return ref[i, j * LANES : (j + 1) * LANES, :].T

    for i in range(3):
        for j in range(3):
            r.back_two[i, j * LANES : (j + 1) * LANES, :] = tap(r.spatial_two, 2 - i, 2 - j)
    zeros = jnp.zeros((LANES, LANES), BF16)
    k1 = r.spatial_one
    here = [[tap(k1, 2, 2), tap(k1, 1, 2), tap(k1, 2, 1), tap(k1, 1, 1)],
            [tap(k1, 2, 0), tap(k1, 1, 0), zeros, zeros]]
    below = [[tap(k1, 0, 2), tap(k1, 0, 1)], [tap(k1, 0, 0), zeros]]
    for ref, blocks in ((r.back_here, here), (r.back_below, below)):
        for i, line in enumerate(blocks):
            for j, block in enumerate(line):
                ref[i * LANES : (i + 1) * LANES, j * LANES : (j + 1) * LANES] = block

    for k in range(nk):
        r.dz4[k] = jnp.broadcast_to(r.mask_one[k], (hh, PAD, LANES)).astype(BF16)
    planes = [(pr, pc) for pr in range(2) for pc in range(2)]
    r.part_m[...] = sum(dot_tn(flat2(r.x[q]), flat2(r.dz4[...])) for q in planes)
    start_pieces(cot_copies, *COT_AT[0])
    t1, t2, active_one, active_two = take_sums(0, [LANES] * 4)
    half_px, full_px = float(hh * wv), float(4 * hh * wv)
    active_gate = active_two[:, 0:1]
    g1, b1 = r.mid_gain[0:1, :], r.mid_bias[0:1, :]
    n1 = coefficients(t1, t2, active_one * full_px, g1, b1)
    halo_wait(0)

    def shifted_right(a):
        return pltpu.roll(a, 1, axis=a.ndim - 2)

    def shifted_left(a):
        return pltpu.roll(a, PAD - 1, axis=a.ndim - 2)

    def affine(norm, m):
        return 0.5 * m * norm.scale, (0.5 * m * norm.shift) * col_mask

    k_one = [r.spatial_one[i] for i in range(3)]

    def second(k, acc):
        m = r.mask_one[k]
        ah, bh = affine(n1, m)
        for pr in range(2):
            for pc in range(2):
                a = half_act(r.z1[pr, pc, k] * ah + bh)
                dst = r.even if pr == 0 else r.odd
                rows = pl.ds(0, hh) if pr == 0 else pl.ds(1, hh)
                if pc == 0:
                    dst[k, rows, :, LANES : 2 * LANES] = a.astype(BF16)
                else:
                    dst[k, rows, :, 2 * LANES : 3 * LANES] = a.astype(BF16)
                    dst[k, rows, :, 0:LANES] = shifted_right(a).astype(BF16)
        for pc in range(2):
            a = half_act(halo_row(0, pc, k) * ah + bh)
            a = jnp.where(row > 0, a, 0.0)
            if pc == 0:
                r.odd[k, 0, :, LANES : 2 * LANES] = a.astype(BF16)
            else:
                r.odd[k, 0, :, 2 * LANES : 3 * LANES] = a.astype(BF16)
                r.odd[k, 0, :, 0:LANES] = shifted_right(a).astype(BF16)
        z = dot(flat2(r.even[k]), k_one[1])
        z += dot(flat2(r.odd[k, 1 : hh + 1]), k_one[2])
        z += dot(flat2(r.odd[k, 0:hh]), k_one[0])
        z = z.reshape(hh, PAD, LANES) * col_mask
        r.z2[k] = z
        return acc[0] + m * folded(z), acc[1] + m * folded(z * z)

    s1, s2 = loop(second, zero8(LANES, 2))
    send_sums(1, [row_sum(s1), row_sum(s2)])
    skip_spread()

    def early(k, c):
        m = r.mask_one[k]
        ah, bh = affine(n1, m)
        for pr in range(2):
            for pc in range(2):
                zhat = (r.z1[pr, pc, k] - n1.mu) * (m * n1.inv)
                r.dz1[pr, pc, k] = zhat.astype(BF16)
                _, r.s1[pr, pc, k] = half_silu(r.z1[pr, pc, k] * ah + bh, half_mask)
        return c

    loop(early)
    for name in ("expand_one", "wide_gain", "wide_bias", "reduce_two"):
        arrived(name)
    r.part_z[...] = sum(dot_tn(flat2(r.x[q]), flat2(r.dz1[q])) for q in planes)
    start_pieces(cot_copies, *COT_AT[1])
    t1, t2 = take_sums(1, [LANES] * 2)
    n2 = coefficients(t1, t2, active_one * half_px, r.mid_gain[1:2, :], r.mid_bias[1:2, :])
    e1 = r.expand_one[...]

    def third(k, acc):
        ah, bh = affine(n2, r.mask_one[k])
        a, s = half_silu(r.z2[k] * ah + bh, half_mask)
        r.s2[k] = s
        a = a.astype(BF16)
        r.a2[k] = a
        z = dot(flat2(a), e1)
        r.z3[k] = z.reshape(hh, PAD, cfg.c_out)
        t = r.mask_one[k] * s
        return (
            acc[0] + folded(z), acc[1] + folded(z * z), acc[2] + folded(t), acc[3] + folded(t * r.z2[k])
        )

    s1, s2, t2_sum, t2z_sum = loop(third, zero8(cfg.c_out, 2) + zero8(LANES, 2))
    send_sums(2, [row_sum(s1), row_sum(s2)])
    slope_sums(r.mask_one, r.s2, r.z2, r.a2, n2)
    advance(4, 0)
    skip_return()
    start_pieces(cot_copies, *COT_AT[2])
    t1, t2 = take_sums(2, [cfg.c_out] * 2)
    ts1, ts2 = skip_take()
    all_px = float(nk * nc) * float(nr) * half_px
    n3 = coefficients(t1, t2, all_px, r.wide_gain[0:1, :], r.wide_bias[0:1, :])
    ns = coefficients(ts1, ts2, all_px, r.wide_gain[1:2, :], r.wide_bias[1:2, :])
    w2 = r.reduce_two[...]

    a3, as_ = 0.5 * n3.scale, 0.5 * ns.scale
    b3 = (0.5 * (n3.shift + ns.shift)) * col_mask

    def fourth(k, acc):
        for i in range(hh):
            h = r.z3[k, i] * a3 + r.zs[k, i] * as_ + b3
            r.hidden[k, i] = half_act(h).astype(BF16)
        z = dot(flat2(r.hidden[k]), w2)
        r.z4[k] = z.reshape(hh, PAD, LANES)
        m = r.mask_two[k]
        return acc[0] + m * folded(z), acc[1] + m * folded(z * z)

    s1, s2 = loop(fourth, zero8(LANES, 2))
    send_sums(3, [row_sum(s1), row_sum(s2)])
    both_edges(1, r.z4)
    halo_start(1)
    halo_start(2)

    def hats(k, c):
        for i in range(hh):
            r.dz3[k, i] = ((r.z3[k, i] - n3.mu) * n3.inv).astype(BF16)
            r.dzs[k, i] = ((r.zs[k, i] - ns.mu) * ns.inv).astype(BF16)
            _, r.s3[k, i] = half_silu(r.z3[k, i] * a3 + r.zs[k, i] * as_ + b3, half_mask)
        return c

    advance(4, 1)
    loop(hats)
    ones = jnp.ones((nk * m_half, LANES), BF16)
    r.expand_z[...] = dot_tn(flat2(r.a2[...]), flat2(r.dz3[...]))
    r.expand_m[...] = dot_tn(flat2(r.a2[...]), ones)
    r.skip_z[...] = dot_tn(flat2(r.x[0, 0]), flat2(r.dzs[...]))
    r.skip_m[...] = dot_tn(flat2(r.x[0, 0]), ones)
    start_pieces(cot_copies, *COT_AT[3])
    t1, t2 = take_sums(3, [LANES] * 2)
    n4 = coefficients(t1, t2, active_two * half_px, r.mid_gain[2:3, :], r.mid_bias[2:3, :])
    halo_wait(1)
    halo_wait(2)

    def put3(dst, k, rows, a):
        dst[k, rows, :, LANES : 2 * LANES] = a.astype(BF16)
        dst[k, rows, :, 0:LANES] = shifted_right(a).astype(BF16)
        dst[k, rows, :, 2 * LANES : 3 * LANES] = shifted_left(a).astype(BF16)

    k_two = [r.spatial_two[i] for i in range(3)]

    def fifth(k, acc):
        m = r.mask_two[k]
        ah, bh = affine(n4, m)
        put3(r.a4, k, pl.ds(1, hh), half_act(r.z4[k] * ah + bh))
        a = half_act(halo_row(1, 0, k) * ah + bh)
        put3(r.a4, k, 0, jnp.where(row > 0, a, 0.0))
        a = half_act(halo_row(2, 0, k) * ah + bh)
        put3(r.a4, k, hh + 1, jnp.where(row < nr - 1, a, 0.0))
        z = sum(dot(flat2(r.a4[k, i : i + hh]), k_two[i]) for i in range(3))
        z = z.reshape(hh, PAD, LANES) * col_mask
        r.z5[k] = z
        return acc[0] + m * folded(z), acc[1] + m * folded(z * z)

    s1, s2 = loop(fifth, zero8(LANES, 2))
    send_sums(4, [row_sum(s1), row_sum(s2)])
    advance(4, 2)
    start_pieces(cot_copies, *COT_AT[4])

    def slope_four(k, c):
        ah, bh = affine(n4, r.mask_two[k])
        _, r.s4[k] = half_silu(r.z4[k] * ah + bh, half_mask)
        return c

    loop(slope_four)
    t1, t2 = take_sums(4, [LANES] * 2)
    n5 = coefficients(t1, t2, active_two * half_px, r.mid_gain[3:4, :], r.mid_bias[3:4, :])
    e2 = r.expand_two[...]

    def sixth(k, acc):
        ah, bh = affine(n5, r.mask_two[k])
        a = half_act(r.z5[k] * ah + bh).astype(BF16)
        r.a5[k] = a
        z = dot(flat2(a), e2)
        r.z6[k] = z.reshape(hh, PAD, cfg.c_out)
        g = r.gates[k]
        return acc[0] + g * folded(z), acc[1] + g * folded(z * z)

    s1, s2 = loop(sixth, zero8(cfg.c_out, 2))
    send_sums(5, [row_sum(v) for v in (s1, s2, t2_sum, t2z_sum)])
    start_pieces(cot_copies, *COT_AT[5])

    def slope_five(k, c):
        ah, bh = affine(n5, r.mask_two[k])
        _, r.s5[k] = half_silu(r.z5[k] * ah + bh, half_mask)
        return c

    loop(slope_five)
    both_edges(3, r.z5)
    halo_start(3)
    halo_start(4)
    advance(4, 3)
    wait_pieces(0)
    cot_local.wait()
    t1, t2, t2_sum, t2z_sum = take_sums(5, [cfg.c_out] * 2 + [LANES] * 2)
    gate_count = active_gate * half_px
    n6 = coefficients(t1, t2, gate_count, r.wide_gain[2:3, :], r.wide_bias[2:3, :])
    pad_rows = jnp.zeros((PAD - wv, cfg.c_out), F32)

    def cot_row(k, i):
        return jnp.concatenate([r.cot_rows[k, i].astype(F32), pad_rows], axis=0)

    def half_pre_two(k, i):
        g = 0.5 * r.gates[k]
        return 0.5 * r.hidden[k, i].astype(F32) + (r.z6[k, i] * (g * n6.scale) + (g * n6.shift) * col_mask)

    def seventh(k, acc):
        g = r.gates[k]
        d1, d2 = acc
        for i in range(hh):
            _, s = half_silu(half_pre_two(k, i))
            live = g * cot_row(k, i) * s
            r.live[k, i] = live
            d1 += folded(live)
            d2 += folded(live * r.z6[k, i])
        return d1, d2

    sums = loop(seventh, zero8(cfg.c_out, 2))
    send_sums(6, [row_sum(v) for v in sums])

    advance(4, 4)

    def results(k, c):
        for i in range(hh):
            hid = r.hidden[k, i].astype(F32)
            a = half_act(half_pre_two(k, i))
            r.out_rows[k, i] = jnp.where(r.gates[k] > 0.0, a, hid)[:wv].astype(BF16)
        return c

    loop(results)
    start_pieces(out_copies, *OUT_AT[0])
    out_local.start()
    db6, q6 = take_sums(6, [cfg.c_out] * 2)
    dg6 = gain_sum(n6, db6, q6)
    c1, c2, c3 = factors(n6, db6, dg6)

    def eighth(k, acc, c1=c1, c2=c2, c3=c3):
        g = r.gates[k]
        f1, f2, f3 = g * c1, g * c2, (g * c3) * col_mask
        for i in range(hh):
            r.dz6[k, i] = (r.live[k, i] * f1 + r.z6[k, i] * f2 + f3).astype(BF16)
        q = dot_nt(flat2(r.dz6[k]), e2).reshape(hh, PAD, LANES) * r.s5[k]
        r.q5[k] = q
        m = r.mask_two[k]
        return acc[0] + m * folded(q), acc[1] + m * folded(q * r.z5[k])

    d1, d2 = loop(eighth, zero8(LANES, 2))
    send_sums(7, [row_sum(d1), row_sum(d2)])
    both_edges(5, r.q5)
    halo_start(5)
    halo_start(6)
    def passed_by(k, c):
        for i in range(hh):
            r.live[k, i] = (1.0 - r.gates[k]) * cot_row(k, i) + r.live[k, i]
        return c

    loop(passed_by)
    expand_grad = dot_tn(flat2(r.a5[...]), flat2(r.dz6[...]))
    stage(0, "expand_two", expand_grad[:, : 3 * LANES])
    stage(3, "expand_rest", expand_grad[:, 3 * LANES :])
    halo_wait(3)
    halo_wait(4)
    advance(4, 5)
    start_pieces(out_copies, *OUT_AT[1])
    db5, q5 = take_sums(7, [LANES] * 2)
    dg5 = gain_sum(n5, db5, q5)
    c1, c2, c3 = factors(n5, db5, dg5)
    halo_wait(5)
    halo_wait(6)

    def ninth(k, acc, c1=c1, c2=c2, c3=c3):
        m = r.mask_two[k]
        f1, f2, f3 = m * c1, m * c2, (m * c3) * col_mask
        put3(r.dz5, k, pl.ds(1, hh), r.q5[k] * f1 + r.z5[k] * f2 + f3)
        d = halo_row(5, 0, k) * f1 + halo_row(3, 0, k) * f2 + f3
        put3(r.dz5, k, 0, jnp.where(row > 0, d, 0.0))
        d = halo_row(6, 0, k) * f1 + halo_row(4, 0, k) * f2 + f3
        put3(r.dz5, k, hh + 1, jnp.where(row < nr - 1, d, 0.0))
        q = sum(dot(flat2(r.dz5[k, i : i + hh]), r.back_two[i]) for i in range(3))
        q = q.reshape(hh, PAD, LANES) * r.s4[k]
        r.q4[k] = q
        return acc[0] + m * folded(q), acc[1] + m * folded(q * r.z4[k])

    d1, d2 = loop(ninth, zero8(LANES, 2))
    send_sums(8, [row_sum(d1), row_sum(d2)])
    halo_put(8, 0, r.z2[:, 0])
    halo_start(8)

    d5 = flat2(r.dz5[:, 1 : hh + 1, :, LANES : 2 * LANES])
    stage(
        0,
        "spatial_two",
        jnp.concatenate([dot_tn(flat2(r.a4[:, i : i + hh]), d5) for i in range(3)], axis=0),
    )
    advance(4, 6)
    advance(0, 0)
    start_pieces(out_copies, *OUT_AT[2])
    db4, q4 = take_sums(8, [LANES] * 2)
    advance(0, 1)
    dg4 = gain_sum(n4, db4, q4)
    c1, c2, c3 = factors(n4, db4, dg4)

    def tenth(k, acc, c1=c1, c2=c2, c3=c3):
        m = r.mask_two[k]
        f1, f2, f3 = m * c1, m * c2, (m * c3) * col_mask
        r.dz4[k] = (r.q4[k] * f1 + r.z4[k] * f2 + f3).astype(BF16)
        back = dot_nt(flat2(r.dz4[k]), w2).reshape(hh, PAD, cfg.c_out)
        e1_, e2_, e3_, u1, u2 = acc
        for i in range(hh):
            d = back[i] + r.live[k, i]
            q = d.astype(BF16).astype(F32) * r.s3[k, i]
            r.q3[k, i] = q
            r.dz3[k, i] = (q * n3.scale).astype(BF16)
            e1_ += folded(q)
            e2_ += folded(q * r.z3[k, i])
            e3_ += folded(q * r.zs[k, i])
        u = dot_nt(flat2(r.dz3[k]), e1).reshape(hh, PAD, LANES)
        r.q2[k] = u
        ut = (r.mask_one[k] * u) * r.s2[k]
        return e1_, e2_, e3_, u1 + folded(ut), u2 + folded(ut * r.z2[k])

    sums = loop(tenth, zero8(cfg.c_out, 3) + zero8(LANES, 2))
    send_sums(9, [row_sum(v) for v in sums])
    halo_put(7, 0, r.q2[:, 0])
    halo_start(7)
    stage(1, "reduce_two", dot_tn(flat2(r.hidden[...]), flat2(r.dz4[...])))
    advance(1, 0)
    expand_q = dot_tn(flat2(r.a2[...]), flat2(r.dz3[...]))
    skip_q = dot_tn(flat2(r.x[0, 0]), flat2(r.dz3[...]))
    halo_wait(8)

    def edge_slope(k, c):
        ah, bh = affine(n2, r.mask_one[k])
        a, t = half_silu(halo_row(8, 0, k) * ah + bh, half_mask)
        r.edge_a[k] = a.astype(BF16)
        r.edge_t[k] = t
        return c

    loop(edge_slope)
    advance(1, 1)
    advance(0, 2)
    start_pieces(out_copies, *OUT_AT[3])
    db3, q3, qs, u_sum, uz_sum = take_sums(9, [cfg.c_out] * 3 + [LANES] * 2)
    dg3, dgs = gain_sum(n3, db3, q3), gain_sum(ns, db3, qs)
    f3_, fs_ = factors(n3, db3, dg3), factors(ns, db3, dgs)
    b, v2 = through(e1, *f3_[1:])
    db2, dg2 = chained(n2, u_sum, uz_sum, t2_sum, t2z_sum, b, v2)
    c1, c2, c3 = factors(n2, db2, dg2)
    b2 = two_terms(b)

    def four(x):
        return jnp.concatenate([x] * (cfg.c_out // LANES), axis=1)

    def by_parts(q_part, z_part, m_part, norm, fs):
        total = q_part + (fs[1] / norm.inv) * z_part[...]
        return total + (fs[2] + fs[1] * norm.mu) * four(m_part[...])

    stage(2, "expand_one", by_parts(expand_q, r.expand_z, r.expand_m, n3, f3_))
    stage(2, "shortcut", by_parts(skip_q * (ns.scale / n3.scale), r.skip_z, r.skip_m, ns, fs_))
    advance(2, 0)
    halo_wait(7)
    edge_ab = sum(dot(flat2(r.edge_a[...]), t) for t in b2).reshape(nk, PAD, LANES)

    def twelfth(k, c, c1=c1, c2=c2, c3=c3):
        m = r.mask_one[k]
        f1, f2, f3 = m * c1, m * c2, (m * c3) * col_mask
        ab = sum(dot(flat2(r.a2[k]), t) for t in b2).reshape(hh, PAD, LANES)
        q = (r.q2[k] + ab + v2) * r.s2[k]
        d = q * f1 + r.z2[k] * f2 + f3
        r.dz2[k, 0:hh, :, 0:LANES] = d.astype(BF16)
        r.dz2[k, 0:hh, :, LANES : 2 * LANES] = shifted_left(d).astype(BF16)
        q = (halo_row(7, 0, k) + edge_ab[k] + v2) * r.edge_t[k]
        d = jnp.where(row < nr - 1, q * f1 + halo_row(8, 0, k) * f2 + f3, 0.0)
        r.dz2[k, hh, :, 0:LANES] = d.astype(BF16)
        r.dz2[k, hh, :, LANES : 2 * LANES] = shifted_left(d).astype(BF16)
        return c

    loop(twelfth)
    d2_ = flat2(r.dz2[:, 0:hh, :, 0:LANES])
    inputs = [r.odd[:, 0:hh], r.even[...], r.odd[:, 1 : hh + 1]]
    stage(3, "spatial_one", jnp.concatenate([dot_tn(flat2(a), d2_) for a in inputs], axis=0))


    advance(3, 0)
    advance(2, 1)

    def thirteenth(k, acc):
        m = r.mask_one[k]
        u = dot(flat2(r.dz2[k, 0:hh]), r.back_here[...])
        v = dot(flat2(r.dz2[k, 1 : hh + 1]), r.back_below[...])
        s1, s2 = acc
        parts = (
            (1, 1, u[:, 0:LANES] + v[:, 0:LANES]),
            (0, 1, u[:, LANES : 2 * LANES]),
            (1, 0, u[:, 2 * LANES : 3 * LANES] + v[:, LANES : 2 * LANES]),
            (0, 0, u[:, 3 * LANES : 4 * LANES]),
        )
        for pr, pc, q in parts:
            q = q.reshape(hh, PAD, LANES) * r.s1[pr, pc, k]
            r.q1[pr, pc, k] = q
            s1 += m * folded(q)
            s2 += m * folded(q * r.z1[pr, pc, k])
        return s1, s2

    d1, d2 = loop(thirteenth, zero8(LANES, 2))
    send_sums(10, [row_sum(d1), row_sum(d2)])
    advance(3, 1)
    advance(0, 3)
    advance(1, 2)
    def masked(k, c):
        for q in planes:
            r.dz1[(*q, k)] = (r.mask_one[k] * r.q1[(*q, k)]).astype(BF16)
        return c

    loop(masked)
    part_q = sum(dot_tn(flat2(r.x[q]), flat2(r.dz1[q])) for q in planes)

    def skip_back(k, c):
        h3 = fs_[2] * col_mask
        for i in range(hh):
            r.dzs[k, i] = (r.q3[k, i] * fs_[0] + r.zs[k, i] * fs_[1] + h3).astype(BF16)
        r.skip_back[k] = dot_nt(flat2(r.dzs[k]), sc).reshape(hh, PAD, cfg.c_in)
        return c

    loop(skip_back)
    start_pieces(out_copies, *OUT_AT[4])
    advance(2, 2)
    db1, q1 = take_sums(10, [LANES] * 2)
    dg1 = gain_sum(n1, db1, q1)
    c1, c2, c3 = factors(n1, db1, dg1)

    total = n1.scale * part_q
    total += (c2 / n1.inv) * r.part_z[...] + (c3 + c2 * n1.mu) * r.part_m[...]
    one_send(total)
    one_spread()
    advance(3, 2)
    advance(0, 4)
    advance(1, 3)
    start_pieces(out_copies, *OUT_AT[5])

    def last(k, acc, c1=c1, c2=c2, c3=c3):
        m = r.mask_one[k]
        f1, f2, f3 = m * c1, m * c2, (m * c3) * col_mask
        for pr in range(2):
            for pc in range(2):
                d = (r.q1[pr, pc, k] * f1 + r.z1[pr, pc, k] * f2 + f3).astype(BF16)
                r.dz1[pr, pc, k] = d
        return acc

    loop(last)

    def images_back(k, c):
        for pr in range(2):
            for pc in range(2):
                g = dot_nt(flat2(r.dz1[pr, pc, k]), w1).reshape(hh, PAD, cfg.c_in)
                if pr == 0 and pc == 0:
                    g += r.skip_back[k]
                for i in range(hh):
                    for q in range(lane_blocks):
                        r.spread[q, 2 * i + pr, pl.ds(pc, PAD, stride=2), :] = g[
                            i, :, q * LANES : (q + 1) * LANES
                        ]
        for i in range(2 * hh):
            for q in range(lane_blocks):
                lanes = slice(q * LANES, (q + 1) * LANES)
                r.x_in[k, i, :, lanes] = r.spread[q, i, 0 : 2 * wv, :].astype(BF16)
        return c

    loop(images_back)
    back_copy = pltpu.make_async_copy(r.x_in, r.images_grad, r.local_sem.at[2])
    back_copy.start()

    for k, v in enumerate((dg1, dg2, dg4, dg5, db1, db2, db4, db5)):
        r.mid_held[k : k + 1, :] = v
    for k, v in enumerate((dg3, dgs, dg6, db3, db3, db6)):
        r.wide_held[k : k + 1, :] = v
    results = []

    def give(src, dst):
        copy = pltpu.make_async_copy(src, dst, r.full_sem.at[len(results)])
        copy.start()
        results.append(copy)

    give(r.mid_held, r.mid_grads)
    give(r.wide_held, r.wide_grads)

    def result(g):
        give(r.full[g], r.summed[g])

    def half_result(g, which):
        size = level_rows(g, 1)
        half = pl.ds(pl.multiple_of(which * size, 16), size)
        give(r.full[g].at[half], r.summed[g].at[half])

    advance(2, 3)
    advance(3, 3)
    one_gather()
    advance(0, 5)
    advance(1, 4)
    advance(2, 4)
    advance(3, 4)
    one_return()
    advance(0, 6)
    result(0)
    advance(1, 5)
    advance(2, 5)
    advance(3, 5)
    one_take()
    give(r.one_whole, r.summed_one)
    advance(1, 6)
    result(1)
    advance(2, 6)
    result(2)
    half_result(3, core)
    advance(3, 6)
    half_result(3, 1 - core)
    wait_pieces(1)
    out_local.wait()
    back_copy.wait()
    for copy in results:
        copy.wait()


def on_device(nr, nc, *args):
    (images, reduce_one, spatial_one, expand_one, shortcut, reduce_two, spatial_two, expand_two,
     mid_gain, mid_bias, wide_gain, wide_bias, widths, depth_gate, cot) = args
    nk, full_rows, full_cols, c_in = images.shape
    hh, wv, c_out = full_rows // 2, full_cols // 2, expand_one.shape[1]
    own = cot.shape[0]
    ndev, nxy, groups = nr * nc, nc // 2, len(GROUPS)
    sizes = [group_rows(g, ndev) for g in range(groups)]
    chunk = (ndev // 2, c_in // ndev, LANES)
    half, quad = (nk, hh, PAD), (2, 2, nk, hh, PAD)

    def f32(*shape):
        return pltpu.VMEM(shape, F32)

    def bf16(*shape):
        return pltpu.VMEM(shape, BF16)

    def dma(*shape):
        return pltpu.SemaphoreType.DMA(shape)

    def mid():
        return f32(*half, LANES)

    def wide():
        return f32(*half, c_out)

    def low(width):
        return bf16(*half, width)

    weights = dict(
        reduce_one=reduce_one, shortcut=shortcut, mid_gain=mid_gain, mid_bias=mid_bias,
        spatial_one=spatial_one.reshape(3, 3 * LANES, LANES), expand_one=expand_one,
        wide_gain=wide_gain, wide_bias=wide_bias, reduce_two=reduce_two,
        spatial_two=spatial_two.reshape(3, 3 * LANES, LANES), expand_two=expand_two,
    )
    scalars = dict(widths=widths.T, depth_gate=depth_gate)
    ins = dict(images=images, cot=cot, weights=weights)
    outs = dict(
        out=jax.ShapeDtypeStruct(cot.shape, BF16),
        images_grad=jax.ShapeDtypeStruct(images.shape, BF16),
        summed=[jax.ShapeDtypeStruct((size, LANES), BF16) for size in sizes[:4]],
        summed_one=jax.ShapeDtypeStruct((2,) + chunk, F32),
        mid_grads=jax.ShapeDtypeStruct((8, LANES), F32),
        wide_grads=jax.ShapeDtypeStruct((6, c_out), F32),
    )
    edges = [bf16(2 if i == 0 else 1, nk, PAD, LANES) for i in range(9)]
    levels = [(n, n // 2, n // nc, n // ndev) for n in sizes]
    halves = {i: ROUND_ROWS[i] // 2 for i in WIDE}
    scratch = dict(
        held={name: pltpu.VMEM(a.shape, a.dtype) for name, a in weights.items()},
        x_in=bf16(*images.shape), spread=f32(c_in // LANES, 2 * hh, 2 * PAD + 8, LANES), x=bf16(*quad, c_in),
        z1=f32(*quad, LANES), s1=f32(*quad, LANES), q1=f32(*quad, LANES), dz1=bf16(*quad, LANES),
        part_z=f32(c_in, LANES), part_m=f32(c_in, LANES),
        one_both=f32(2, *chunk), one_came=f32(*chunk), one_half=f32(*chunk), one_slots=f32(*chunk),
        one_whole=f32(2, *chunk), slope_z=low(LANES),
        edge_a=bf16(nk, PAD, LANES), edge_t=f32(nk, PAD, LANES),
        expand_z=f32(LANES, c_out), expand_m=f32(LANES, LANES), skip_z=f32(c_in, c_out),
        skip_m=f32(c_in, LANES), mid_held=f32(8, LANES), wide_held=f32(6, c_out),
        pair_rows=f32(2, 4, LANES), pair_came=f32(4, LANES), pair_chips=f32(ndev // 2, 4, LANES),
        pair_total=f32(2, 4, LANES),
        even=low(3 * LANES), odd=bf16(nk, hh + 1, PAD, 3 * LANES), dz2=bf16(nk, hh + 1, PAD, 2 * LANES),
        a4=bf16(nk, hh + 2, PAD, 3 * LANES), dz5=bf16(nk, hh + 2, PAD, 3 * LANES),
        cot_rows=bf16(nk, hh, wv, c_out), out_rows=bf16(nk, hh, wv, c_out), skip_back=f32(*half, c_in),
        back_two=bf16(3, 3 * LANES, LANES), back_here=bf16(2 * LANES, 4 * LANES),
        back_below=bf16(2 * LANES, 2 * LANES),
        mask_one=f32(nk, 1, LANES), mask_two=f32(nk, 1, LANES), gates=f32(nk, 1, c_out),
        z2=mid(), s2=mid(), q2=mid(), z4=mid(), s4=mid(), q4=mid(), z5=mid(), s5=mid(), q5=mid(),
        z3=wide(), zs=wide(), s3=wide(), q3=wide(), z6=wide(), live=wide(),
        a2=low(LANES), a5=low(LANES), dz4=low(LANES),
        hidden=low(c_out), dz6=low(c_out), dz3=low(c_out), dzs=low(c_out),
        edge=edges, halo=edges,
        sums=[
            f32(ndev // 2 if i in WIDE else ndev, halves.get(i, n), LANES)
            for i, n in enumerate(ROUND_ROWS)
        ],
        both={i: f32(2, n, LANES) for i, n in halves.items()},
        totals={i: f32(2, n, LANES) for i, n in halves.items()},
        from_pair={i: f32(n, LANES) for i, n in halves.items()},
        part=[[pltpu.VMEM((n[i], LANES), t) for i in range(3)] for n, t in zip(levels, GROUP_TYPES)],
        came=[
            [pltpu.VMEM((m - 1, n[i + 1], LANES), t) for i, m in enumerate((2, nxy, nr))]
            for n, t in zip(levels, GROUP_TYPES)
        ],
        full=[pltpu.VMEM((n, LANES), t) for n, t in zip(sizes, GROUP_TYPES)],
        image_sem=dma(nk), local_sem=dma(3), full_sem=dma(groups + 4), weight_sem=dma(len(weights)),
        sum_send=pltpu.SemaphoreType.DMA, sum_recv=dma(len(ROUND_ROWS)), halo_send=dma(9), halo_recv=dma(9),
        row_send=dma(2), row_recv=dma(2), pair_send=dma(12), pair_recv=dma(12), chip_send=dma(3),
        chip_recv=dma(3), grad_send=dma(groups), grad_recv=dma(groups, 6),
    )
    cfg = SimpleNamespace(
        nr=nr, nc=nc, nk=nk, hh=hh, wv=wv, c_in=c_in, c_out=c_out, group_size=sizes,
        pieces=split(hh, 7), order=list(weights),
    )
    flat, trees = [], []
    for part in (scalars, ins, outs, scratch):
        leaves, tree = jax.tree.flatten(part)
        flat.append(leaves)
        trees.append(tree)

    def body(*refs):
        named, at = {}, 0
        for leaves, tree in zip(flat, trees):
            named.update(jax.tree.unflatten(tree, refs[at : at + len(leaves)]))
            at += len(leaves)
        mega(cfg, SimpleNamespace(**named, **named["held"]))

    smem, hbm = pl.BlockSpec(memory_space=pltpu.SMEM), pl.BlockSpec(memory_space=pl.ANY)
    result = pl.pallas_call(
        body,
        out_shape=flat[2],
        in_specs=[smem] * len(flat[0]) + [hbm] * len(flat[1]),
        out_specs=[hbm] * len(flat[2]),
        scratch_shapes=flat[3],
        compiler_params=pltpu.CompilerParams(
            collective_id=0, has_side_effects=True, vmem_limit_bytes=60 << 20
        ),
    )(*flat[0], *flat[1])
    made = SimpleNamespace(**jax.tree.unflatten(trees[2], result))
    parts = [made.out, made.images_grad, *made.summed, made.summed_one, made.mid_grads, made.wide_grads]
    return finished(parts, mid_gain.shape, wide_gain.shape)


WEIGHTS = (
    ("reduce_one", (256, 128)),
    ("spatial_one", (3, 3, 128, 128)),
    ("expand_one", (128, 512)),
    ("shortcut", (256, 512)),
    ("reduce_two", (512, 128)),
    ("spatial_two", (3, 3, 128, 128)),
    ("expand_two", (128, 512)),
)


def finish(*refs):
    n = len(GROUPS) + 4
    ins, outs, held = refs[:n], refs[n : n + 13], refs[n + 13 : 2 * n + 13]
    wide_to, (in_sem, out_sem) = refs[2 * n + 13 : 2 * n + 24], refs[2 * n + 24 :]
    chunks = [(0, i) for i in range(4)] + [(1, i) for i in range(4)]

    def part(ref, which, i):
        size = ref.shape[1 - which] // 4
        return ref.at[:, pl.ds(i * size, size)] if which == 0 else ref.at[pl.ds(i * size, size)]

    small = [pltpu.make_async_copy(ins[i], held[i], in_sem.at[i]) for i in (n - 2, n - 1, *range(2, n - 2))]
    large = [
        pltpu.make_async_copy(part(ins[w], w, i), part(held[w], w, i), in_sem.at[n + 4 * w + i])
        for w, i in chunks
    ]
    for copy in small + large:
        copy.start()
    leaving = []

    def leave(src, dst):
        copy = pltpu.make_async_copy(src, dst, out_sem.at[len(leaving)])
        copy.start()
        leaving.append(copy)

    for i in range(2):
        small[i].wait()
    mid, wide = held[n - 2], held[n - 1]
    grads = (mid[0:4, :], mid[4:8, :], wide[0:3, :], wide[3:6, :])
    for ref, value, to in zip(wide_to[7:], grads, outs[9:]):
        ref[...] = value
        leave(ref, to)
    names = [name for name, _ in WEIGHTS]
    for g, group in enumerate(GROUPS[:4]):
        small[2 + g].wait()
        summed = held[2 + g]
        at = 0
        for name, rows in group:
            rest = name not in names
            which = names.index("expand_two" if rest else name)
            ref = wide_to[which]
            if len(ref.shape) == 4:
                for i in range(9):
                    lo = at + i * LANES
                    ref[i // 3, i % 3] = summed[lo : lo + LANES, :].astype(F32)
            else:
                height = ref.shape[0]
                first = ref.shape[1] // LANES - 1 if rest else 0
                for q in range(rows // height):
                    lo, to = at + q * height, (first + q) * LANES
                    ref[:, to : to + LANES] = summed[lo : lo + height, :].astype(F32)
            if rest or name != "expand_two":
                leave(ref, outs[2 + which])
            at += rows
    small[n - 3].wait()
    wide_to[0][...] = held[n - 3][...].reshape(wide_to[0].shape)
    leave(wide_to[0], outs[2])
    for copy, (w, i) in zip(large, chunks):
        copy.wait()
        leave(part(held[w], w, i), part(outs[w], w, i))
    for copy in leaving:
        copy.wait()


def finished(parts, mid_shape, wide_shape):
    hbm = pl.BlockSpec(memory_space=pl.ANY)
    outs = [jax.ShapeDtypeStruct(p.shape, p.dtype) for p in parts[:2]]
    outs += [jax.ShapeDtypeStruct(s, F32) for _, s in WEIGHTS]
    outs += [jax.ShapeDtypeStruct(s, F32) for s in (mid_shape, mid_shape, wide_shape, wide_shape)]
    dma = pltpu.SemaphoreType.DMA
    return tuple(
        pl.pallas_call(
            finish,
            out_shape=outs,
            in_specs=[hbm] * len(parts),
            out_specs=[hbm] * 13,
            scratch_shapes=[pltpu.VMEM(p.shape, p.dtype) for p in parts]
            + [pltpu.VMEM(o.shape, o.dtype) for o in outs[2:]]
            + [dma((len(parts) + 8,)), dma((19,))],
            compiler_params=pltpu.CompilerParams(vmem_limit_bytes=60 << 20),
        )(*parts)
    )


def solution(mesh):
    nr, nc = mesh.shape["rows"], mesh.shape["crops"]
    whole = P()
    return jax.shard_map(
        functools.partial(on_device, nr, nc),
        mesh=mesh,
        in_specs=(P("crops", "rows", None, None),)
        + (whole,) * 11
        + (P("crops", None), P("crops"), P(("crops", "rows"), None, None, None)),
        out_specs=(P(("crops", "rows"), None, None, None), P("crops", "rows", None, None))
        + (whole,) * 11,
        check_vma=False,
    )
```

```python
import functools
from types import SimpleNamespace

import jax
import jax.numpy as jnp
from jax import lax
from jax.experimental import pallas as pl
from jax.experimental.pallas import tpu as pltpu
from jax.sharding import PartitionSpec as P

MESH = pl.DeviceIdType.MESH
F32 = jnp.float32
BF16 = jnp.bfloat16
epsilon = 1e-05
COT_AT = ((0,), (1,), (2, 3), (4,), (5, 6), ())
OUT_AT = ((0, 1), (2,), (3, 4), (5, 6), (), ())
PAD = 32
LANES = 128

ROUND_ROWS = (4, 2, 8, 2, 2, 10, 8, 2, 2, 14, 2)
WIDE = (2, 5, 6, 9)


GROUPS = (
    (("expand_two", 384), ("spatial_two", 1152)),
    (("reduce_two", 512),),
    (("expand_one", 512), ("shortcut", 1024)),
    (("spatial_one", 1152), ("expand_rest", 128)),
    (("slope", 128), ("slope_z", 128)),
)
GROUP_TYPES = (BF16, BF16, BF16, BF16, F32)


def group_rows(g, devices):
    group, unit = GROUPS[g], (16 if GROUP_TYPES[g] == BF16 else 8) * devices
    return -(-sum(rows for _, rows in group) // unit) * unit


def split(rows, parts):
    return [(i * rows // parts, (i + 1) * rows // parts) for i in range(parts)]


def dot(a, b):
    return lax.dot_general(a, b, (((1,), (0,)), ((), ())), preferred_element_type=F32)


def dot_nt(a, b):
    return lax.dot_general(a, b, (((1,), (1,)), ((), ())), preferred_element_type=F32)


def dot_tn(a, b):
    return lax.dot_general(a, b, (((0,), (0,)), ((), ())), preferred_element_type=F32)


def two_terms(x):
    high = x.astype(BF16)
    return high, (x - high.astype(F32)).astype(BF16)


def half_act(h):
    return h + h * jnp.tanh(h)


def half_silu(h, half_mask=0.5):
    t = jnp.tanh(h)
    p = h * t
    return h + p, (half_mask + half_mask * t) * (1.0 + (h - p))


def folded(x):
    return jnp.sum(x.reshape(-1, 8, x.shape[-1]), axis=0)


def row_sum(x):
    return jnp.sum(x, axis=0, keepdims=True)


def flat2(x):
    return x.reshape(-1, x.shape[-1])


def mega(cfg, r):
    nr, nc, nk, hh, wv = cfg.nr, cfg.nc, cfg.nk, cfg.hh, cfg.wv
    ndev, nxy, own = nr * nc, nc // 2, nk // nr
    m_half = hh * PAD
    row = lax.axis_index("rows")
    col = lax.axis_index("crops")
    xy, core = lax.div(col, 2), lax.rem(col, 2)
    me = row * nc + col

    barrier = pltpu.get_barrier_semaphore()

    def place(i):
        return (lax.div(i, nc), lax.rem(i, nc))

    def greet(k, c):
        pl.semaphore_signal(
            barrier, inc=1, device_id=place(lax.rem(me + k, ndev)), device_id_type=MESH
        )
        return c

    lax.fori_loop(1, ndev, greet, 0)

    image_copies = [
        pltpu.make_async_copy(r.images.at[k], r.x_in.at[k], r.image_sem.at[k]) for k in range(nk)
    ]
    weight_copies = {
        name: pltpu.make_async_copy(r.weights[name], r.held[name], r.weight_sem.at[i])
        for i, name in enumerate(cfg.order)
    }
    for i, copy in enumerate(weight_copies.values()):
        copy.start()
        if i == 0:
            for other in image_copies:
                other.start()

    def arrived(*names):
        for name in names:
            weight_copies[name].wait()

    lane = lax.broadcasted_iota(jnp.int32, (1, LANES), 1)
    for k in range(nk):
        gate = (jnp.full((1, LANES), r.depth_gate[k], jnp.int32) > 0).astype(F32)
        r.mask_one[k] = (lane < r.widths[0, k]).astype(F32)
        r.mask_two[k] = (lane < r.widths[1, k]).astype(F32) * gate
        r.gates[k] = jnp.concatenate([gate] * 4, axis=1)
    col_mask = (lax.broadcasted_iota(jnp.int32, (PAD, 1), 0) < wv).astype(F32)
    half_mask = 0.5 * col_mask

    chips = nr * nxy
    chip = row * nxy + xy

    def chip_copy(src, dst, to, send_sem, recv_sem):
        return pltpu.make_async_remote_copy(
            src_ref=src,
            dst_ref=dst,
            send_sem=send_sem,
            recv_sem=recv_sem,
            device_id=(lax.div(to, nxy), lax.rem(to, nxy) * 2 + core),
            device_id_type=MESH,
        )

    def to_chips(copy_to):
        def send(k, c):
            copy_to(lax.rem(chip + k, chips)).start()
            return c

        lax.fori_loop(1, chips, send, 0)

    def all_of(ref, n, sem):
        pltpu.make_async_copy(ref.at[pl.ds(0, n)], ref.at[pl.ds(0, n)], sem).wait()

    def to_all(copy_to):
        def send(k, c):
            copy_to(lax.rem(me + k, ndev)).start()
            return c

        lax.fori_loop(1, ndev, send, 0)

    def sum_copy(idx, p):
        mine = r.sums[idx].at[me]
        return pltpu.make_async_remote_copy(
            src_ref=mine,
            dst_ref=mine,
            send_sem=r.sum_send,
            recv_sem=r.sum_recv.at[idx],
            device_id=place(p),
            device_id_type=MESH,
        )

    def pair_copy(step, src, dst):
        return pltpu.make_async_remote_copy(
            src_ref=src,
            dst_ref=dst,
            send_sem=r.pair_send.at[step],
            recv_sem=r.pair_recv.at[step],
            device_id=(row, xy * 2 + 1 - core),
            device_id_type=MESH,
        )

    def lines(vectors):
        return [v[:, q * LANES : (q + 1) * LANES] for v in vectors for q in range(v.shape[1] // LANES)]

    def send_sums(idx, vectors):
        rows = lines(vectors)
        assert len(rows) == ROUND_ROWS[idx]
        slots = r.sums[idx]
        if idx in WIDE:
            half = len(rows) // 2
            both, came = r.both[idx], r.from_pair[idx]
            for at, v in enumerate(rows):
                both[at // half, at % half : at % half + 1, :] = v
            copy = pair_copy(WIDE.index(idx), both.at[1 - core], came)
            copy.start()
            copy.wait()
            slots[chip] = both[core] + came[...]
        else:
            for at, v in enumerate(rows):
                slots[me, at : at + 1, :] = v
        if idx in WIDE:
            mine = slots.at[chip]
            to_chips(lambda to: chip_copy(mine, mine, to, r.sum_send, r.sum_recv.at[idx]))
        else:
            to_all(lambda p: sum_copy(idx, p))

    def take_sums(idx, widths):
        slots = r.sums[idx]
        others = slots.shape[0] - 1
        all_of(slots, others, r.sum_recv.at[idx])
        if idx in WIDE:
            totals = r.totals[idx]
            totals[core] = jnp.sum(slots[...], axis=0)
            mine = totals.at[core]
            copy = pair_copy(4 + WIDE.index(idx), mine, mine)
            copy.start()
            copy.wait()
            half = ROUND_ROWS[idx] // 2
            rows = [totals[at // half, at % half : at % half + 1, :] for at in range(2 * half)]
        else:
            total = jnp.sum(slots[...], axis=0)
            rows = [total[at : at + 1, :] for at in range(ROUND_ROWS[idx])]
        all_of(slots, others, r.sum_send)
        result, at = [], 0
        for w in widths:
            parts = rows[at : at + w // LANES]
            at += w // LANES
            result.append(jnp.concatenate(parts, axis=1) if len(parts) > 1 else parts[0])
        return result

    up_ok, down_ok = row > 0, row < nr - 1
    halo_up = (False, False, True, False, True, False, True, True, True)

    def halo(idx):
        return pltpu.make_async_remote_copy(
            src_ref=r.edge[idx],
            dst_ref=r.halo[idx],
            send_sem=r.halo_send.at[idx],
            recv_sem=r.halo_recv.at[idx],
            device_id=(row - 1 if halo_up[idx] else row + 1, col),
            device_id_type=MESH,
        )

    def halo_put(idx, at, rows):
        r.edge[idx][at] = rows.astype(BF16)

    def halo_start(idx):
        @pl.when(up_ok if halo_up[idx] else down_ok)
        def _():
            halo(idx).start()

    def halo_wait(idx):
        @pl.when(up_ok if halo_up[idx] else down_ok)
        def _():
            halo(idx).wait_send()

        @pl.when(down_ok if halo_up[idx] else up_ok)
        def _():
            halo(idx).wait_recv()

    def halo_row(idx, at, k):
        return r.halo[idx][at, k].astype(F32)

    def both_edges(idx, ref):
        halo_put(idx, 0, ref[:, hh - 1])
        halo_put(idx + 1, 0, ref[:, 0])

    def skip_send(vectors):
        for at, v in enumerate(lines(vectors)):
            r.pair_rows[at // 4, at % 4 : at % 4 + 1, :] = v
        pair_copy(8, r.pair_rows.at[1 - core], r.pair_came).start()

    def skip_spread():
        pair_copy(8, r.pair_rows.at[1 - core], r.pair_came).wait()
        r.pair_chips[chip] = r.pair_rows[core] + r.pair_came[...]
        mine = r.pair_chips.at[chip]
        to_chips(lambda to: chip_copy(mine, mine, to, r.chip_send.at[0], r.chip_recv.at[0]))

    def skip_return():
        all_of(r.pair_chips, chips - 1, r.chip_recv.at[0])
        all_of(r.pair_chips, chips - 1, r.chip_send.at[0])
        r.pair_total[core] = jnp.sum(r.pair_chips[...], axis=0)
        mine = r.pair_total.at[core]
        pair_copy(9, mine, mine).start()

    def skip_take():
        mine = r.pair_total.at[core]
        pair_copy(9, mine, mine).wait()
        return [
            jnp.concatenate([r.pair_total[i, q : q + 1, :] for q in range(4)], axis=1)
            for i in range(2)
        ]

    axes = (("core", 2), ("xy", nxy), ("rows", nr))
    seat = {"core": core, "xy": xy, "rows": row}

    def device_of(kind, i):
        if kind == "core":
            return (row, xy * 2 + i)
        if kind == "xy":
            return (row, i * 2 + core)
        return (i, col)

    def level_rows(g, level):
        size = cfg.group_size[g]
        for _, n in axes[:level]:
            size //= n
        return size

    def offset(g, level):
        at = 0
        for i, (kind, _) in enumerate(axes[:level]):
            at = at + seat[kind] * level_rows(g, i + 1)
        return pl.multiple_of(at, 8) if level else 0

    def scatter_send(g, level):
        kind, n = axes[level]
        chunk = level_rows(g, level + 1)
        for k in range(1, n):
            p = lax.rem(seat[kind] + k, n)
            pltpu.make_async_remote_copy(
                src_ref=r.part[g][level].at[pl.ds(pl.multiple_of(p * chunk, 8), chunk)],
                dst_ref=r.came[g][level].at[k - 1],
                send_sem=r.grad_send.at[g],
                recv_sem=r.grad_recv.at[g, level],
                device_id=device_of(kind, p),
                device_id_type=MESH,
            ).start()

    def scatter_take(g, level):
        kind, n = axes[level]
        chunk = level_rows(g, level + 1)
        came = r.came[g][level]
        pltpu.make_async_copy(came, came, r.grad_recv.at[g, level]).wait()
        mine = pl.ds(pl.multiple_of(seat[kind] * chunk, 8), chunk)
        total = r.part[g][level][mine, :].astype(F32) + jnp.sum(came[...].astype(F32), axis=0)
        pltpu.make_async_copy(came, came, r.grad_send.at[g]).wait()
        if level + 1 < len(axes):
            r.part[g][level + 1][...] = total.astype(GROUP_TYPES[g])
        else:
            r.full[g][pl.ds(offset(g, 3), chunk), :] = total.astype(GROUP_TYPES[g])

    def gather_send(g, level):
        kind, n = axes[level]
        size = level_rows(g, level + 1)
        region = r.full[g].at[pl.ds(offset(g, level + 1), size)]
        for k in range(1, n):
            p = lax.rem(seat[kind] + k, n)
            pltpu.make_async_remote_copy(
                src_ref=region,
                dst_ref=region,
                send_sem=r.grad_send.at[g],
                recv_sem=r.grad_recv.at[g, 3 + level],
                device_id=device_of(kind, p),
                device_id_type=MESH,
            ).start()

    def gather_take(g, level):
        n = axes[level][1]
        size = level_rows(g, level + 1) * (n - 1)
        bytes_of = r.full[g].at[pl.ds(0, size)]
        pltpu.make_async_copy(bytes_of, bytes_of, r.grad_recv.at[g, 3 + level]).wait()
        pltpu.make_async_copy(bytes_of, bytes_of, r.grad_send.at[g]).wait()

    steps = (
        (scatter_send, 0), (scatter_take, 0), (scatter_send, 1), (scatter_take, 1),
        (scatter_send, 2), (scatter_take, 2), (gather_send, 2), (gather_take, 2),
        (gather_send, 1), (gather_take, 1), (gather_send, 0), (gather_take, 0),
    )

    def advance(g, phase):
        for fn, level in steps[max(0, 2 * phase - 1) : 2 * phase + 1]:
            fn(g, level)

    def stage(g, name, value):
        at = 0
        for other, rows in GROUPS[g]:
            if other == name:
                break
            at += rows
        blocks = value.shape[1] // LANES
        for q in range(blocks):
            n = value.shape[0]
            lo = at + q * n
            r.part[g][0][lo : lo + n, :] = value[:, q * LANES : (q + 1) * LANES].astype(GROUP_TYPES[g])

    def one_send(value):
        r.one_both[...] = value.reshape(2, chips, -1, LANES)
        pair_copy(10, r.one_both.at[1 - core], r.one_came).start()

    def one_spread():
        pair_copy(10, r.one_both.at[1 - core], r.one_came).wait()
        half, slots = r.one_half, r.one_slots
        half[...] = r.one_both[core] + r.one_came[...]
        sems = (r.chip_send.at[1], r.chip_recv.at[1])
        to_chips(lambda to: chip_copy(half.at[to], slots.at[chip], to, *sems))

    def one_gather():
        slots = r.one_slots
        all_of(slots, chips - 1, r.chip_recv.at[1])
        slots[chip] = r.one_half[chip]
        r.one_whole[core, chip] = jnp.sum(slots[...], axis=0)
        mine = r.one_whole.at[core, chip]
        sems = (r.chip_send.at[2], r.chip_recv.at[2])
        to_chips(lambda to: chip_copy(mine, mine, to, *sems))

    def one_return():
        slots = r.one_slots
        all_of(slots, chips - 1, r.chip_send.at[1])
        all_of(slots, chips - 1, r.chip_recv.at[2])
        all_of(slots, chips - 1, r.chip_send.at[2])
        mine = r.one_whole.at[core]
        pair_copy(11, mine, mine).start()

    def one_take():
        mine = r.one_whole.at[core]
        pair_copy(11, mine, mine).wait()

    def coefficients(total, square, count, gain, bias):
        n = jnp.maximum(count, 1.0)
        mu = total / n
        inv = lax.rsqrt(square / n - mu * mu + epsilon)
        scale = gain * inv
        return SimpleNamespace(n=n, mu=mu, inv=inv, scale=scale, shift=bias - mu * scale)

    def factors(norm, dbias, dgain):
        c2 = -norm.scale * norm.inv * dgain / norm.n
        c3 = -norm.scale * dbias / norm.n - c2 * norm.mu
        return norm.scale, c2, c3

    def gain_sum(norm, total, z_total):
        return norm.inv * (z_total - norm.mu * total)

    def slope_sums(mask, slope, z, a, norm):
        def scaled(k, c):
            t = mask[k] * slope[k]
            r.dz4[k] = t.astype(BF16)
            r.slope_z[k] = (t * ((z[k] - norm.mu) * norm.inv)).astype(BF16)
            return c

        loop(scaled)
        flat_a = flat2(a[...])
        stage(4, "slope", dot_tn(flat_a, flat2(r.dz4[...])))
        stage(4, "slope_z", dot_tn(flat_a, flat2(r.slope_z[...])))

    def through(weight, c2, c3):
        high, low = two_terms(weight.astype(F32) * c2)
        b = dot_nt(high, weight) + dot_nt(low, weight)
        v = sum(dot_nt(jnp.broadcast_to(c, (16, c.shape[1])), weight) for c in two_terms(c3))
        return b, v[0:1]

    def chained(norm, u_sum, uz_sum, t_sum, tz_sum, b, v):
        k1, k2 = r.full[4][0:LANES, :], r.full[4][LANES : 2 * LANES, :]
        dbias = u_sum + row_sum(k1 * b) + t_sum * v
        dgain = gain_sum(norm, u_sum, uz_sum) + row_sum(k2 * b) + gain_sum(norm, t_sum, tz_sum) * v
        return dbias, dgain

    def loop(body, init=0):
        for k in range(nk):
            init = body(k, init)
        return init

    def zero8(width, count):
        return tuple(jnp.zeros((8, width), F32) for _ in range(count))

    def row_pieces(src_of, dst_of, send, recv, local):
        pieces = []
        for w, (lo, hi) in enumerate(cfg.pieces):
            for k in range(1, nr):
                p = lax.rem(row + k, nr)
                pieces.append(
                    pltpu.make_async_remote_copy(
                        src_ref=src_of(p, lo, hi - lo),
                        dst_ref=dst_of(lo, hi - lo),
                        send_sem=send,
                        recv_sem=recv,
                        device_id=(p, col),
                        device_id_type=MESH,
                    )
                )
        here = pltpu.make_async_copy(src_of(row, 0, hh), dst_of(0, hh), local)
        return pieces, here

    def wait_pieces(which):
        bytes_of = r.out_rows.at[pl.ds(0, nk - own)]
        pltpu.make_async_copy(bytes_of, bytes_of, r.row_recv.at[which]).wait()
        pltpu.make_async_copy(bytes_of, bytes_of, r.row_send.at[which]).wait()

    def start_pieces(pieces, *which):
        for w in which:
            for copy in pieces[w * (nr - 1) : (w + 1) * (nr - 1)]:
                copy.start()

    cot_copies, cot_local = row_pieces(
        lambda p, lo, n: r.cot.at[:, pl.ds(p * hh + lo, n)],
        lambda lo, n: r.cot_rows.at[pl.ds(row * own, own), pl.ds(lo, n)],
        r.row_send.at[0], r.row_recv.at[0], r.local_sem.at[0],
    )
    out_copies, out_local = row_pieces(
        lambda p, lo, n: r.out_rows.at[pl.ds(p * own, own), pl.ds(lo, n)],
        lambda lo, n: r.out.at[:, pl.ds(row * hh + lo, n)],
        r.row_send.at[1], r.row_recv.at[1], r.local_sem.at[1],
    )
    cot_local.start()

    lane_blocks = cfg.c_in // LANES
    for slot in range(2 * hh):
        for q in range(lane_blocks):
            r.spread[q, slot, 2 * wv : 2 * PAD, :] = jnp.zeros((2 * PAD - 2 * wv, LANES), F32)
    arrived("reduce_one")
    w1 = r.reduce_one[...]
    acc = zero8(LANES, 2)
    for copy in image_copies:
        copy.wait()

    def first(k, acc):
        for i in range(2 * hh):
            for q in range(lane_blocks):
                lanes = slice(q * LANES, (q + 1) * LANES)
                r.spread[q, i, 0 : 2 * wv, :] = r.x_in[k, i, :, lanes].astype(F32)
        m = r.mask_one[k]
        s1, s2 = acc
        for pr in range(2):
            for pc in range(2):
                for i in range(hh):
                    for q in range(lane_blocks):
                        lanes = slice(q * LANES, (q + 1) * LANES)
                        r.x[pr, pc, k, i, :, lanes] = r.spread[
                            q, 2 * i + pr, pl.ds(pc, PAD, stride=2), :
                        ].astype(BF16)
                z = dot(flat2(r.x[pr, pc, k]), w1)
                r.z1[pr, pc, k] = z.reshape(hh, PAD, LANES)
                s1 += m * folded(z)
                s2 += m * folded(z * z)
        return s1, s2

    s1, s2 = loop(first, acc)
    count_one = sum(r.mask_one[k] for k in range(nk))
    count_two = sum(r.mask_two[k] for k in range(nk))
    arrived("shortcut")
    sc = r.shortcut[...]

    def skip(k, acc):
        z = dot(flat2(r.x[0, 0, k]), sc)
        r.zs[k] = z.reshape(hh, PAD, cfg.c_out)
        return acc[0] + folded(z), acc[1] + folded(z * z)

    zs1, zs2 = loop(skip, zero8(cfg.c_out, 2))
    for pc in range(2):
        halo_put(0, pc, r.z1[1, pc, :, hh - 1])
    pl.semaphore_wait(barrier, ndev - 1)
    send_sums(0, [row_sum(s1), row_sum(s2), count_one, count_two])
    halo_start(0)
    skip_send([row_sum(zs1), row_sum(zs2)])
    arrived("mid_gain", "mid_bias", "spatial_one")
    arrived("spatial_two", "expand_two")
    def tap(ref, i, j):
        return ref[i, j * LANES : (j + 1) * LANES, :].T

    for i in range(3):
        for j in range(3):
            r.back_two[i, j * LANES : (j + 1) * LANES, :] = tap(r.spatial_two, 2 - i, 2 - j)
    zeros = jnp.zeros((LANES, LANES), BF16)
    k1 = r.spatial_one
    here = [[tap(k1, 2, 2), tap(k1, 1, 2), tap(k1, 2, 1), tap(k1, 1, 1)],
            [tap(k1, 2, 0), tap(k1, 1, 0), zeros, zeros]]
    below = [[tap(k1, 0, 2), tap(k1, 0, 1)], [tap(k1, 0, 0), zeros]]
    for ref, blocks in ((r.back_here, here), (r.back_below, below)):
        for i, line in enumerate(blocks):
            for j, block in enumerate(line):
                ref[i * LANES : (i + 1) * LANES, j * LANES : (j + 1) * LANES] = block

    for k in range(nk):
        r.dz4[k] = jnp.broadcast_to(r.mask_one[k], (hh, PAD, LANES)).astype(BF16)
    planes = [(pr, pc) for pr in range(2) for pc in range(2)]
    r.part_m[...] = sum(dot_tn(flat2(r.x[q]), flat2(r.dz4[...])) for q in planes)
    start_pieces(cot_copies, *COT_AT[0])
    t1, t2, active_one, active_two = take_sums(0, [LANES] * 4)
    half_px, full_px = float(hh * wv), float(4 * hh * wv)
    active_gate = active_two[:, 0:1]
    g1, b1 = r.mid_gain[0:1, :], r.mid_bias[0:1, :]
    n1 = coefficients(t1, t2, active_one * full_px, g1, b1)
    halo_wait(0)

    def shifted_right(a):
        return pltpu.roll(a, 1, axis=a.ndim - 2)

    def shifted_left(a):
        return pltpu.roll(a, PAD - 1, axis=a.ndim - 2)

    def affine(norm, m):
        return 0.5 * m * norm.scale, (0.5 * m * norm.shift) * col_mask

    k_one = [r.spatial_one[i] for i in range(3)]

    def second(k, acc):
        m = r.mask_one[k]
        ah, bh = affine(n1, m)
        for pr in range(2):
            for pc in range(2):
                a = half_act(r.z1[pr, pc, k] * ah + bh)
                dst = r.even if pr == 0 else r.odd
                rows = pl.ds(0, hh) if pr == 0 else pl.ds(1, hh)
                if pc == 0:
                    dst[k, rows, :, LANES : 2 * LANES] = a.astype(BF16)
                else:
                    dst[k, rows, :, 2 * LANES : 3 * LANES] = a.astype(BF16)
                    dst[k, rows, :, 0:LANES] = shifted_right(a).astype(BF16)
        for pc in range(2):
            a = half_act(halo_row(0, pc, k) * ah + bh)
            a = jnp.where(row > 0, a, 0.0)
            if pc == 0:
                r.odd[k, 0, :, LANES : 2 * LANES] = a.astype(BF16)
            else:
                r.odd[k, 0, :, 2 * LANES : 3 * LANES] = a.astype(BF16)
                r.odd[k, 0, :, 0:LANES] = shifted_right(a).astype(BF16)
        z = dot(flat2(r.even[k]), k_one[1])
        z += dot(flat2(r.odd[k, 1 : hh + 1]), k_one[2])
        z += dot(flat2(r.odd[k, 0:hh]), k_one[0])
        z = z.reshape(hh, PAD, LANES) * col_mask
        r.z2[k] = z
        return acc[0] + m * folded(z), acc[1] + m * folded(z * z)

    s1, s2 = loop(second, zero8(LANES, 2))
    send_sums(1, [row_sum(s1), row_sum(s2)])
    skip_spread()

    def early(k, c):
        m = r.mask_one[k]
        ah, bh = affine(n1, m)
        for pr in range(2):
            for pc in range(2):
                zhat = (r.z1[pr, pc, k] - n1.mu) * (m * n1.inv)
                r.dz1[pr, pc, k] = zhat.astype(BF16)
                _, r.s1[pr, pc, k] = half_silu(r.z1[pr, pc, k] * ah + bh, half_mask)
        return c

    loop(early)
    for name in ("expand_one", "wide_gain", "wide_bias", "reduce_two"):
        arrived(name)
    r.part_z[...] = sum(dot_tn(flat2(r.x[q]), flat2(r.dz1[q])) for q in planes)
    start_pieces(cot_copies, *COT_AT[1])
    t1, t2 = take_sums(1, [LANES] * 2)
    n2 = coefficients(t1, t2, active_one * half_px, r.mid_gain[1:2, :], r.mid_bias[1:2, :])
    e1 = r.expand_one[...]

    def third(k, acc):
        ah, bh = affine(n2, r.mask_one[k])
        a, s = half_silu(r.z2[k] * ah + bh, half_mask)
        r.s2[k] = s
        a = a.astype(BF16)
        r.a2[k] = a
        z = dot(flat2(a), e1)
        r.z3[k] = z.reshape(hh, PAD, cfg.c_out)
        t = r.mask_one[k] * s
        return (
            acc[0] + folded(z), acc[1] + folded(z * z), acc[2] + folded(t), acc[3] + folded(t * r.z2[k])
        )

    s1, s2, t2_sum, t2z_sum = loop(third, zero8(cfg.c_out, 2) + zero8(LANES, 2))
    send_sums(2, [row_sum(s1), row_sum(s2)])
    slope_sums(r.mask_one, r.s2, r.z2, r.a2, n2)
    advance(4, 0)
    skip_return()
    start_pieces(cot_copies, *COT_AT[2])
    t1, t2 = take_sums(2, [cfg.c_out] * 2)
    ts1, ts2 = skip_take()
    all_px = float(nk * nc) * float(nr) * half_px
    n3 = coefficients(t1, t2, all_px, r.wide_gain[0:1, :], r.wide_bias[0:1, :])
    ns = coefficients(ts1, ts2, all_px, r.wide_gain[1:2, :], r.wide_bias[1:2, :])
    w2 = r.reduce_two[...]

    a3, as_ = 0.5 * n3.scale, 0.5 * ns.scale
    b3 = (0.5 * (n3.shift + ns.shift)) * col_mask

    def fourth(k, acc):
        for i in range(hh):
            h = r.z3[k, i] * a3 + r.zs[k, i] * as_ + b3
            r.hidden[k, i] = half_act(h).astype(BF16)
        z = dot(flat2(r.hidden[k]), w2)
        r.z4[k] = z.reshape(hh, PAD, LANES)
        m = r.mask_two[k]
        return acc[0] + m * folded(z), acc[1] + m * folded(z * z)

    s1, s2 = loop(fourth, zero8(LANES, 2))
    send_sums(3, [row_sum(s1), row_sum(s2)])
    both_edges(1, r.z4)
    halo_start(1)
    halo_start(2)

    def hats(k, c):
        for i in range(hh):
            r.dz3[k, i] = ((r.z3[k, i] - n3.mu) * n3.inv).astype(BF16)
            r.dzs[k, i] = ((r.zs[k, i] - ns.mu) * ns.inv).astype(BF16)
            _, r.s3[k, i] = half_silu(r.z3[k, i] * a3 + r.zs[k, i] * as_ + b3, half_mask)
        return c

    advance(4, 1)
    loop(hats)
    ones = jnp.ones((nk * m_half, LANES), BF16)
    r.expand_z[...] = dot_tn(flat2(r.a2[...]), flat2(r.dz3[...]))
    r.expand_m[...] = dot_tn(flat2(r.a2[...]), ones)
    r.skip_z[...] = dot_tn(flat2(r.x[0, 0]), flat2(r.dzs[...]))
    r.skip_m[...] = dot_tn(flat2(r.x[0, 0]), ones)
    start_pieces(cot_copies, *COT_AT[3])
    t1, t2 = take_sums(3, [LANES] * 2)
    n4 = coefficients(t1, t2, active_two * half_px, r.mid_gain[2:3, :], r.mid_bias[2:3, :])
    halo_wait(1)
    halo_wait(2)

    def put3(dst, k, rows, a):
        dst[k, rows, :, LANES : 2 * LANES] = a.astype(BF16)
        dst[k, rows, :, 0:LANES] = shifted_right(a).astype(BF16)
        dst[k, rows, :, 2 * LANES : 3 * LANES] = shifted_left(a).astype(BF16)

    k_two = [r.spatial_two[i] for i in range(3)]

    def fifth(k, acc):
        m = r.mask_two[k]
        ah, bh = affine(n4, m)
        put3(r.a4, k, pl.ds(1, hh), half_act(r.z4[k] * ah + bh))
        a = half_act(halo_row(1, 0, k) * ah + bh)
        put3(r.a4, k, 0, jnp.where(row > 0, a, 0.0))
        a = half_act(halo_row(2, 0, k) * ah + bh)
        put3(r.a4, k, hh + 1, jnp.where(row < nr - 1, a, 0.0))
        z = sum(dot(flat2(r.a4[k, i : i + hh]), k_two[i]) for i in range(3))
        z = z.reshape(hh, PAD, LANES) * col_mask
        r.z5[k] = z
        return acc[0] + m * folded(z), acc[1] + m * folded(z * z)

    s1, s2 = loop(fifth, zero8(LANES, 2))
    send_sums(4, [row_sum(s1), row_sum(s2)])
    advance(4, 2)
    start_pieces(cot_copies, *COT_AT[4])

    def slope_four(k, c):
        ah, bh = affine(n4, r.mask_two[k])
        _, r.s4[k] = half_silu(r.z4[k] * ah + bh, half_mask)
        return c

    loop(slope_four)
    t1, t2 = take_sums(4, [LANES] * 2)
    n5 = coefficients(t1, t2, active_two * half_px, r.mid_gain[3:4, :], r.mid_bias[3:4, :])
    e2 = r.expand_two[...]

    def sixth(k, acc):
        ah, bh = affine(n5, r.mask_two[k])
        a = half_act(r.z5[k] * ah + bh).astype(BF16)
        r.a5[k] = a
        z = dot(flat2(a), e2)
        r.z6[k] = z.reshape(hh, PAD, cfg.c_out)
        g = r.gates[k]
        return acc[0] + g * folded(z), acc[1] + g * folded(z * z)

    s1, s2 = loop(sixth, zero8(cfg.c_out, 2))
    send_sums(5, [row_sum(v) for v in (s1, s2, t2_sum, t2z_sum)])
    start_pieces(cot_copies, *COT_AT[5])

    def slope_five(k, c):
        ah, bh = affine(n5, r.mask_two[k])
        _, r.s5[k] = half_silu(r.z5[k] * ah + bh, half_mask)
        return c

    loop(slope_five)
    both_edges(3, r.z5)
    halo_start(3)
    halo_start(4)
    advance(4, 3)
    wait_pieces(0)
    cot_local.wait()
    t1, t2, t2_sum, t2z_sum = take_sums(5, [cfg.c_out] * 2 + [LANES] * 2)
    gate_count = active_gate * half_px
    n6 = coefficients(t1, t2, gate_count, r.wide_gain[2:3, :], r.wide_bias[2:3, :])
    pad_rows = jnp.zeros((PAD - wv, cfg.c_out), F32)

    def cot_row(k, i):
        return jnp.concatenate([r.cot_rows[k, i].astype(F32), pad_rows], axis=0)

    def half_pre_two(k, i):
        g = 0.5 * r.gates[k]
        return 0.5 * r.hidden[k, i].astype(F32) + (r.z6[k, i] * (g * n6.scale) + (g * n6.shift) * col_mask)

    def seventh(k, acc):
        g = r.gates[k]
        d1, d2 = acc
        for i in range(hh):
            _, s = half_silu(half_pre_two(k, i))
            live = g * cot_row(k, i) * s
            r.live[k, i] = live
            d1 += folded(live)
            d2 += folded(live * r.z6[k, i])
        return d1, d2

    sums = loop(seventh, zero8(cfg.c_out, 2))
    send_sums(6, [row_sum(v) for v in sums])

    advance(4, 4)

    def results(k, c):
        for i in range(hh):
            hid = r.hidden[k, i].astype(F32)
            a = half_act(half_pre_two(k, i))
            r.out_rows[k, i] = jnp.where(r.gates[k] > 0.0, a, hid)[:wv].astype(BF16)
        return c

    loop(results)
    start_pieces(out_copies, *OUT_AT[0])
    out_local.start()
    db6, q6 = take_sums(6, [cfg.c_out] * 2)
    dg6 = gain_sum(n6, db6, q6)
    c1, c2, c3 = factors(n6, db6, dg6)

    def eighth(k, acc, c1=c1, c2=c2, c3=c3):
        g = r.gates[k]
        f1, f2, f3 = g * c1, g * c2, (g * c3) * col_mask
        for i in range(hh):
            r.dz6[k, i] = (r.live[k, i] * f1 + r.z6[k, i] * f2 + f3).astype(BF16)
        q = dot_nt(flat2(r.dz6[k]), e2).reshape(hh, PAD, LANES) * r.s5[k]
        r.q5[k] = q
        m = r.mask_two[k]
        return acc[0] + m * folded(q), acc[1] + m * folded(q * r.z5[k])

    d1, d2 = loop(eighth, zero8(LANES, 2))
    send_sums(7, [row_sum(d1), row_sum(d2)])
    both_edges(5, r.q5)
    halo_start(5)
    halo_start(6)
    def passed_by(k, c):
        for i in range(hh):
            r.live[k, i] = (1.0 - r.gates[k]) * cot_row(k, i) + r.live[k, i]
        return c

    loop(passed_by)
    expand_grad = dot_tn(flat2(r.a5[...]), flat2(r.dz6[...]))
    stage(0, "expand_two", expand_grad[:, : 3 * LANES])
    stage(3, "expand_rest", expand_grad[:, 3 * LANES :])
    halo_wait(3)
    halo_wait(4)
    advance(4, 5)
    start_pieces(out_copies, *OUT_AT[1])
    db5, q5 = take_sums(7, [LANES] * 2)
    dg5 = gain_sum(n5, db5, q5)
    c1, c2, c3 = factors(n5, db5, dg5)
    halo_wait(5)
    halo_wait(6)

    def ninth(k, acc, c1=c1, c2=c2, c3=c3):
        m = r.mask_two[k]
        f1, f2, f3 = m * c1, m * c2, (m * c3) * col_mask
        put3(r.dz5, k, pl.ds(1, hh), r.q5[k] * f1 + r.z5[k] * f2 + f3)
        d = halo_row(5, 0, k) * f1 + halo_row(3, 0, k) * f2 + f3
        put3(r.dz5, k, 0, jnp.where(row > 0, d, 0.0))
        d = halo_row(6, 0, k) * f1 + halo_row(4, 0, k) * f2 + f3
        put3(r.dz5, k, hh + 1, jnp.where(row < nr - 1, d, 0.0))
        q = sum(dot(flat2(r.dz5[k, i : i + hh]), r.back_two[i]) for i in range(3))
        q = q.reshape(hh, PAD, LANES) * r.s4[k]
        r.q4[k] = q
        return acc[0] + m * folded(q), acc[1] + m * folded(q * r.z4[k])

    d1, d2 = loop(ninth, zero8(LANES, 2))
    send_sums(8, [row_sum(d1), row_sum(d2)])
    halo_put(8, 0, r.z2[:, 0])
    halo_start(8)

    d5 = flat2(r.dz5[:, 1 : hh + 1, :, LANES : 2 * LANES])
    stage(
        0,
        "spatial_two",
        jnp.concatenate([dot_tn(flat2(r.a4[:, i : i + hh]), d5) for i in range(3)], axis=0),
    )
    advance(4, 6)
    advance(0, 0)
    start_pieces(out_copies, *OUT_AT[2])
    db4, q4 = take_sums(8, [LANES] * 2)
    advance(0, 1)
    dg4 = gain_sum(n4, db4, q4)
    c1, c2, c3 = factors(n4, db4, dg4)

    def tenth(k, acc, c1=c1, c2=c2, c3=c3):
        m = r.mask_two[k]
        f1, f2, f3 = m * c1, m * c2, (m * c3) * col_mask
        r.dz4[k] = (r.q4[k] * f1 + r.z4[k] * f2 + f3).astype(BF16)
        back = dot_nt(flat2(r.dz4[k]), w2).reshape(hh, PAD, cfg.c_out)
        e1_, e2_, e3_, u1, u2 = acc
        for i in range(hh):
            d = back[i] + r.live[k, i]
            q = d.astype(BF16).astype(F32) * r.s3[k, i]
            r.q3[k, i] = q
            r.dz3[k, i] = (q * n3.scale).astype(BF16)
            e1_ += folded(q)
            e2_ += folded(q * r.z3[k, i])
            e3_ += folded(q * r.zs[k, i])
        u = dot_nt(flat2(r.dz3[k]), e1).reshape(hh, PAD, LANES)
        r.q2[k] = u
        ut = (r.mask_one[k] * u) * r.s2[k]
        return e1_, e2_, e3_, u1 + folded(ut), u2 + folded(ut * r.z2[k])

    sums = loop(tenth, zero8(cfg.c_out, 3) + zero8(LANES, 2))
    send_sums(9, [row_sum(v) for v in sums])
    halo_put(7, 0, r.q2[:, 0])
    halo_start(7)
    stage(1, "reduce_two", dot_tn(flat2(r.hidden[...]), flat2(r.dz4[...])))
    advance(1, 0)
    expand_q = dot_tn(flat2(r.a2[...]), flat2(r.dz3[...]))
    skip_q = dot_tn(flat2(r.x[0, 0]), flat2(r.dz3[...]))
    halo_wait(8)

    def edge_slope(k, c):
        ah, bh = affine(n2, r.mask_one[k])
        a, t = half_silu(halo_row(8, 0, k) * ah + bh, half_mask)
        r.edge_a[k] = a.astype(BF16)
        r.edge_t[k] = t
        return c

    loop(edge_slope)
    advance(1, 1)
    advance(0, 2)
    start_pieces(out_copies, *OUT_AT[3])
    db3, q3, qs, u_sum, uz_sum = take_sums(9, [cfg.c_out] * 3 + [LANES] * 2)
    dg3, dgs = gain_sum(n3, db3, q3), gain_sum(ns, db3, qs)
    f3_, fs_ = factors(n3, db3, dg3), factors(ns, db3, dgs)
    b, v2 = through(e1, *f3_[1:])
    db2, dg2 = chained(n2, u_sum, uz_sum, t2_sum, t2z_sum, b, v2)
    c1, c2, c3 = factors(n2, db2, dg2)
    b2 = two_terms(b)

    def four(x):
        return jnp.concatenate([x] * (cfg.c_out // LANES), axis=1)

    def by_parts(q_part, z_part, m_part, norm, fs):
        total = q_part + (fs[1] / norm.inv) * z_part[...]
        return total + (fs[2] + fs[1] * norm.mu) * four(m_part[...])

    halo_wait(7)
    edge_ab = sum(dot(flat2(r.edge_a[...]), t) for t in b2).reshape(nk, PAD, LANES)

    def twelfth(k, c, c1=c1, c2=c2, c3=c3):
        m = r.mask_one[k]
        f1, f2, f3 = m * c1, m * c2, (m * c3) * col_mask
        ab = sum(dot(flat2(r.a2[k]), t) for t in b2).reshape(hh, PAD, LANES)
        q = (r.q2[k] + ab + v2) * r.s2[k]
        d = q * f1 + r.z2[k] * f2 + f3
        r.dz2[k, 0:hh, :, 0:LANES] = d.astype(BF16)
        r.dz2[k, 0:hh, :, LANES : 2 * LANES] = shifted_left(d).astype(BF16)
        q = (halo_row(7, 0, k) + edge_ab[k] + v2) * r.edge_t[k]
        d = jnp.where(row < nr - 1, q * f1 + halo_row(8, 0, k) * f2 + f3, 0.0)
        r.dz2[k, hh, :, 0:LANES] = d.astype(BF16)
        r.dz2[k, hh, :, LANES : 2 * LANES] = shifted_left(d).astype(BF16)
        return c

    loop(twelfth)
    stage(2, "expand_one", by_parts(expand_q, r.expand_z, r.expand_m, n3, f3_))
    stage(2, "shortcut", by_parts(skip_q * (ns.scale / n3.scale), r.skip_z, r.skip_m, ns, fs_))
    advance(2, 0)
    d2_ = flat2(r.dz2[:, 0:hh, :, 0:LANES])
    inputs = [r.odd[:, 0:hh], r.even[...], r.odd[:, 1 : hh + 1]]
    stage(3, "spatial_one", jnp.concatenate([dot_tn(flat2(a), d2_) for a in inputs], axis=0))


    advance(3, 0)
    advance(2, 1)

    def thirteenth(k, acc):
        m = r.mask_one[k]
        u = dot(flat2(r.dz2[k, 0:hh]), r.back_here[...])
        v = dot(flat2(r.dz2[k, 1 : hh + 1]), r.back_below[...])
        s1, s2 = acc
        parts = (
            (1, 1, u[:, 0:LANES] + v[:, 0:LANES]),
            (0, 1, u[:, LANES : 2 * LANES]),
            (1, 0, u[:, 2 * LANES : 3 * LANES] + v[:, LANES : 2 * LANES]),
            (0, 0, u[:, 3 * LANES : 4 * LANES]),
        )
        for pr, pc, q in parts:
            q = q.reshape(hh, PAD, LANES) * r.s1[pr, pc, k]
            r.q1[pr, pc, k] = q
            s1 += m * folded(q)
            s2 += m * folded(q * r.z1[pr, pc, k])
        return s1, s2

    d1, d2 = loop(thirteenth, zero8(LANES, 2))
    send_sums(10, [row_sum(d1), row_sum(d2)])
    advance(3, 1)
    advance(0, 3)
    advance(1, 2)
    def masked(k, c):
        for q in planes:
            r.dz1[(*q, k)] = (r.mask_one[k] * r.q1[(*q, k)]).astype(BF16)
        return c

    loop(masked)
    part_q = sum(dot_tn(flat2(r.x[q]), flat2(r.dz1[q])) for q in planes)

    def skip_back(k, c):
        h3 = fs_[2] * col_mask
        for i in range(hh):
            r.dzs[k, i] = (r.q3[k, i] * fs_[0] + r.zs[k, i] * fs_[1] + h3).astype(BF16)
        r.skip_back[k] = dot_nt(flat2(r.dzs[k]), sc).reshape(hh, PAD, cfg.c_in)
        return c

    loop(skip_back)
    start_pieces(out_copies, *OUT_AT[4])
    advance(2, 2)
    db1, q1 = take_sums(10, [LANES] * 2)
    dg1 = gain_sum(n1, db1, q1)
    c1, c2, c3 = factors(n1, db1, dg1)

    total = n1.scale * part_q
    total += (c2 / n1.inv) * r.part_z[...] + (c3 + c2 * n1.mu) * r.part_m[...]
    one_send(total)
    one_spread()
    advance(3, 2)
    advance(0, 4)
    advance(1, 3)
    start_pieces(out_copies, *OUT_AT[5])

    def last(k, acc, c1=c1, c2=c2, c3=c3):
        m = r.mask_one[k]
        f1, f2, f3 = m * c1, m * c2, (m * c3) * col_mask
        for pr in range(2):
            for pc in range(2):
                d = (r.q1[pr, pc, k] * f1 + r.z1[pr, pc, k] * f2 + f3).astype(BF16)
                r.dz1[pr, pc, k] = d
        return acc

    loop(last)

    def images_back(k, c):
        for pr in range(2):
            for pc in range(2):
                g = dot_nt(flat2(r.dz1[pr, pc, k]), w1).reshape(hh, PAD, cfg.c_in)
                if pr == 0 and pc == 0:
                    g += r.skip_back[k]
                for i in range(hh):
                    for q in range(lane_blocks):
                        r.spread[q, 2 * i + pr, pl.ds(pc, PAD, stride=2), :] = g[
                            i, :, q * LANES : (q + 1) * LANES
                        ]
        for i in range(2 * hh):
            for q in range(lane_blocks):
                lanes = slice(q * LANES, (q + 1) * LANES)
                r.x_in[k, i, :, lanes] = r.spread[q, i, 0 : 2 * wv, :].astype(BF16)
        return c

    loop(images_back)
    back_copy = pltpu.make_async_copy(r.x_in, r.images_grad, r.local_sem.at[2])
    back_copy.start()

    for k, v in enumerate((dg1, dg2, dg4, dg5, db1, db2, db4, db5)):
        r.mid_held[k : k + 1, :] = v
    for k, v in enumerate((dg3, dgs, dg6, db3, db3, db6)):
        r.wide_held[k : k + 1, :] = v
    results = []

    def give(src, dst):
        copy = pltpu.make_async_copy(src, dst, r.full_sem.at[len(results)])
        copy.start()
        results.append(copy)

    give(r.mid_held, r.mid_grads)
    give(r.wide_held, r.wide_grads)

    def result(g):
        give(r.full[g], r.summed[g])

    def half_result(g, which):
        size = level_rows(g, 1)
        half = pl.ds(pl.multiple_of(which * size, 16), size)
        give(r.full[g].at[half], r.summed[g].at[half])

    advance(2, 3)
    advance(3, 3)
    one_gather()
    advance(0, 5)
    advance(1, 4)
    advance(2, 4)
    advance(3, 4)
    one_return()
    advance(0, 6)
    result(0)
    advance(1, 5)
    advance(2, 5)
    advance(3, 5)
    one_take()
    give(r.one_whole, r.summed_one)
    advance(1, 6)
    result(1)
    advance(2, 6)
    result(2)
    half_result(3, core)
    advance(3, 6)
    half_result(3, 1 - core)
    wait_pieces(1)
    out_local.wait()
    back_copy.wait()
    for copy in results:
        copy.wait()


def on_device(nr, nc, *args):
    (images, reduce_one, spatial_one, expand_one, shortcut, reduce_two, spatial_two, expand_two,
     mid_gain, mid_bias, wide_gain, wide_bias, widths, depth_gate, cot) = args
    nk, full_rows, full_cols, c_in = images.shape
    hh, wv, c_out = full_rows // 2, full_cols // 2, expand_one.shape[1]
    own = cot.shape[0]
    ndev, nxy, groups = nr * nc, nc // 2, len(GROUPS)
    sizes = [group_rows(g, ndev) for g in range(groups)]
    chunk = (ndev // 2, c_in // ndev, LANES)
    half, quad = (nk, hh, PAD), (2, 2, nk, hh, PAD)

    def f32(*shape):
        return pltpu.VMEM(shape, F32)

    def bf16(*shape):
        return pltpu.VMEM(shape, BF16)

    def dma(*shape):
        return pltpu.SemaphoreType.DMA(shape)

    def mid():
        return f32(*half, LANES)

    def wide():
        return f32(*half, c_out)

    def low(width):
        return bf16(*half, width)

    weights = dict(
        reduce_one=reduce_one, shortcut=shortcut, mid_gain=mid_gain, mid_bias=mid_bias,
        spatial_one=spatial_one.reshape(3, 3 * LANES, LANES), expand_one=expand_one,
        wide_gain=wide_gain, wide_bias=wide_bias, reduce_two=reduce_two,
        spatial_two=spatial_two.reshape(3, 3 * LANES, LANES), expand_two=expand_two,
    )
    scalars = dict(widths=widths.T, depth_gate=depth_gate)
    ins = dict(images=images, cot=cot, weights=weights)
    outs = dict(
        out=jax.ShapeDtypeStruct(cot.shape, BF16),
        images_grad=jax.ShapeDtypeStruct(images.shape, BF16),
        summed=[jax.ShapeDtypeStruct((size, LANES), BF16) for size in sizes[:4]],
        summed_one=jax.ShapeDtypeStruct((2,) + chunk, F32),
        mid_grads=jax.ShapeDtypeStruct((8, LANES), F32),
        wide_grads=jax.ShapeDtypeStruct((6, c_out), F32),
    )
    edges = [bf16(2 if i == 0 else 1, nk, PAD, LANES) for i in range(9)]
    levels = [(n, n // 2, n // nc, n // ndev) for n in sizes]
    halves = {i: ROUND_ROWS[i] // 2 for i in WIDE}
    scratch = dict(
        held={name: pltpu.VMEM(a.shape, a.dtype) for name, a in weights.items()},
        x_in=bf16(*images.shape), spread=f32(c_in // LANES, 2 * hh, 2 * PAD + 8, LANES), x=bf16(*quad, c_in),
        z1=f32(*quad, LANES), s1=f32(*quad, LANES), q1=f32(*quad, LANES), dz1=bf16(*quad, LANES),
        part_z=f32(c_in, LANES), part_m=f32(c_in, LANES),
        one_both=f32(2, *chunk), one_came=f32(*chunk), one_half=f32(*chunk), one_slots=f32(*chunk),
        one_whole=f32(2, *chunk), slope_z=low(LANES),
        edge_a=bf16(nk, PAD, LANES), edge_t=f32(nk, PAD, LANES),
        expand_z=f32(LANES, c_out), expand_m=f32(LANES, LANES), skip_z=f32(c_in, c_out),
        skip_m=f32(c_in, LANES), mid_held=f32(8, LANES), wide_held=f32(6, c_out),
        pair_rows=f32(2, 4, LANES), pair_came=f32(4, LANES), pair_chips=f32(ndev // 2, 4, LANES),
        pair_total=f32(2, 4, LANES),
        even=low(3 * LANES), odd=bf16(nk, hh + 1, PAD, 3 * LANES), dz2=bf16(nk, hh + 1, PAD, 2 * LANES),
        a4=bf16(nk, hh + 2, PAD, 3 * LANES), dz5=bf16(nk, hh + 2, PAD, 3 * LANES),
        cot_rows=bf16(nk, hh, wv, c_out), out_rows=bf16(nk, hh, wv, c_out), skip_back=f32(*half, c_in),
        back_two=bf16(3, 3 * LANES, LANES), back_here=bf16(2 * LANES, 4 * LANES),
        back_below=bf16(2 * LANES, 2 * LANES),
        mask_one=f32(nk, 1, LANES), mask_two=f32(nk, 1, LANES), gates=f32(nk, 1, c_out),
        z2=mid(), s2=mid(), q2=mid(), z4=mid(), s4=mid(), q4=mid(), z5=mid(), s5=mid(), q5=mid(),
        z3=wide(), zs=wide(), s3=wide(), q3=wide(), z6=wide(), live=wide(),
        a2=low(LANES), a5=low(LANES), dz4=low(LANES),
        hidden=low(c_out), dz6=low(c_out), dz3=low(c_out), dzs=low(c_out),
        edge=edges, halo=edges,
        sums=[
            f32(ndev // 2 if i in WIDE else ndev, halves.get(i, n), LANES)
            for i, n in enumerate(ROUND_ROWS)
        ],
        both={i: f32(2, n, LANES) for i, n in halves.items()},
        totals={i: f32(2, n, LANES) for i, n in halves.items()},
        from_pair={i: f32(n, LANES) for i, n in halves.items()},
        part=[[pltpu.VMEM((n[i], LANES), t) for i in range(3)] for n, t in zip(levels, GROUP_TYPES)],
        came=[
            [pltpu.VMEM((m - 1, n[i + 1], LANES), t) for i, m in enumerate((2, nxy, nr))]
            for n, t in zip(levels, GROUP_TYPES)
        ],
        full=[pltpu.VMEM((n, LANES), t) for n, t in zip(sizes, GROUP_TYPES)],
        image_sem=dma(nk), local_sem=dma(3), full_sem=dma(groups + 4), weight_sem=dma(len(weights)),
        sum_send=pltpu.SemaphoreType.DMA, sum_recv=dma(len(ROUND_ROWS)), halo_send=dma(9), halo_recv=dma(9),
        row_send=dma(2), row_recv=dma(2), pair_send=dma(12), pair_recv=dma(12), chip_send=dma(3),
        chip_recv=dma(3), grad_send=dma(groups), grad_recv=dma(groups, 6),
    )
    cfg = SimpleNamespace(
        nr=nr, nc=nc, nk=nk, hh=hh, wv=wv, c_in=c_in, c_out=c_out, group_size=sizes,
        pieces=split(hh, 7), order=list(weights),
    )
    flat, trees = [], []
    for part in (scalars, ins, outs, scratch):
        leaves, tree = jax.tree.flatten(part)
        flat.append(leaves)
        trees.append(tree)

    def body(*refs):
        named, at = {}, 0
        for leaves, tree in zip(flat, trees):
            named.update(jax.tree.unflatten(tree, refs[at : at + len(leaves)]))
            at += len(leaves)
        mega(cfg, SimpleNamespace(**named, **named["held"]))

    smem, hbm = pl.BlockSpec(memory_space=pltpu.SMEM), pl.BlockSpec(memory_space=pl.ANY)
    result = pl.pallas_call(
        body,
        out_shape=flat[2],
        in_specs=[smem] * len(flat[0]) + [hbm] * len(flat[1]),
        out_specs=[hbm] * len(flat[2]),
        scratch_shapes=flat[3],
        compiler_params=pltpu.CompilerParams(
            collective_id=0, has_side_effects=True, vmem_limit_bytes=60 << 20
        ),
    )(*flat[0], *flat[1])
    made = SimpleNamespace(**jax.tree.unflatten(trees[2], result))
    parts = [made.out, made.images_grad, *made.summed, made.summed_one, made.mid_grads, made.wide_grads]
    return finished(parts, mid_gain.shape, wide_gain.shape)


WEIGHTS = (
    ("reduce_one", (256, 128)),
    ("spatial_one", (3, 3, 128, 128)),
    ("expand_one", (128, 512)),
    ("shortcut", (256, 512)),
    ("reduce_two", (512, 128)),
    ("spatial_two", (3, 3, 128, 128)),
    ("expand_two", (128, 512)),
)


def finish(*refs):
    n = len(GROUPS) + 4
    ins, outs, held = refs[:n], refs[n : n + 13], refs[n + 13 : 2 * n + 13]
    wide_to, (in_sem, out_sem) = refs[2 * n + 13 : 2 * n + 24], refs[2 * n + 24 :]
    chunks = [(0, i) for i in range(4)] + [(1, i) for i in range(4)]

    def part(ref, which, i):
        size = ref.shape[1 - which] // 4
        return ref.at[:, pl.ds(i * size, size)] if which == 0 else ref.at[pl.ds(i * size, size)]

    small = [pltpu.make_async_copy(ins[i], held[i], in_sem.at[i]) for i in (n - 2, n - 1, *range(2, n - 2))]
    large = [
        pltpu.make_async_copy(part(ins[w], w, i), part(held[w], w, i), in_sem.at[n + 4 * w + i])
        for w, i in chunks
    ]
    for copy in small + large:
        copy.start()
    leaving = []

    def leave(src, dst):
        copy = pltpu.make_async_copy(src, dst, out_sem.at[len(leaving)])
        copy.start()
        leaving.append(copy)

    for i in range(2):
        small[i].wait()
    mid, wide = held[n - 2], held[n - 1]
    grads = (mid[0:4, :], mid[4:8, :], wide[0:3, :], wide[3:6, :])
    for ref, value, to in zip(wide_to[7:], grads, outs[9:]):
        ref[...] = value
        leave(ref, to)
    names = [name for name, _ in WEIGHTS]
    for g, group in enumerate(GROUPS[:4]):
        small[2 + g].wait()
        summed = held[2 + g]
        at = 0
        for name, rows in group:
            rest = name not in names
            which = names.index("expand_two" if rest else name)
            ref = wide_to[which]
            if len(ref.shape) == 4:
                for i in range(9):
                    lo = at + i * LANES
                    ref[i // 3, i % 3] = summed[lo : lo + LANES, :].astype(F32)
            else:
                height = ref.shape[0]
                first = ref.shape[1] // LANES - 1 if rest else 0
                for q in range(rows // height):
                    lo, to = at + q * height, (first + q) * LANES
                    ref[:, to : to + LANES] = summed[lo : lo + height, :].astype(F32)
            if rest or name != "expand_two":
                leave(ref, outs[2 + which])
            at += rows
    small[n - 3].wait()
    wide_to[0][...] = held[n - 3][...].reshape(wide_to[0].shape)
    leave(wide_to[0], outs[2])
    for copy, (w, i) in zip(large, chunks):
        copy.wait()
        leave(part(held[w], w, i), part(outs[w], w, i))
    for copy in leaving:
        copy.wait()


def finished(parts, mid_shape, wide_shape):
    hbm = pl.BlockSpec(memory_space=pl.ANY)
    outs = [jax.ShapeDtypeStruct(p.shape, p.dtype) for p in parts[:2]]
    outs += [jax.ShapeDtypeStruct(s, F32) for _, s in WEIGHTS]
    outs += [jax.ShapeDtypeStruct(s, F32) for s in (mid_shape, mid_shape, wide_shape, wide_shape)]
    dma = pltpu.SemaphoreType.DMA
    return tuple(
        pl.pallas_call(
            finish,
            out_shape=outs,
            in_specs=[hbm] * len(parts),
            out_specs=[hbm] * 13,
            scratch_shapes=[pltpu.VMEM(p.shape, p.dtype) for p in parts]
            + [pltpu.VMEM(o.shape, o.dtype) for o in outs[2:]]
            + [dma((len(parts) + 8,)), dma((19,))],
            compiler_params=pltpu.CompilerParams(vmem_limit_bytes=60 << 20),
        )(*parts)
    )


def solution(mesh):
    nr, nc = mesh.shape["rows"], mesh.shape["crops"]
    whole = P()
    return jax.shard_map(
        functools.partial(on_device, nr, nc),
        mesh=mesh,
        in_specs=(P("crops", "rows", None, None),)
        + (whole,) * 11
        + (P("crops", None), P("crops"), P(("crops", "rows"), None, None, None)),
        out_specs=(P(("crops", "rows"), None, None, None), P("crops", "rows", None, None))
        + (whole,) * 11,
        check_vma=False,
    )
```
